128 devices in a mesh: row: 16 (over x, y_hi, core), col: 8 (over y_lo, z).
Axes of the slice: x: 4, y: 4 (y_hi: 2, y_lo: 2; y = y_hi * 2 + y_lo), z: 4, core: 2. Of those that a mesh axis runs over, the one named last changes fastest.
Arguments:
- pair: bfloat16 [1024, 1024, 128], P('row', 'col'), may hold values from -3 to 3
- norm_gain: float32 [128], replicated, may hold values from 0.5 to 1.5
- norm_shift: float32 [128], replicated, may hold values from -3 to 3
- proj_weight: bfloat16 [128, 384], replicated, may hold values from -0.5 to 0.5
- proj_bias: float32 [384], replicated, may hold values from -3 to 3
- mid_gain: float32 [64], replicated, may hold values from 0.5 to 1.5
- mid_shift: float32 [64], replicated, may hold values from -3 to 3
- out_weight: bfloat16 [64, 128], replicated, may hold values from -1.5 to 1.5
- out_bias: float32 [128], replicated, may hold values from -3 to 3
- conv_gain: float32 [2, 128], replicated, may hold values from 0.5 to 1.5
- conv_shift: float32 [2, 128], replicated, may hold values from -3 to 3
- convolution_weight: bfloat16 [2, 9, 128, 128], replicated, may hold values from -0.375 to 0.375
- convolution_bias: float32 [2, 128], replicated, may hold values from -2 to 2
Outputs:
- refined: bfloat16 [1024, 1024, 128], P('row', 'col')
The draws below stay inside these ranges and needn't reach their ends.
All inputs are finite; a program needn't handle non-finite values.
Results may differ from the reference program's by a relative error of at most 0.008.
Values may be sent and summed in bfloat16 or wider, within the bound.
No kernel may reach another device: no remote copies, remote signals or barrier semaphores. Data moves between devices by JAX's collectives and lax.ppermute only.
A program may use at most 128 MiB of HBM per device.

```python
import jax
import jax.numpy as jnp
from jax import lax

CH = 128
HID = 64
FIRST_DILATION = 2
SECOND_DILATION = 4
RES = 1024


def block_levels(key, dims, cuts, smallest, largest):
    def one(dim, shards_of):
        heights = jax.random.uniform(jax.random.fold_in(jax.random.fold_in(key, 6), dim), (shards_of,), jnp.float32, smallest / len(cuts), largest / len(cuts))
        return jnp.repeat(jnp.exp(heights), dims[dim] // shards_of).reshape((-1,) + (1,) * (len(dims) - dim - 1))

    level = one(*cuts[0])
    for cut in cuts[1:]:
        level = level * one(*cut)
    return level


def bell_draw(own_key, shape, deviation, limit, shards=(), dtype=jnp.bfloat16):
    loudness = block_levels(own_key, shape, shards, -0.22, 0.18) if shards else 1.0
    values = jax.random.normal(own_key, shape, jnp.float32) * deviation * loudness
    return jnp.minimum(jnp.maximum(values, -limit), limit).astype(dtype)


def setup_inputs(seed: int = 0) -> dict:
    streams_of = jax.random.split(jax.random.key(seed), 14)
    return {
        "pair": bell_draw(streams_of[0], (RES, RES, CH), 0.5, 3.0, ((0, 16), (1, 8))),
        "norm_gain": jnp.clip(jax.random.uniform(streams_of[1], (CH,), jnp.float32, 0.5, 1.5), 0.5, 1.5),
        "norm_shift": bell_draw(streams_of[2], (CH,), 0.5, 3.0, (), jnp.float32),
        "proj_weight": bell_draw(streams_of[3], (CH, 4 * HID + CH), CH ** -0.5, 0.5),
        "proj_bias": bell_draw(streams_of[4], (4 * HID + CH,), 0.5, 3.0, (), jnp.float32),
        "mid_gain": jnp.clip(jax.random.uniform(streams_of[5], (HID,), jnp.float32, 0.5, 1.5), 0.5, 1.5),
        "mid_shift": bell_draw(streams_of[6], (HID,), 0.5, 3.0, (), jnp.float32),
        "out_weight": bell_draw(streams_of[7], (HID, CH), (HID // 4) ** -0.5, 1.5),
        "out_bias": bell_draw(streams_of[8], (CH,), 0.5, 3.0, (), jnp.float32),
        "conv_gain": jnp.clip(jax.random.uniform(streams_of[9], (2, CH), jnp.float32, 0.5, 1.5), 0.5, 1.5),
        "conv_shift": bell_draw(streams_of[10], (2, CH), 0.5, 3.0, (), jnp.float32),
        "convolution_weight": bell_draw(streams_of[11], (2, 9, CH, CH), (2 * CH) ** -0.5, 0.375),
        "convolution_bias": bell_draw(streams_of[12], (2, CH), 0.3, 2.0, (), jnp.float32),
    }


EPS = 1e-05

def normalize(values, gain, shift):
    mean = lax.optimization_barrier(jnp.mean(values, axis=-1, keepdims=True))
    centred = values - mean
    spread = lax.optimization_barrier(jnp.mean(centred * centred, axis=-1, keepdims=True))
    return centred * lax.rsqrt(spread + EPS) * gain + shift

def apply_convolution(source, kernel, spacing):
    width = source.shape[2]
    result = lax.conv_general_dilated(source[None], kernel.reshape(3, 3, width, width), (1, 1), [(spacing, spacing), (spacing, spacing)], rhs_dilation=(spacing, spacing), dimension_numbers=('NHWC', 'HWIO', 'NHWC'), preferred_element_type=jnp.float32)
    return result[0]

def reference(pair, norm_gain, norm_shift, proj_weight, proj_bias, mid_gain, mid_shift, out_weight, out_bias, conv_gain, conv_shift, convolution_weight, convolution_bias):
    hidden = mid_gain.shape[0]

    def project_row(row_position):
        normed = normalize(row_position.astype(jnp.float32), norm_gain, norm_shift).astype(jnp.bfloat16)
        projected = jnp.dot(normed, proj_weight, preferred_element_type=jnp.float32) + proj_bias
        return projected

    def factor_row(row_position):
        projected = project_row(row_position)
        left_row = (jax.nn.sigmoid(projected[:, :hidden]) * projected[:, hidden:2 * hidden]).astype(jnp.bfloat16)
        right_row = (jax.nn.sigmoid(projected[:, 2 * hidden:3 * hidden]) * projected[:, 3 * hidden:4 * hidden]).astype(jnp.bfloat16)
        return (left_row, right_row)
    left, right = lax.map(factor_row, pair)
    triangle = jnp.einsum('ikc,jkc->ijc', left.astype(jnp.float32), right.astype(jnp.float32), precision=lax.Precision.HIGHEST)

    def update_row(operands):
        row_position, tri_row = operands
        projected = project_row(row_position)
        out_gate = jax.nn.sigmoid(projected[:, 4 * hidden:])
        mid = normalize(tri_row, mid_gain, mid_shift).astype(jnp.bfloat16)
        update = jnp.dot(mid, out_weight, preferred_element_type=jnp.float32) + out_bias
        return (row_position.astype(jnp.float32) + out_gate * update).astype(jnp.bfloat16)
    updated = lax.map(update_row, (pair, triangle)).astype(jnp.float32)
    symmetric = ((updated + jnp.transpose(updated, (1, 0, 2))) * 0.5).astype(jnp.bfloat16)
    symmetric_wide = symmetric.astype(jnp.float32)
    first_input = jax.nn.relu(normalize(symmetric_wide, conv_gain[0], conv_shift[0])).astype(jnp.bfloat16)
    first_result = symmetric_wide + convolution_bias[0] + apply_convolution(first_input, convolution_weight[0], FIRST_DILATION)
    second_input = jax.nn.relu(normalize(first_result, conv_gain[1], conv_shift[1])).astype(jnp.bfloat16)
    return (first_result + convolution_bias[1] + apply_convolution(second_input, convolution_weight[1], SECOND_DILATION)).astype(jnp.bfloat16)
```

```python
import jax
import jax.numpy as jnp
from jax import lax
from jax.experimental import pallas as pl
from jax.experimental.pallas import tpu as pltpu
from jax.sharding import PartitionSpec as P

FIRST_DILATION = 2
SECOND_DILATION = 4
HALO = FIRST_DILATION + SECOND_DILATION
EPS = 1e-05
BF = jnp.bfloat16
F32 = jnp.float32
MIB = 1 << 20
ROWS, COLS, CH, HID = 64, 128, 128, 64
NR, NC = 16, 8


def sigmoid(x):
    return 0.5 * jnp.tanh(0.5 * x) + 0.5


def normalize(values, gain, shift):
    mean = jnp.mean(values, axis=-1, keepdims=True)
    centred = values - mean
    spread = jnp.mean(centred * centred, axis=-1, keepdims=True)
    return centred * lax.rsqrt(spread + EPS) * gain + shift


NT = (((1,), (1,)), ((), ()))
TN = (((0,), (0,)), ((), ()))

STEP = 16


def factor_kernel(pair_ref, gain_ref, shift_ref, weight_ref, bias_ref, out_ref, lay_ref):
    step = pl.program_id(0)
    block = pair_ref[...]
    cells = block.astype(F32).reshape(STEP * COLS, CH)
    normed = normalize(cells, gain_ref[...], shift_ref[...]).astype(BF)
    projected = (
        lax.dot_general(weight_ref[...], normed, NT, preferred_element_type=F32) + bias_ref[...]
    )
    start = pl.multiple_of(step * STEP, STEP)
    for side in range(2):
        base = 2 * HID * side
        factor = sigmoid(projected[base : base + HID]) * projected[base + HID : base + 2 * HID]
        for row in range(STEP):
            lay_ref[pl.ds(row, HID, stride=STEP), :] = factor[:, row * COLS : (row + 1) * COLS]
        out_ref[:, side, :, 0, pl.ds(start, STEP), :] = (
            lay_ref[...].astype(BF).reshape(8, 8, STEP, COLS)
        )
    for row in range(STEP):
        for q in range(2):
            local = 2 * row + q
            group = step * 2 + local // 16
            side = (local // 8) % 2
            column = local % 8
            for half in range(2):
                out_ref[group, side, column, 1, half * 32 : half * 32 + 32, :] = pair_ref[
                    row, half * 64 + q * 32 : half * 64 + q * 32 + 32, :
                ]


def factors(pair, gain, shift, weight_t, bias_t):
    whole = lambda *shape: pl.BlockSpec(shape, lambda s: (0,) * len(shape))
    return pl.pallas_call(
        factor_kernel,
        grid=(ROWS // STEP,),
        out_shape=jax.ShapeDtypeStruct((8, 2, 8, 2, ROWS, COLS), BF),
        in_specs=[
            pl.BlockSpec((STEP, COLS, CH), lambda s: (s, 0, 0)),
            whole(1, CH),
            whole(1, CH),
            whole(4 * HID, CH),
            whole(4 * HID, 1),
        ],
        out_specs=whole(8, 2, 8, 2, ROWS, COLS),
        scratch_shapes=[pltpu.VMEM((HID * STEP, COLS), F32)],
        compiler_params=pltpu.CompilerParams(vmem_limit_bytes=40 * MIB),
        name="factors",
    )(pair, gain, shift, weight_t, bias_t)


def product_kernel(own_ref, moved_ref, other_ref, out_ref, rhs_ref):
    for col in range(NC):
        rhs_ref[:, col * COLS : (col + 1) * COLS] = other_ref[:, col].reshape(NR * ROWS, COLS)
    half = NR // 2
    for part in range(2):
        lhs = jnp.concatenate(
            [
                own_ref[part * half : (part + 1) * half, col, 0].reshape(half * ROWS, COLS)
                for col in range(NC)
            ],
            axis=1,
        )
        for block in range(4):
            result = lax.dot_general(
                lhs,
                rhs_ref[block * 256 : (block + 1) * 256, :],
                NT,
                preferred_element_type=F32,
            ).astype(BF)
            for col in range(2):
                out_ref[part * half : (part + 1) * half, block * 2 + col, 0] = result[
                    :, col * COLS : (col + 1) * COLS
                ].reshape(half, ROWS, COLS)
    for row in range(NR):
        for col in range(NC):
            side = row % 2
            for e in range(2):
                out_ref[row, col, 1, e * 32 : e * 32 + 32, :] = moved_ref[
                    2 * col + e, row // 2, 0, side * 32 : side * 32 + 32, :
                ]


def product(received, other):
    whole = lambda *shape: pl.BlockSpec(shape, lambda s: (0,) * len(shape))
    slot = lambda k: pl.BlockSpec((NR, NC, 1, ROWS, COLS), lambda s: (0, 0, k, 0, 0))
    return pl.pallas_call(
        product_kernel,
        grid=(1,),
        out_shape=jax.ShapeDtypeStruct((NR, NC, 2, ROWS, COLS), BF),
        in_specs=[slot(0), slot(1), whole(NR, NC, ROWS, COLS)],
        out_specs=whole(NR, NC, 2, ROWS, COLS),
        scratch_shapes=[pltpu.VMEM((NR * ROWS, NC * COLS), BF)],
        compiler_params=pltpu.CompilerParams(vmem_limit_bytes=48 * MIB),
        name="product",
    )(received, received, other)


def channel_normalize(values, gain, shift):
    mean = jnp.mean(values, axis=0, keepdims=True)
    centred = values - mean
    spread = jnp.mean(centred * centred, axis=0, keepdims=True)
    return centred * lax.rsqrt(spread + EPS) * gain + shift


USTEP = 16


def update_kernel(
    pair_ref, tri_ref, mirror_ref, gain_ref, shift_ref, gate_ref, gate_bias_ref,
    mid_gain_ref, mid_shift_ref, out_weight_ref, out_bias_ref, sym_ref, cells_ref, lay_ref,
):
    step = pl.program_id(0)

    @pl.when(step == 0)
    def _():
        for d in range(128):
            for e in range(2):
                at = (e * 64 + d // 2) * 64 + (d % 2) * 32
                cells_ref[at : at + 32, :] = mirror_ref[d, 0, e * 32 : e * 32 + 32, :].astype(F32)

    def gated(cells, side, row):
        normed = normalize(cells, gain_ref[...], shift_ref[...]).astype(BF)
        gate = sigmoid(
            jnp.dot(normed, gate_ref[...], preferred_element_type=F32) + gate_bias_ref[...]
        )
        mid = lay_ref[side, pl.ds(row, HID, stride=USTEP), :].astype(BF)
        change = (
            lax.dot_general(mid, out_weight_ref[...], TN, preferred_element_type=F32)
            + out_bias_ref[...]
        )
        return (cells + gate * change).astype(BF).astype(F32)

    for side in range(2):
        tri = tri_ref[:, side, :, 0].astype(F32).reshape(HID, USTEP, COLS)
        mid = channel_normalize(tri, mid_gain_ref[...], mid_shift_ref[...])
        lay_ref[side] = mid.reshape(HID * USTEP, COLS)

    def body(row, carry):
        own = gated(pair_ref[row].astype(F32), 0, row)
        mirrored = gated(cells_ref[pl.ds(step * USTEP + row, COLS, stride=ROWS), :], 1, row)
        sym_ref[row] = ((own + mirrored) * 0.5).astype(BF)
        return carry

    lax.fori_loop(0, USTEP, body, 0, unroll=4)


def update(pair, received, gain, shift, gate, gate_bias, mid_gain, mid_shift, out_weight, out_bias):
    whole = lambda *shape: pl.BlockSpec(shape, lambda s: (0,) * len(shape))
    tri = received.reshape(8, 2, 8, 2, ROWS, COLS)
    cells = received.reshape(128, 2, ROWS, COLS)
    return pl.pallas_call(
        update_kernel,
        grid=(ROWS // USTEP,),
        out_shape=jax.ShapeDtypeStruct((ROWS, COLS, CH), BF),
        in_specs=[
            pl.BlockSpec((USTEP, COLS, CH), lambda s: (s, 0, 0)),
            pl.BlockSpec((8, 2, 8, 1, USTEP, COLS), lambda s: (0, 0, 0, 0, s, 0)),
            pl.BlockSpec((128, 1, ROWS, COLS), lambda s: (0, 1, 0, 0)),
            whole(1, CH),
            whole(1, CH),
            whole(CH, CH),
            whole(1, CH),
            whole(HID, 1, 1),
            whole(HID, 1, 1),
            whole(HID, CH),
            whole(1, CH),
        ],
        out_specs=pl.BlockSpec((USTEP, COLS, CH), lambda s: (s, 0, 0)),
        scratch_shapes=[
            pltpu.VMEM((COLS * ROWS, CH), F32),
            pltpu.VMEM((2, HID * USTEP, COLS), F32),
        ],
        compiler_params=pltpu.CompilerParams(vmem_limit_bytes=48 * MIB),
        name="update",
    )(pair, tri, cells, gain, shift, gate, gate_bias, mid_gain, mid_shift, out_weight, out_bias)


TALL = ROWS + 2 * HALO
WIDE = 160
FIRST_TALL = ROWS + 2 * SECOND_DILATION
FIRST_WIDE = 144


def convolution_kernel(
    place_ref, sym_ref, top_ref, bottom_ref, low_ref, high_ref, gain_ref, shift_ref, bias_ref,
    weight_ref, out_ref, wide_ref, act_ref, cols_ref, first_ref, second_ref, second_cols_ref,
):
    row_at, col_at = place_ref[0], place_ref[1]

    def fill(row, carry):
        def put(centre):
            wide_ref[row, 0:16, :] = jnp.zeros((16, CH), F32)
            wide_ref[row, 144:160, :] = jnp.zeros((16, CH), F32)
            wide_ref[row, 16:144, :] = centre.astype(F32)
            wide_ref[row, 10:16, :] = low_ref[row].astype(F32)
            wide_ref[row, 144:150, :] = high_ref[row].astype(F32)

        @pl.when(row < HALO)
        def _():
            put(top_ref[row])

        @pl.when((row >= HALO) & (row < HALO + ROWS))
        def _():
            put(sym_ref[row - HALO])

        @pl.when(row >= HALO + ROWS)
        def _():
            put(bottom_ref[row - HALO - ROWS])

        act = jnp.maximum(
            normalize(wide_ref[row], gain_ref[0:1], shift_ref[0:1]), 0.0
        )
        column = lax.broadcasted_iota(jnp.int32, (WIDE, CH), 0) + (col_at - 16)
        inside_row = (row + row_at >= HALO) & (row + row_at < HALO + NR * ROWS)
        inside = (column >= 0) & (column < NC * COLS) & inside_row
        act_ref[...] = jnp.where(inside, act, 0.0)
        for tap in range(3):
            cols_ref[row, :, tap * CH : (tap + 1) * CH] = act_ref[
                6 + 2 * tap : 6 + 2 * tap + FIRST_WIDE, :
            ].astype(BF)
        return carry

    lax.fori_loop(0, TALL, fill, 0)

    group = 8

    def convolve_first(step, carry):
        at = step * group
        total = jnp.zeros((group * FIRST_WIDE, CH), F32)
        for tap in range(3):
            total = total + jnp.dot(
                cols_ref[pl.ds(at + 2 * tap, group)].reshape(group * FIRST_WIDE, 3 * CH),
                weight_ref[0, tap],
                preferred_element_type=F32,
            )
        first = (
            total.reshape(group, FIRST_WIDE, CH)
            + wide_ref[pl.ds(at + 2, group), 8:152, :]
            + bias_ref[0:1].reshape(1, 1, CH)
        )
        first_ref[pl.ds(at, group)] = first[:, 8:136]
        act = jnp.maximum(
            normalize(
                first, gain_ref[1:2].reshape(1, 1, CH), shift_ref[1:2].reshape(1, 1, CH)
            ),
            0.0,
        )
        row = lax.broadcasted_iota(jnp.int32, (group, FIRST_WIDE, CH), 0) + (row_at + at - 4)
        column = lax.broadcasted_iota(jnp.int32, (group, FIRST_WIDE, CH), 1) + (col_at - 8)
        inside = (row >= 0) & (row < NR * ROWS) & (column >= 0) & (column < NC * COLS)
        second_ref[...] = jnp.where(inside, act, 0.0)
        for tap in range(3):
            second_cols_ref[pl.ds(at, group), :, tap * CH : (tap + 1) * CH] = second_ref[
                :, 4 + 4 * tap : 4 + 4 * tap + COLS, :
            ].astype(BF)
        return carry

    lax.fori_loop(0, FIRST_TALL // group, convolve_first, 0)

    def convolve_second(step, carry):
        at = step * group
        total = jnp.zeros((group * COLS, CH), F32)
        for tap in range(3):
            total = total + jnp.dot(
                second_cols_ref[pl.ds(at + 4 * tap, group)].reshape(group * COLS, 3 * CH),
                weight_ref[1, tap],
                preferred_element_type=F32,
            )
        out_ref[pl.ds(at, group)] = (
            total.reshape(group, COLS, CH)
            + first_ref[pl.ds(at + 4, group)]
            + bias_ref[1:2].reshape(1, 1, CH)
        ).astype(BF)
        return carry

    lax.fori_loop(0, ROWS // group, convolve_second, 0)


def convolutions(place, sym, top, bottom, low, high, gain, shift, bias, weight):
    vmem = pl.BlockSpec(memory_space=pltpu.VMEM)
    return pl.pallas_call(
        convolution_kernel,
        out_shape=jax.ShapeDtypeStruct((ROWS, COLS, CH), BF),
        in_specs=[pl.BlockSpec(memory_space=pltpu.SMEM)] + [vmem] * 9,
        out_specs=vmem,
        scratch_shapes=[
            pltpu.VMEM((TALL, WIDE, CH), F32),
            pltpu.VMEM((WIDE, CH), F32),
            pltpu.VMEM((TALL, FIRST_WIDE, 3 * CH), BF),
            pltpu.VMEM((FIRST_TALL, COLS, CH), F32),
            pltpu.VMEM((8, FIRST_WIDE, CH), F32),
            pltpu.VMEM((FIRST_TALL, COLS, 3 * CH), BF),
        ],
        compiler_params=pltpu.CompilerParams(vmem_limit_bytes=56 * MIB),
        name="convolutions",
    )(place, sym, top, bottom, low, high, gain, shift, bias, weight)


def neighbours(low_strip, high_strip, axis):
    count = lax.axis_size(axis)
    forward = [(i, i + 1) for i in range(count - 1)]
    backward = [(i + 1, i) for i in range(count - 1)]
    return lax.ppermute(high_strip, axis, forward), lax.ppermute(low_strip, axis, backward)


def local(
    pair, norm_gain, norm_shift, proj_weight, proj_bias, mid_gain, mid_shift, out_weight, out_bias,
    conv_gain, conv_shift, convolution_weight, convolution_bias,
):
    gain, shift = norm_gain[None], norm_shift[None]
    sent = factors(
        pair, gain, shift, proj_weight[:, : 4 * HID].T, proj_bias[: 4 * HID, None]
    )
    received = lax.all_to_all(
        sent.reshape(128, 2, ROWS, COLS), ("row", "col"), split_axis=0, concat_axis=0, tiled=True
    ).reshape(NR, NC, 2, ROWS, COLS)
    other = lax.ppermute(received[:, :, 0], "row", [(i, i ^ 1) for i in range(NR)])
    back = product(received, other)
    returned = lax.all_to_all(
        back.reshape(128, 2, ROWS, COLS), ("row", "col"), split_axis=0, concat_axis=0, tiled=True
    )
    sym = update(
        pair, returned, gain, shift, proj_weight[:, 4 * HID :], proj_bias[None, 4 * HID :],
        mid_gain[:, None, None], mid_shift[:, None, None], out_weight, out_bias[None],
    )
    top, bottom = neighbours(sym[:HALO], sym[ROWS - HALO :], "row")
    edge = lambda low, high: jnp.concatenate(
        [top[:, low:high], sym[:, low:high], bottom[:, low:high]], axis=0
    )
    low, high = neighbours(edge(0, HALO), edge(COLS - HALO, COLS), "col")
    place = jnp.stack([lax.axis_index("row") * ROWS, lax.axis_index("col") * COLS]).astype(jnp.int32)
    return convolutions(
        place, sym, top, bottom, low, high, conv_gain, conv_shift, convolution_bias,
        convolution_weight.reshape(2, 3, 3 * CH, CH),
    )


def solution(mesh):
    return jax.shard_map(
        local,
        mesh=mesh,
        in_specs=(P("row", "col", None),) + (P(),) * 12,
        out_specs=P("row", "col", None),
        check_vma=False,
    )
```

```python
import jax
import jax.numpy as jnp
from jax import lax
from jax.experimental import pallas as pl
from jax.experimental.pallas import tpu as pltpu
from jax.sharding import PartitionSpec as P

FIRST_DILATION = 2
SECOND_DILATION = 4
HALO = FIRST_DILATION + SECOND_DILATION
EPS = 1e-05
BF = jnp.bfloat16
F32 = jnp.float32
MIB = 1 << 20
ROWS, COLS, CH, HID = 64, 128, 128, 64
NR, NC = 16, 8


def sigmoid(x):
    return 0.5 * jnp.tanh(0.5 * x) + 0.5


def normalize(values, gain, shift):
    mean = jnp.mean(values, axis=-1, keepdims=True)
    centred = values - mean
    spread = jnp.mean(centred * centred, axis=-1, keepdims=True)
    return centred * lax.rsqrt(spread + EPS) * gain + shift


NT = (((1,), (1,)), ((), ()))
TN = (((0,), (0,)), ((), ()))

STEP = 16


def factor_kernel(pair_ref, gain_ref, shift_ref, weight_ref, bias_ref, out_ref, lay_ref):
    step = pl.program_id(0)
    block = pair_ref[...]
    cells = block.astype(F32).reshape(STEP * COLS, CH)
    normed = normalize(cells, gain_ref[...], shift_ref[...]).astype(BF)
    bias = jnp.transpose(jnp.broadcast_to(bias_ref[:, : 4 * HID], (COLS, 4 * HID)))
    projected = lax.dot_general(
        weight_ref[:, : 4 * HID], normed, (((0,), (1,)), ((), ())), preferred_element_type=F32
    )
    start = pl.multiple_of(step * STEP, STEP)
    for side in range(2):
        base = 2 * HID * side
        for row in range(STEP):
            part = slice(row * COLS, (row + 1) * COLS)
            gate = projected[base : base + HID, part] + bias[base : base + HID]
            value = projected[base + HID : base + 2 * HID, part] + bias[base + HID : base + 2 * HID]
            lay_ref[pl.ds(row, HID, stride=STEP), :] = sigmoid(gate) * value
        out_ref[:, side, :, 0, pl.ds(start, STEP), :] = (
            lay_ref[...].astype(BF).reshape(8, 8, STEP, COLS)
        )
    for row in range(STEP):
        for q in range(2):
            local = 2 * row + q
            group = step * 2 + local // 16
            side = (local // 8) % 2
            column = local % 8
            for half in range(2):
                out_ref[group, side, column, 1, half * 32 : half * 32 + 32, :] = pair_ref[
                    row, half * 64 + q * 32 : half * 64 + q * 32 + 32, :
                ]


FACTORS_VMEM = 60


def factors(pair, gain, shift, weight, bias):
    whole = lambda *shape: pl.BlockSpec(shape, lambda s: (0,) * len(shape))
    return pl.pallas_call(
        factor_kernel,
        grid=(ROWS // STEP,),
        out_shape=jax.ShapeDtypeStruct((8, 2, 8, 2, ROWS, COLS), BF),
        in_specs=[
            pl.BlockSpec((STEP, COLS, CH), lambda s: (s, 0, 0)),
            whole(1, CH),
            whole(1, CH),
            whole(CH, 4 * HID + CH),
            whole(1, 4 * HID + CH),
        ],
        out_specs=whole(8, 2, 8, 2, ROWS, COLS),
        scratch_shapes=[pltpu.VMEM((HID * STEP, COLS), F32)],
        compiler_params=pltpu.CompilerParams(vmem_limit_bytes=FACTORS_VMEM * MIB),
        name="factors",
    )(pair, gain, shift, weight, bias)


def product_kernel(own_ref, moved_ref, other_ref, out_ref, rhs_ref):
    for col in range(NC):
        rhs_ref[:, col * COLS : (col + 1) * COLS] = other_ref[:, col].reshape(NR * ROWS, COLS)
    half = NR // 2
    for part in range(2):
        lhs = jnp.concatenate(
            [
                own_ref[part * half : (part + 1) * half, col, 0].reshape(half * ROWS, COLS)
                for col in range(NC)
            ],
            axis=1,
        )
        for block in range(4):
            result = lax.dot_general(
                lhs,
                rhs_ref[block * 256 : (block + 1) * 256, :],
                NT,
                preferred_element_type=F32,
            ).astype(BF)
            for col in range(2):
                out_ref[part * half : (part + 1) * half, block * 2 + col, 0] = result[
                    :, col * COLS : (col + 1) * COLS
                ].reshape(half, ROWS, COLS)
    for row in range(NR):
        for col in range(NC):
            side = row % 2
            for e in range(2):
                out_ref[row, col, 1, e * 32 : e * 32 + 32, :] = moved_ref[
                    2 * col + e, row // 2, 0, side * 32 : side * 32 + 32, :
                ]


def product(received, other):
    whole = lambda *shape: pl.BlockSpec(shape, lambda s: (0,) * len(shape))
    slot = lambda k: pl.BlockSpec((NR, NC, 1, ROWS, COLS), lambda s: (0, 0, k, 0, 0))
    return pl.pallas_call(
        product_kernel,
        grid=(1,),
        out_shape=jax.ShapeDtypeStruct((NR, NC, 2, ROWS, COLS), BF),
        in_specs=[slot(0), slot(1), whole(NR, NC, ROWS, COLS)],
        out_specs=whole(NR, NC, 2, ROWS, COLS),
        scratch_shapes=[pltpu.VMEM((NR * ROWS, NC * COLS), BF)],
        compiler_params=pltpu.CompilerParams(vmem_limit_bytes=48 * MIB),
        name="product",
    )(received, received, other)


def gate_kernel(pair_ref, gain_ref, shift_ref, weight_ref, bias_ref, out_ref):
    cells = pair_ref[...].astype(F32).reshape(STEP * COLS, CH)
    normed = normalize(cells, gain_ref[...], shift_ref[...]).astype(BF)
    gate = jnp.dot(normed, weight_ref[...], preferred_element_type=F32) + bias_ref[...]
    out_ref[...] = sigmoid(gate).reshape(STEP, COLS, CH)


def gates(pair, gain, shift, weight, bias):
    whole = lambda *shape: pl.BlockSpec(shape, lambda s: (0,) * len(shape))
    block = pl.BlockSpec((STEP, COLS, CH), lambda s: (s, 0, 0))
    return pl.pallas_call(
        gate_kernel,
        grid=(ROWS // STEP,),
        out_shape=jax.ShapeDtypeStruct((ROWS, COLS, CH), F32),
        in_specs=[block, whole(1, CH), whole(1, CH), whole(CH, CH), whole(1, CH)],
        out_specs=block,
        compiler_params=pltpu.CompilerParams(vmem_limit_bytes=24 * MIB),
        cost_estimate=pl.CostEstimate(
            flops=2 * ROWS * COLS * CH * CH, bytes_accessed=6 * ROWS * COLS * CH, transcendentals=ROWS * COLS * CH
        ),
        name="gates",
    )(pair, gain, shift, weight, bias)


USTEP = 16
UNROLL_U = 1
UGROUP = 8
PITCH = 72


def update_kernel(
    pair_ref, own_gate_ref, tri_ref, mirror_ref, gain_ref, shift_ref, gate_ref, gate_bias_ref,
    out_weight_ref, out_bias_ref, sym_ref, cells_ref, lay_ref,
):
    step = pl.program_id(0)

    @pl.when(step == 0)
    def _():
        for d in range(128):
            for e in range(2):
                at = (e * 64 + d // 2) * PITCH + (d % 2) * 32
                cells_ref[at : at + 32, :] = mirror_ref[d, 0, e * 32 : e * 32 + 32, :].astype(F32)

    tri = tri_ref[:, :, :, 0].astype(F32)
    mean = jnp.mean(tri, axis=(0, 2), keepdims=True)
    centred = tri - mean
    spread = jnp.mean(centred * centred, axis=(0, 2), keepdims=True)
    lay_ref[...] = (centred * lax.rsqrt(spread + EPS)).reshape(2 * HID * USTEP, COLS)

    def body(part, carry):
        first = part * UGROUP
        change, cells = [], []
        for k in range(UGROUP):
            mid = lay_ref[pl.ds(first + k, 2 * HID, stride=USTEP), :].astype(BF)
            change.append(
                lax.dot_general(mid, out_weight_ref[...], TN, preferred_element_type=F32)
            )
            cells.append(
                cells_ref[pl.ds(step * USTEP + first + k, COLS, stride=PITCH), :]
            )
        change = jnp.concatenate(change, axis=0) + out_bias_ref[...]
        cells = jnp.concatenate(cells, axis=0)
        size = UGROUP * COLS
        own = (
            pair_ref[pl.ds(first, UGROUP)].astype(F32).reshape(size, CH)
            + own_gate_ref[pl.ds(first, UGROUP)].reshape(size, CH) * change[:, :CH]
        )
        normed = normalize(cells, gain_ref[...], shift_ref[...]).astype(BF)
        gate = sigmoid(
            jnp.dot(normed, gate_ref[...], preferred_element_type=F32) + gate_bias_ref[...]
        )
        mirrored = cells + gate * change[:, CH:]
        total = own.astype(BF).astype(F32) + mirrored.astype(BF).astype(F32)
        sym_ref[pl.ds(first, UGROUP)] = (total * 0.5).astype(BF).reshape(UGROUP, COLS, CH)
        return carry

    lax.fori_loop(0, USTEP // UGROUP, body, 0, unroll=UNROLL_U)


def update(pair, own_gate, received, gain, shift, gate, gate_bias, out_weight, out_bias):
    whole = lambda *shape: pl.BlockSpec(shape, lambda s: (0,) * len(shape))
    tri = received.reshape(8, 2, 8, 2, ROWS, COLS)
    cells = received.reshape(128, 2, ROWS, COLS)
    block = pl.BlockSpec((USTEP, COLS, CH), lambda s: (s, 0, 0))
    return pl.pallas_call(
        update_kernel,
        grid=(ROWS // USTEP,),
        out_shape=jax.ShapeDtypeStruct((ROWS, COLS, CH), BF),
        in_specs=[
            block,
            block,
            pl.BlockSpec((8, 2, 8, 1, USTEP, COLS), lambda s: (0, 0, 0, 0, s, 0)),
            pl.BlockSpec((128, 1, ROWS, COLS), lambda s: (0, 1, 0, 0)),
            whole(1, CH),
            whole(1, CH),
            whole(CH, CH),
            whole(1, CH),
            whole(2 * HID, 2 * CH),
            whole(1, 2 * CH),
        ],
        out_specs=block,
        scratch_shapes=[
            pltpu.VMEM((COLS * PITCH, CH), F32),
            pltpu.VMEM((2 * HID * USTEP, COLS), F32),
        ],
        compiler_params=pltpu.CompilerParams(vmem_limit_bytes=48 * MIB),
        name="update",
    )(pair, own_gate, tri, cells, gain, shift, gate, gate_bias, out_weight, out_bias)


def output_weight(weight, bias, gain, shift):
    scaled = (gain[:, None] * weight.astype(F32)).astype(BF).reshape(8, 1, 8, CH)
    nothing = jnp.zeros_like(scaled)
    own = jnp.concatenate([scaled, nothing], axis=1)
    mirrored = jnp.concatenate([nothing, scaled], axis=1)
    full = jnp.concatenate([own, mirrored], axis=3).reshape(2 * HID, 2 * CH)
    offset = bias + jnp.sum(shift[:, None] * weight.astype(F32), axis=0)
    return full, jnp.concatenate([offset, offset])[None]


TALL = ROWS + 2 * HALO
SIDE = 8
WIDE = COLS + 2 * SIDE
FIRST_TALL = ROWS + 2 * SECOND_DILATION
GROUP_A, GROUP_B, GROUP_C = 4, 4, 8
UNROLL_A, UNROLL_B = 2, 6


def convolution_kernel(
    place_ref, sym_ref, top_ref, bottom_ref, low_ref, high_ref, gain_ref, shift_ref, bias_ref,
    weight_hbm, out_hbm, tall_ref, act_ref, cols_ref, first_ref, second_ref, second_cols_ref,
    weight_ref, out_ref, sems, out_sems,
):
    def rows_copy(k):
        return pltpu.make_async_copy(
            sym_ref.at[16 * k : 16 * k + 16],
            tall_ref.at[HALO + 16 * k : HALO + 16 * k + 16],
            sems.at[k],
        )

    top_copy = pltpu.make_async_copy(top_ref, tall_ref.at[0:HALO], sems.at[4])
    bottom_copy = pltpu.make_async_copy(bottom_ref, tall_ref.at[HALO + ROWS : TALL], sems.at[5])
    weight_copy = pltpu.make_async_copy(weight_hbm, weight_ref, sems.at[6])
    top_copy.start()
    for k in range(4):
        rows_copy(k).start()
    bottom_copy.start()
    weight_copy.start()
    above = place_ref[0] > 0
    below = place_ref[0] < (NR - 1) * ROWS
    low_ok = (place_ref[1] > 0).astype(F32)
    high_ok = (place_ref[1] < (NC - 1) * COLS).astype(F32)
    act_ref[...] = jnp.zeros((GROUP_A, WIDE + 16, CH), F32)

    def values(at, count):
        return jnp.concatenate(
            [
                low_ref[pl.ds(at, count)].astype(F32),
                tall_ref[pl.ds(at, count)].astype(F32),
                high_ref[pl.ds(at, count)].astype(F32),
            ],
            axis=1,
        )

    def activate(cells, which):
        return jnp.maximum(
            normalize(
                cells,
                gain_ref[which : which + 1].reshape(1, 1, CH),
                shift_ref[which : which + 1].reshape(1, 1, CH),
            ),
            0.0,
        )

    def prepare(step, carry):
        at = step * GROUP_A
        act = activate(values(at, GROUP_A), 0)
        act_ref[:, 8:16, :] = act[:, :SIDE] * low_ok
        act_ref[:, 16 : 16 + COLS, :] = act[:, SIDE : SIDE + COLS]
        act_ref[:, 16 + COLS : 24 + COLS, :] = act[:, SIDE + COLS :] * high_ok
        for tap in range(3):
            cols_ref[pl.ds(at, GROUP_A), :, tap * CH : (tap + 1) * CH] = act_ref[
                :, 6 + 2 * tap : 6 + 2 * tap + WIDE, :
            ].astype(BF)
        return carry

    top_copy.wait()
    begin = 0
    for k, end in enumerate((20, 36, 52, TALL)):
        rows_copy(k).wait()
        if k == 3:
            bottom_copy.wait()
        lax.fori_loop(begin // GROUP_A, end // GROUP_A, prepare, 0, unroll=UNROLL_A)
        begin = end
    weight_copy.wait()

    @pl.when(jnp.logical_not(above))
    def _():
        cols_ref[0:HALO] = jnp.zeros((HALO, WIDE, 3 * CH), BF)

    @pl.when(jnp.logical_not(below))
    def _():
        cols_ref[HALO + ROWS :] = jnp.zeros((HALO, WIDE, 3 * CH), BF)

    def paired(source_ref, at, spacing, group, width, which):
        sets = group // (2 * spacing)
        lhs = jnp.concatenate(
            [
                jnp.concatenate(
                    [
                        source_ref[pl.ds(at + 2 * spacing * k + spacing * slot, spacing)]
                        for k in range(sets)
                    ],
                    axis=0,
                ).reshape(group // 2 * width, 3 * CH)
                for slot in range(4)
            ],
            axis=1,
        )
        total = jnp.dot(lhs, weight_ref[which], preferred_element_type=F32)
        near = total[:, :CH].reshape(sets, spacing, width, CH)
        far = total[:, CH:].reshape(sets, spacing, width, CH)
        return jnp.concatenate([near, far], axis=1).reshape(group, width, CH)

    def convolve_first(step, carry):
        at = step * GROUP_B
        first = (
            paired(cols_ref, at, FIRST_DILATION, GROUP_B, WIDE, 0)
            + values(at + 2, GROUP_B)
            + bias_ref[0:1].reshape(1, 1, CH)
        )
        first_ref[pl.ds(at, GROUP_B)] = first[:, SIDE : SIDE + COLS]
        act = activate(first, 1)
        second_ref[:, :SIDE, :] = act[:, :SIDE] * low_ok
        second_ref[:, SIDE : SIDE + COLS, :] = act[:, SIDE : SIDE + COLS]
        second_ref[:, SIDE + COLS :, :] = act[:, SIDE + COLS :] * high_ok
        for tap in range(3):
            second_cols_ref[pl.ds(at, GROUP_B), :, tap * CH : (tap + 1) * CH] = second_ref[
                :, 4 + 4 * tap : 4 + 4 * tap + COLS, :
            ].astype(BF)
        return carry

    lax.fori_loop(0, FIRST_TALL // GROUP_B, convolve_first, 0, unroll=UNROLL_B)

    @pl.when(jnp.logical_not(above))
    def _():
        second_cols_ref[0:SECOND_DILATION] = jnp.zeros((SECOND_DILATION, COLS, 3 * CH), BF)

    @pl.when(jnp.logical_not(below))
    def _():
        second_cols_ref[SECOND_DILATION + ROWS :] = jnp.zeros(
            (SECOND_DILATION, COLS, 3 * CH), BF
        )

    def out_copy(k):
        return pltpu.make_async_copy(
            out_ref.at[16 * k : 16 * k + 16], out_hbm.at[16 * k : 16 * k + 16], out_sems.at[k]
        )

    for k in range(4):
        for part in range(16 // GROUP_C):
            at = 16 * k + part * GROUP_C
            out_ref[at : at + GROUP_C] = (
                paired(second_cols_ref, at, SECOND_DILATION, GROUP_C, COLS, 1)
                + first_ref[at + 4 : at + 4 + GROUP_C]
                + bias_ref[1:2].reshape(1, 1, CH)
            ).astype(BF)
        out_copy(k).start()
    for k in range(4):
        out_copy(k).wait()


def convolutions(place, sym, top, bottom, low, high, gain, shift, bias, weight):
    vmem = pl.BlockSpec(memory_space=pltpu.VMEM)
    anywhere = pl.BlockSpec(memory_space=pl.ANY)
    return pl.pallas_call(
        convolution_kernel,
        out_shape=jax.ShapeDtypeStruct((ROWS, COLS, CH), BF),
        in_specs=[pl.BlockSpec(memory_space=pltpu.SMEM)] + [anywhere] * 3 + [vmem] * 5 + [anywhere],
        out_specs=anywhere,
        scratch_shapes=[
            pltpu.VMEM((TALL, COLS, CH), BF),
            pltpu.VMEM((GROUP_A, WIDE + 16, CH), F32),
            pltpu.VMEM((TALL, WIDE, 3 * CH), BF),
            pltpu.VMEM((FIRST_TALL, COLS, CH), F32),
            pltpu.VMEM((GROUP_B, WIDE, CH), F32),
            pltpu.VMEM((FIRST_TALL, COLS, 3 * CH), BF),
            pltpu.VMEM((2, 12 * CH, 2 * CH), BF),
            pltpu.VMEM((ROWS, COLS, CH), BF),
            pltpu.SemaphoreType.DMA((7,)),
            pltpu.SemaphoreType.DMA((4,)),
        ],
        compiler_params=pltpu.CompilerParams(vmem_limit_bytes=44 * MIB),
        name="convolutions",
    )(place, sym, top, bottom, low, high, gain, shift, bias, weight)


def paired_weight(weight):
    taps = weight.reshape(3, 3 * CH, CH)
    near = jnp.concatenate([taps, jnp.zeros_like(taps[:1])], axis=0)
    far = jnp.concatenate([jnp.zeros_like(taps[:1]), taps], axis=0)
    return jnp.concatenate([near, far], axis=2).reshape(12 * CH, 2 * CH)


def neighbours(low_strip, high_strip, axis):
    count = lax.axis_size(axis)
    forward = [(i, i + 1) for i in range(count - 1)]
    backward = [(i + 1, i) for i in range(count - 1)]
    return lax.ppermute(high_strip, axis, forward), lax.ppermute(low_strip, axis, backward)


def local(
    pair, norm_gain, norm_shift, proj_weight, proj_bias, mid_gain, mid_shift, out_weight, out_bias,
    conv_gain, conv_shift, convolution_weight, convolution_bias,
):
    gain, shift = norm_gain[None], norm_shift[None]
    sent = factors(pair, gain, shift, proj_weight, proj_bias[None])
    received = lax.all_to_all(
        sent.reshape(128, 2, ROWS, COLS), ("row", "col"), split_axis=0, concat_axis=0, tiled=True
    ).reshape(NR, NC, 2, ROWS, COLS)
    other = lax.ppermute(received[:, :, 0], "row", [(i, i ^ 1) for i in range(NR)])
    back = product(received, other)
    returned = lax.all_to_all(
        back.reshape(128, 2, ROWS, COLS), ("row", "col"), split_axis=0, concat_axis=0, tiled=True
    )
    gate, gate_bias = proj_weight[:, 4 * HID :], proj_bias[None, 4 * HID :]
    sym = update(
        pair, gates(pair, gain, shift, gate, gate_bias), returned, gain, shift, gate, gate_bias,
        *output_weight(out_weight, out_bias, mid_gain, mid_shift),
    )
    top, bottom = neighbours(sym[:HALO], sym[ROWS - HALO :], "row")
    edge = lambda low, high: jnp.concatenate(
        [top[:, low:high], sym[:, low:high], bottom[:, low:high]], axis=0
    )
    low, high = neighbours(edge(0, SIDE), edge(COLS - SIDE, COLS), "col")
    place = jnp.stack([lax.axis_index("row") * ROWS, lax.axis_index("col") * COLS]).astype(jnp.int32)
    return convolutions(
        place, sym, top, bottom, low, high, conv_gain, conv_shift, convolution_bias,
        jnp.stack([paired_weight(convolution_weight[0]), paired_weight(convolution_weight[1])]),
    )


def solution(mesh):
    return jax.shard_map(
        local,
        mesh=mesh,
        in_specs=(P("row", "col", None),) + (P(),) * 12,
        out_specs=P("row", "col", None),
        check_vma=False,
    )
```

```python
import jax
import jax.numpy as jnp
from jax import lax
from jax.experimental import pallas as pl
from jax.experimental.pallas import tpu as pltpu
from jax.sharding import PartitionSpec as P

FIRST_DILATION = 2
SECOND_DILATION = 4
HALO = FIRST_DILATION + SECOND_DILATION
EPS = 1e-05
BF = jnp.bfloat16
F32 = jnp.float32
MIB = 1 << 20
ROWS, COLS, CH, HID = 64, 128, 128, 64
NR, NC = 16, 8


def sigmoid(x):
    return 0.5 * jnp.tanh(0.5 * x) + 0.5


def normalize(values, gain, shift):
    mean = jnp.mean(values, axis=-1, keepdims=True)
    centred = values - mean
    spread = jnp.mean(centred * centred, axis=-1, keepdims=True)
    return centred * lax.rsqrt(spread + EPS) * gain + shift


NT = (((1,), (1,)), ((), ()))
TN = (((0,), (0,)), ((), ()))

STEP = 16


def factor_kernel(
    pair_ref, gain_ref, shift_ref, weight_ref, bias_ref, out_ref, lay_ref, stage_ref, cells_ref,
    cell_sems, stage_sems,
):
    step = pl.program_id(0)

    def cell_copy(k):
        return pltpu.make_async_copy(
            cells_ref.at[k], out_ref.at[pl.ds(2 * k, 2), :, :, :, 1], cell_sems.at[k]
        )

    def stage_copy(k):
        start = pl.multiple_of(k * STEP, STEP)
        return pltpu.make_async_copy(
            stage_ref.at[k], out_ref.at[:, :, :, :, 0, pl.ds(start, STEP), :], stage_sems.at[k]
        )

    for row in range(STEP):
        for q in range(2):
            for half in range(2):
                start = half * 64 + q * 32
                cells_ref[
                    step, row // 8, (row // 4) % 2, row % 4, q, half * 32 : half * 32 + 32, :
                ] = pair_ref[row, start : start + 32, :]
    cell_copy(step).start()
    cells = pair_ref[...].astype(F32).reshape(STEP * COLS, CH)
    normed = normalize(cells, gain_ref[...], shift_ref[...]).astype(BF)
    bias = jnp.transpose(jnp.broadcast_to(bias_ref[:, : 4 * HID], (COLS, 4 * HID)))
    projected = lax.dot_general(
        weight_ref[:, : 4 * HID], normed, (((0,), (1,)), ((), ())), preferred_element_type=F32
    )
    for side in range(2):
        base = 2 * HID * side
        for row in range(STEP):
            part = slice(row * COLS, (row + 1) * COLS)
            gate = projected[base : base + HID, part] + bias[base : base + HID]
            value = projected[base + HID : base + 2 * HID, part] + bias[base + HID : base + 2 * HID]
            lay_ref[pl.ds(row, HID, stride=STEP), :] = sigmoid(gate) * value
        stage_ref[step, :, side] = lay_ref[...].astype(BF).reshape(8, 4, 2, STEP, COLS)
    stage_copy(step).start()

    @pl.when(step == ROWS // STEP - 1)
    def _():
        for k in range(ROWS // STEP):
            cell_copy(k).wait()
            stage_copy(k).wait()


FACTORS_VMEM = 60


def factors(pair, gain, shift, weight, bias):
    whole = lambda *shape: pl.BlockSpec(shape, lambda s: (0,) * len(shape))
    steps = ROWS // STEP
    return pl.pallas_call(
        factor_kernel,
        grid=(steps,),
        out_shape=jax.ShapeDtypeStruct((8, 2, 4, 2, 2, ROWS, COLS), BF),
        in_specs=[
            pl.BlockSpec((STEP, COLS, CH), lambda s: (s, 0, 0)),
            whole(1, CH),
            whole(1, CH),
            whole(CH, 4 * HID + CH),
            whole(1, 4 * HID + CH),
        ],
        out_specs=pl.BlockSpec(memory_space=pl.ANY),
        scratch_shapes=[
            pltpu.VMEM((HID * STEP, COLS), F32),
            pltpu.VMEM((steps, 8, 2, 4, 2, STEP, COLS), BF),
            pltpu.VMEM((steps, 2, 2, 4, 2, ROWS, COLS), BF),
            pltpu.SemaphoreType.DMA((steps,)),
            pltpu.SemaphoreType.DMA((steps,)),
        ],
        compiler_params=pltpu.CompilerParams(vmem_limit_bytes=FACTORS_VMEM * MIB),
        name="factors",
    )(pair, gain, shift, weight, bias)


def plane_kernel(received_ref, out_ref, hold_ref, in_sems, out_sems):
    parts = [slice(k * NR // 4, (k + 1) * NR // 4) for k in range(4)]
    inward = [
        pltpu.make_async_copy(received_ref.at[part, :, 0], hold_ref.at[part], in_sems.at[k])
        for k, part in enumerate(parts)
    ]
    outward = [
        pltpu.make_async_copy(hold_ref.at[part], out_ref.at[part], out_sems.at[k])
        for k, part in enumerate(parts)
    ]
    for copy in inward:
        copy.start()
    for k in range(4):
        inward[k].wait()
        outward[k].start()
    for copy in outward:
        copy.wait()


def plane(received):
    return pl.pallas_call(
        plane_kernel,
        out_shape=jax.ShapeDtypeStruct((NR, NC, ROWS, COLS), BF),
        in_specs=[pl.BlockSpec(memory_space=pl.ANY)],
        out_specs=pl.BlockSpec(memory_space=pl.ANY),
        scratch_shapes=[
            pltpu.VMEM((NR, NC, ROWS, COLS), BF),
            pltpu.SemaphoreType.DMA((4,)),
            pltpu.SemaphoreType.DMA((4,)),
        ],
        compiler_params=pltpu.CompilerParams(vmem_limit_bytes=PLANE_VMEM * MIB),
        name="plane",
    )(received)


PLANE_VMEM = 60
PRODUCT_VMEM = 60


def product_kernel(
    received_ref, other_ref, out_ref, lhs_ref, rhs_ref, result_ref, cells_ref,
    lhs_sems, rhs_sems, cell_sems, out_sems, cell_out_sem,
):
    half = NR // 2

    def columns(col):
        return slice(col * COLS, (col + 1) * COLS)

    lhs = [
        pltpu.make_async_copy(
            received_ref.at[:, side, col, 0],
            lhs_ref.at[side, :, :, columns(col)],
            lhs_sems.at[side, col],
        )
        for side in range(2)
        for col in range(NC)
    ]
    rhs = [
        pltpu.make_async_copy(
            other_ref.at[:, col], rhs_ref.at[:, :, columns(col)], rhs_sems.at[col]
        )
        for col in range(NC)
    ]
    cells = [
        pltpu.make_async_copy(
            received_ref.at[col, e, :, 1, side * 32 : side * 32 + 32, :],
            cells_ref.at[:, side, col, e * 32 : e * 32 + 32, :],
            cell_sems.at[col, e, side],
        )
        for col in range(NC)
        for e in range(2)
        for side in range(2)
    ]
    for copy in rhs + lhs + cells:
        copy.start()
    for copy in rhs:
        copy.wait()
    outs = []
    for side in range(2):
        for copy in lhs[side * NC : side * NC + NC]:
            copy.wait()
        own = lhs_ref[side].reshape(half * ROWS, NC * COLS)
        for block in range(4):
            result = lax.dot_general(
                own,
                rhs_ref[4 * block : 4 * block + 4].reshape(256, NC * COLS),
                NT,
                preferred_element_type=F32,
            ).astype(BF)
            for col in range(2):
                result_ref[side, :, block * 2 + col] = result[:, columns(col)].reshape(
                    half, ROWS, COLS
                )
        copy = pltpu.make_async_copy(
            result_ref.at[side], out_ref.at[:, side, :, 0], out_sems.at[side]
        )
        copy.start()
        outs.append(copy)
        if side == 0:
            for moved in cells:
                moved.wait()
            copy = pltpu.make_async_copy(cells_ref, out_ref.at[:, :, :, 1], cell_out_sem)
            copy.start()
            outs.append(copy)
    for copy in outs:
        copy.wait()


def product(received, other):
    anywhere = pl.BlockSpec(memory_space=pl.ANY)
    half = NR // 2
    return pl.pallas_call(
        product_kernel,
        out_shape=jax.ShapeDtypeStruct((half, 2, NC, 2, ROWS, COLS), BF),
        in_specs=[anywhere, anywhere],
        out_specs=anywhere,
        scratch_shapes=[
            pltpu.VMEM((2, half, ROWS, NC * COLS), BF),
            pltpu.VMEM((NR, ROWS, NC * COLS), BF),
            pltpu.VMEM((2, half, NC, ROWS, COLS), BF),
            pltpu.VMEM((half, 2, NC, ROWS, COLS), BF),
            pltpu.SemaphoreType.DMA((2, NC)),
            pltpu.SemaphoreType.DMA((NC,)),
            pltpu.SemaphoreType.DMA((NC, 2, 2)),
            pltpu.SemaphoreType.DMA((2,)),
            pltpu.SemaphoreType.DMA(()),
        ],
        compiler_params=pltpu.CompilerParams(vmem_limit_bytes=PRODUCT_VMEM * MIB),
        name="product",
    )(received.reshape(half, 2, NC, 2, ROWS, COLS), other)


def gate_kernel(pair_ref, gain_ref, shift_ref, weight_ref, bias_ref, out_ref):
    cells = pair_ref[...].astype(F32).reshape(STEP * COLS, CH)
    normed = normalize(cells, gain_ref[...], shift_ref[...]).astype(BF)
    gate = jnp.dot(normed, weight_ref[...], preferred_element_type=F32) + bias_ref[...]
    out_ref[...] = sigmoid(gate).reshape(STEP, COLS, CH)


def gates(pair, gain, shift, weight, bias):
    whole = lambda *shape: pl.BlockSpec(shape, lambda s: (0,) * len(shape))
    block = pl.BlockSpec((STEP, COLS, CH), lambda s: (s, 0, 0))
    return pl.pallas_call(
        gate_kernel,
        grid=(ROWS // STEP,),
        out_shape=jax.ShapeDtypeStruct((ROWS, COLS, CH), F32),
        in_specs=[block, whole(1, CH), whole(1, CH), whole(CH, CH), whole(1, CH)],
        out_specs=block,
        compiler_params=pltpu.CompilerParams(vmem_limit_bytes=24 * MIB),
        cost_estimate=pl.CostEstimate(
            flops=2 * ROWS * COLS * CH * CH, bytes_accessed=6 * ROWS * COLS * CH, transcendentals=ROWS * COLS * CH
        ),
        name="gates",
    )(pair, gain, shift, weight, bias)


USTEP = 16
UNROLL_U = 1
UGROUP = 8
PITCH = 72


def update_kernel(
    pair_ref, own_gate_ref, tri_ref, mirror_ref, gain_ref, shift_ref, gate_ref, gate_bias_ref,
    out_weight_ref, out_bias_ref, sym_ref, cells_ref, lay_ref,
):
    step = pl.program_id(0)

    @pl.when(step == 0)
    def _():
        for d in range(128):
            for e in range(2):
                at = (e * 64 + d // 2) * PITCH + (d % 2) * 32
                cells_ref[at : at + 32, :] = mirror_ref[d, 0, e * 32 : e * 32 + 32, :].astype(F32)

    tri = tri_ref[:, :, :, 0].astype(F32)
    mean = jnp.mean(tri, axis=(0, 2), keepdims=True)
    centred = tri - mean
    spread = jnp.mean(centred * centred, axis=(0, 2), keepdims=True)
    lay_ref[...] = (centred * lax.rsqrt(spread + EPS)).reshape(2 * HID * USTEP, COLS)

    def body(part, carry):
        first = part * UGROUP
        change, cells = [], []
        for k in range(UGROUP):
            mid = lay_ref[pl.ds(first + k, 2 * HID, stride=USTEP), :].astype(BF)
            change.append(
                lax.dot_general(mid, out_weight_ref[...], TN, preferred_element_type=F32)
            )
            cells.append(
                cells_ref[pl.ds(step * USTEP + first + k, COLS, stride=PITCH), :]
            )
        change = jnp.concatenate(change, axis=0) + out_bias_ref[...]
        cells = jnp.concatenate(cells, axis=0)
        size = UGROUP * COLS
        own = (
            pair_ref[pl.ds(first, UGROUP)].astype(F32).reshape(size, CH)
            + own_gate_ref[pl.ds(first, UGROUP)].reshape(size, CH) * change[:, :CH]
        )
        normed = normalize(cells, gain_ref[...], shift_ref[...]).astype(BF)
        gate = sigmoid(
            jnp.dot(normed, gate_ref[...], preferred_element_type=F32) + gate_bias_ref[...]
        )
        mirrored = cells + gate * change[:, CH:]
        total = own.astype(BF).astype(F32) + mirrored.astype(BF).astype(F32)
        sym_ref[pl.ds(first, UGROUP)] = (total * 0.5).astype(BF).reshape(UGROUP, COLS, CH)
        return carry

    lax.fori_loop(0, USTEP // UGROUP, body, 0, unroll=UNROLL_U)


def update(pair, own_gate, received, gain, shift, gate, gate_bias, out_weight, out_bias):
    whole = lambda *shape: pl.BlockSpec(shape, lambda s: (0,) * len(shape))
    tri = received.reshape(8, 2, 8, 2, ROWS, COLS)
    cells = received.reshape(128, 2, ROWS, COLS)
    block = pl.BlockSpec((USTEP, COLS, CH), lambda s: (s, 0, 0))
    return pl.pallas_call(
        update_kernel,
        grid=(ROWS // USTEP,),
        out_shape=jax.ShapeDtypeStruct((ROWS, COLS, CH), BF),
        in_specs=[
            block,
            block,
            pl.BlockSpec((8, 2, 8, 1, USTEP, COLS), lambda s: (0, 0, 0, 0, s, 0)),
            pl.BlockSpec((128, 1, ROWS, COLS), lambda s: (0, 1, 0, 0)),
            whole(1, CH),
            whole(1, CH),
            whole(CH, CH),
            whole(1, CH),
            whole(2 * HID, 2 * CH),
            whole(1, 2 * CH),
        ],
        out_specs=block,
        scratch_shapes=[
            pltpu.VMEM((COLS * PITCH, CH), F32),
            pltpu.VMEM((2 * HID * USTEP, COLS), F32),
        ],
        compiler_params=pltpu.CompilerParams(vmem_limit_bytes=48 * MIB),
        name="update",
    )(pair, own_gate, tri, cells, gain, shift, gate, gate_bias, out_weight, out_bias)


def output_weight(weight, bias, gain, shift):
    scaled = (gain[:, None] * weight.astype(F32)).astype(BF).reshape(8, 1, 8, CH)
    nothing = jnp.zeros_like(scaled)
    own = jnp.concatenate([scaled, nothing], axis=1)
    mirrored = jnp.concatenate([nothing, scaled], axis=1)
    full = jnp.concatenate([own, mirrored], axis=3).reshape(2 * HID, 2 * CH)
    offset = bias + jnp.sum(shift[:, None] * weight.astype(F32), axis=0)
    return full, jnp.concatenate([offset, offset])[None]


TALL = ROWS + 2 * HALO
SIDE = 8
WIDE = COLS + 2 * SIDE
FIRST_TALL = ROWS + 2 * SECOND_DILATION
GROUP_A, GROUP_B, GROUP_C = 4, 4, 8
UNROLL_A, UNROLL_B = 2, 6
CONV_VMEM = 62


def convolution_kernel(
    place_ref, sym_ref, top_ref, bottom_ref, low_ref, high_ref, gain_ref, shift_ref, bias_ref,
    weight_hbm, out_hbm, tall_ref, act_ref, cols_ref, first_ref, second_ref, second_cols_ref,
    weight_ref, out_ref, sems, out_sems,
):
    def rows_copy(k):
        return pltpu.make_async_copy(
            sym_ref.at[16 * k : 16 * k + 16],
            tall_ref.at[HALO + 16 * k : HALO + 16 * k + 16],
            sems.at[k],
        )

    top_copy = pltpu.make_async_copy(top_ref, tall_ref.at[0:HALO], sems.at[4])
    bottom_copy = pltpu.make_async_copy(bottom_ref, tall_ref.at[HALO + ROWS : TALL], sems.at[5])
    weight_copy = pltpu.make_async_copy(weight_hbm, weight_ref, sems.at[6])
    top_copy.start()
    for k in range(4):
        rows_copy(k).start()
    bottom_copy.start()
    weight_copy.start()
    above = place_ref[0] > 0
    below = place_ref[0] < (NR - 1) * ROWS
    low_ok = (place_ref[1] > 0).astype(F32)
    high_ok = (place_ref[1] < (NC - 1) * COLS).astype(F32)
    act_ref[...] = jnp.zeros((GROUP_A, WIDE + 16, CH), F32)

    def values(at, count):
        return jnp.concatenate(
            [
                low_ref[pl.ds(at, count)].astype(F32),
                tall_ref[pl.ds(at, count)].astype(F32),
                high_ref[pl.ds(at, count)].astype(F32),
            ],
            axis=1,
        )

    def activate(cells, which):
        return jnp.maximum(
            normalize(
                cells,
                gain_ref[which : which + 1].reshape(1, 1, CH),
                shift_ref[which : which + 1].reshape(1, 1, CH),
            ),
            0.0,
        )

    def prepare(step, carry):
        at = step * GROUP_A
        act = activate(values(at, GROUP_A), 0)
        act_ref[:, 8:16, :] = act[:, :SIDE] * low_ok
        act_ref[:, 16 : 16 + COLS, :] = act[:, SIDE : SIDE + COLS]
        act_ref[:, 16 + COLS : 24 + COLS, :] = act[:, SIDE + COLS :] * high_ok
        for tap in range(3):
            cols_ref[pl.ds(at, GROUP_A), :, tap * CH : (tap + 1) * CH] = act_ref[
                :, 6 + 2 * tap : 6 + 2 * tap + WIDE, :
            ].astype(BF)
        return carry

    top_copy.wait()
    begin = 0
    for k, end in enumerate((20, 36, 52, TALL)):
        rows_copy(k).wait()
        if k == 3:
            bottom_copy.wait()
        lax.fori_loop(begin // GROUP_A, end // GROUP_A, prepare, 0, unroll=UNROLL_A)
        begin = end
    weight_copy.wait()

    @pl.when(jnp.logical_not(above))
    def _():
        cols_ref[0:HALO] = jnp.zeros((HALO, WIDE, 3 * CH), BF)

    @pl.when(jnp.logical_not(below))
    def _():
        cols_ref[HALO + ROWS :] = jnp.zeros((HALO, WIDE, 3 * CH), BF)

    def paired(source_ref, at, spacing, group, width, which):
        sets = group // (2 * spacing)
        lhs = jnp.concatenate(
            [
                jnp.concatenate(
                    [
                        source_ref[pl.ds(at + 2 * spacing * k + spacing * slot, spacing)]
                        for k in range(sets)
                    ],
                    axis=0,
                ).reshape(group // 2 * width, 3 * CH)
                for slot in range(4)
            ],
            axis=1,
        )
        total = jnp.dot(lhs, weight_ref[which], preferred_element_type=F32)
        near = total[:, :CH].reshape(sets, spacing, width, CH)
        far = total[:, CH:].reshape(sets, spacing, width, CH)
        return jnp.concatenate([near, far], axis=1).reshape(group, width, CH)

    def convolve_first(step, carry):
        at = step * GROUP_B
        first = (
            paired(cols_ref, at, FIRST_DILATION, GROUP_B, WIDE, 0)
            + values(at + 2, GROUP_B)
            + bias_ref[0:1].reshape(1, 1, CH)
        )
        first_ref[pl.ds(at, GROUP_B)] = first[:, SIDE : SIDE + COLS]
        act = activate(first, 1)
        second_ref[:, :SIDE, :] = act[:, :SIDE] * low_ok
        second_ref[:, SIDE : SIDE + COLS, :] = act[:, SIDE : SIDE + COLS]
        second_ref[:, SIDE + COLS :, :] = act[:, SIDE + COLS :] * high_ok
        for tap in range(3):
            second_cols_ref[pl.ds(at, GROUP_B), :, tap * CH : (tap + 1) * CH] = second_ref[
                :, 4 + 4 * tap : 4 + 4 * tap + COLS, :
            ].astype(BF)
        return carry

    lax.fori_loop(0, FIRST_TALL // GROUP_B, convolve_first, 0, unroll=UNROLL_B)

    @pl.when(jnp.logical_not(above))
    def _():
        second_cols_ref[0:SECOND_DILATION] = jnp.zeros((SECOND_DILATION, COLS, 3 * CH), BF)

    @pl.when(jnp.logical_not(below))
    def _():
        second_cols_ref[SECOND_DILATION + ROWS :] = jnp.zeros(
            (SECOND_DILATION, COLS, 3 * CH), BF
        )

    def out_copy(k):
        return pltpu.make_async_copy(
            out_ref.at[16 * k : 16 * k + 16], out_hbm.at[16 * k : 16 * k + 16], out_sems.at[k]
        )

    for k in range(4):
        for part in range(16 // GROUP_C):
            at = 16 * k + part * GROUP_C
            out_ref[at : at + GROUP_C] = (
                paired(second_cols_ref, at, SECOND_DILATION, GROUP_C, COLS, 1)
                + first_ref[at + 4 : at + 4 + GROUP_C]
                + bias_ref[1:2].reshape(1, 1, CH)
            ).astype(BF)
        out_copy(k).start()
    for k in range(4):
        out_copy(k).wait()


def convolutions(place, sym, top, bottom, low, high, gain, shift, bias, weight):
    vmem = pl.BlockSpec(memory_space=pltpu.VMEM)
    anywhere = pl.BlockSpec(memory_space=pl.ANY)
    return pl.pallas_call(
        convolution_kernel,
        out_shape=jax.ShapeDtypeStruct((ROWS, COLS, CH), BF),
        in_specs=[pl.BlockSpec(memory_space=pltpu.SMEM)] + [anywhere] * 3 + [vmem] * 5 + [anywhere],
        out_specs=anywhere,
        scratch_shapes=[
            pltpu.VMEM((TALL, COLS, CH), BF),
            pltpu.VMEM((GROUP_A, WIDE + 16, CH), F32),
            pltpu.VMEM((TALL, WIDE, 3 * CH), BF),
            pltpu.VMEM((FIRST_TALL, COLS, CH), F32),
            pltpu.VMEM((GROUP_B, WIDE, CH), F32),
            pltpu.VMEM((FIRST_TALL, COLS, 3 * CH), BF),
            pltpu.VMEM((2, 12 * CH, 2 * CH), BF),
            pltpu.VMEM((ROWS, COLS, CH), BF),
            pltpu.SemaphoreType.DMA((7,)),
            pltpu.SemaphoreType.DMA((4,)),
        ],
        compiler_params=pltpu.CompilerParams(vmem_limit_bytes=CONV_VMEM * MIB),
        name="convolutions",
    )(place, sym, top, bottom, low, high, gain, shift, bias, weight)


def paired_weight(weight):
    taps = weight.reshape(3, 3 * CH, CH)
    near = jnp.concatenate([taps, jnp.zeros_like(taps[:1])], axis=0)
    far = jnp.concatenate([jnp.zeros_like(taps[:1]), taps], axis=0)
    return jnp.concatenate([near, far], axis=2).reshape(12 * CH, 2 * CH)


def neighbours(low_strip, high_strip, axis):
    count = lax.axis_size(axis)
    forward = [(i, i + 1) for i in range(count - 1)]
    backward = [(i + 1, i) for i in range(count - 1)]
    return lax.ppermute(high_strip, axis, forward), lax.ppermute(low_strip, axis, backward)


def local(
    pair, norm_gain, norm_shift, proj_weight, proj_bias, mid_gain, mid_shift, out_weight, out_bias,
    conv_gain, conv_shift, convolution_weight, convolution_bias,
):
    gain, shift = norm_gain[None], norm_shift[None]
    sent = factors(pair, gain, shift, proj_weight, proj_bias.reshape(1, 4 * HID + CH))
    received = lax.all_to_all(
        sent.reshape(128, 2, ROWS, COLS), ("row", "col"), split_axis=0, concat_axis=0, tiled=True
    ).reshape(NR, NC, 2, ROWS, COLS)
    other = lax.ppermute(plane(received), "row", [(i, i ^ 1) for i in range(NR)])
    back = product(received, other)
    returned = lax.all_to_all(
        back.reshape(128, 2, ROWS, COLS), ("row", "col"), split_axis=0, concat_axis=0, tiled=True
    )
    gate, gate_bias = proj_weight[:, 4 * HID :], proj_bias[None, 4 * HID :]
    sym = update(
        pair, gates(pair, gain, shift, gate, gate_bias), returned, gain, shift, gate, gate_bias,
        *output_weight(out_weight, out_bias, mid_gain, mid_shift),
    )
    top, bottom = neighbours(sym[:HALO], sym[ROWS - HALO :], "row")
    edge = lambda low, high: jnp.concatenate(
        [top[:, low:high], sym[:, low:high], bottom[:, low:high]], axis=0
    )
    low, high = neighbours(edge(0, SIDE), edge(COLS - SIDE, COLS), "col")
    place = jnp.stack([lax.axis_index("row") * ROWS, lax.axis_index("col") * COLS]).astype(jnp.int32)
    return convolutions(
        place, sym, top, bottom, low, high, conv_gain, conv_shift, convolution_bias,
        jnp.stack([paired_weight(convolution_weight[0]), paired_weight(convolution_weight[1])]),
    )


def solution(mesh):
    return jax.shard_map(
        local,
        mesh=mesh,
        in_specs=(P("row", "col", None),) + (P(),) * 12,
        out_specs=P("row", "col", None),
        check_vma=False,
    )
```

```python
import jax
import jax.numpy as jnp
from jax import lax
from jax.experimental import pallas as pl
from jax.experimental.pallas import tpu as pltpu
from jax.sharding import PartitionSpec as P

FIRST_DILATION = 2
SECOND_DILATION = 4
HALO = FIRST_DILATION + SECOND_DILATION
EPS = 1e-05
BF = jnp.bfloat16
F32 = jnp.float32
MIB = 1 << 20
ROWS, COLS, CH, HID = 64, 128, 128, 64
NR, NC = 16, 8


def sigmoid(x):
    return 0.5 * jnp.tanh(0.5 * x) + 0.5


def normalize(values, gain, shift):
    mean = jnp.mean(values, axis=-1, keepdims=True)
    centred = values - mean
    spread = jnp.mean(centred * centred, axis=-1, keepdims=True)
    return centred * lax.rsqrt(spread + EPS) * gain + shift


NT = (((1,), (1,)), ((), ()))
TN = (((0,), (0,)), ((), ()))

STEP = 16


def factor_kernel(
    pair_ref, gain_ref, shift_ref, weight_ref, bias_ref, out_ref, lay_ref, stage_ref, cells_ref,
    cell_sems, stage_sems,
):
    step = pl.program_id(0)

    def cell_copy(k):
        return pltpu.make_async_copy(
            cells_ref.at[k], out_ref.at[pl.ds(2 * k, 2), :, :, :, 1], cell_sems.at[k]
        )

    def stage_copy(k):
        start = pl.multiple_of(k * STEP, STEP)
        return pltpu.make_async_copy(
            stage_ref.at[k], out_ref.at[:, :, :, :, 0, pl.ds(start, STEP), :], stage_sems.at[k]
        )

    for row in range(STEP):
        for q in range(2):
            for half in range(2):
                start = half * 64 + q * 32
                cells_ref[
                    step, row // 8, (row // 4) % 2, row % 4, q, half * 32 : half * 32 + 32, :
                ] = pair_ref[row, start : start + 32, :]
    cell_copy(step).start()
    cells = pair_ref[...].astype(F32).reshape(STEP * COLS, CH)
    normed = normalize(cells, gain_ref[...], shift_ref[...]).astype(BF)
    bias = jnp.transpose(jnp.broadcast_to(bias_ref[:, : 4 * HID], (COLS, 4 * HID)))
    projected = lax.dot_general(
        weight_ref[:, : 4 * HID], normed, (((0,), (1,)), ((), ())), preferred_element_type=F32
    )
    for side in range(2):
        base = 2 * HID * side
        for row in range(STEP):
            part = slice(row * COLS, (row + 1) * COLS)
            gate = projected[base : base + HID, part] + bias[base : base + HID]
            value = projected[base + HID : base + 2 * HID, part] + bias[base + HID : base + 2 * HID]
            lay_ref[pl.ds(row, HID, stride=STEP), :] = sigmoid(gate) * value
        stage_ref[step, :, side] = lay_ref[...].astype(BF).reshape(8, 4, 2, STEP, COLS)
    stage_copy(step).start()

    @pl.when(step == ROWS // STEP - 1)
    def _():
        for k in range(ROWS // STEP):
            cell_copy(k).wait()
            stage_copy(k).wait()


FACTORS_VMEM = 60


def factors(pair, gain, shift, weight, bias):
    whole = lambda *shape: pl.BlockSpec(shape, lambda s: (0,) * len(shape))
    steps = ROWS // STEP
    return pl.pallas_call(
        factor_kernel,
        grid=(steps,),
        out_shape=jax.ShapeDtypeStruct((8, 2, 4, 2, 2, ROWS, COLS), BF),
        in_specs=[
            pl.BlockSpec((STEP, COLS, CH), lambda s: (s, 0, 0)),
            whole(1, CH),
            whole(1, CH),
            whole(CH, 4 * HID + CH),
            whole(1, 4 * HID + CH),
        ],
        out_specs=pl.BlockSpec(memory_space=pl.ANY),
        scratch_shapes=[
            pltpu.VMEM((HID * STEP, COLS), F32),
            pltpu.VMEM((steps, 8, 2, 4, 2, STEP, COLS), BF),
            pltpu.VMEM((steps, 2, 2, 4, 2, ROWS, COLS), BF),
            pltpu.SemaphoreType.DMA((steps,)),
            pltpu.SemaphoreType.DMA((steps,)),
        ],
        compiler_params=pltpu.CompilerParams(vmem_limit_bytes=FACTORS_VMEM * MIB),
        name="factors",
    )(pair, gain, shift, weight, bias)


def plane_kernel(received_ref, out_ref, hold_ref, in_sems, out_sems):
    parts = [slice(k * NR // 4, (k + 1) * NR // 4) for k in range(4)]
    inward = [
        pltpu.make_async_copy(received_ref.at[part, :, 0], hold_ref.at[part], in_sems.at[k])
        for k, part in enumerate(parts)
    ]
    outward = [
        pltpu.make_async_copy(hold_ref.at[part], out_ref.at[part], out_sems.at[k])
        for k, part in enumerate(parts)
    ]
    for copy in inward:
        copy.start()
    for k in range(4):
        inward[k].wait()
        outward[k].start()
    for copy in outward:
        copy.wait()


def plane(received):
    return pl.pallas_call(
        plane_kernel,
        out_shape=jax.ShapeDtypeStruct((NR, NC, ROWS, COLS), BF),
        in_specs=[pl.BlockSpec(memory_space=pl.ANY)],
        out_specs=pl.BlockSpec(memory_space=pl.ANY),
        scratch_shapes=[
            pltpu.VMEM((NR, NC, ROWS, COLS), BF),
            pltpu.SemaphoreType.DMA((4,)),
            pltpu.SemaphoreType.DMA((4,)),
        ],
        compiler_params=pltpu.CompilerParams(vmem_limit_bytes=PLANE_VMEM * MIB),
        name="plane",
    )(received)


PLANE_VMEM = 60
PRODUCT_VMEM = 60


def product_kernel(
    received_ref, other_ref, out_ref, lhs_ref, rhs_ref, result_ref, cells_ref,
    lhs_sems, rhs_sems, cell_sems, out_sems, cell_out_sem,
):
    half = NR // 2

    def columns(col):
        return slice(col * COLS, (col + 1) * COLS)

    lhs = [
        pltpu.make_async_copy(
            received_ref.at[:, side, col, 0],
            lhs_ref.at[side, :, :, columns(col)],
            lhs_sems.at[side, col],
        )
        for side in range(2)
        for col in range(NC)
    ]
    rhs = [
        pltpu.make_async_copy(
            other_ref.at[:, col], rhs_ref.at[:, :, columns(col)], rhs_sems.at[col]
        )
        for col in range(NC)
    ]
    cells = [
        pltpu.make_async_copy(
            received_ref.at[col, e, :, 1, side * 32 : side * 32 + 32, :],
            cells_ref.at[:, side, col, e * 32 : e * 32 + 32, :],
            cell_sems.at[col, e, side],
        )
        for col in range(NC)
        for e in range(2)
        for side in range(2)
    ]
    for copy in rhs + lhs + cells:
        copy.start()
    for copy in rhs:
        copy.wait()
    outs = []
    for side in range(2):
        for copy in lhs[side * NC : side * NC + NC]:
            copy.wait()
        own = lhs_ref[side].reshape(half * ROWS, NC * COLS)
        for block in range(4):
            result = lax.dot_general(
                own,
                rhs_ref[4 * block : 4 * block + 4].reshape(256, NC * COLS),
                NT,
                preferred_element_type=F32,
            ).astype(BF)
            for col in range(2):
                result_ref[side, :, block * 2 + col] = result[:, columns(col)].reshape(
                    half, ROWS, COLS
                )
        copy = pltpu.make_async_copy(
            result_ref.at[side], out_ref.at[:, side, :, 0], out_sems.at[side]
        )
        copy.start()
        outs.append(copy)
        if side == 0:
            for moved in cells:
                moved.wait()
            copy = pltpu.make_async_copy(cells_ref, out_ref.at[:, :, :, 1], cell_out_sem)
            copy.start()
            outs.append(copy)
    for copy in outs:
        copy.wait()


def product(received, other):
    anywhere = pl.BlockSpec(memory_space=pl.ANY)
    half = NR // 2
    return pl.pallas_call(
        product_kernel,
        out_shape=jax.ShapeDtypeStruct((half, 2, NC, 2, ROWS, COLS), BF),
        in_specs=[anywhere, anywhere],
        out_specs=anywhere,
        scratch_shapes=[
            pltpu.VMEM((2, half, ROWS, NC * COLS), BF),
            pltpu.VMEM((NR, ROWS, NC * COLS), BF),
            pltpu.VMEM((2, half, NC, ROWS, COLS), BF),
            pltpu.VMEM((half, 2, NC, ROWS, COLS), BF),
            pltpu.SemaphoreType.DMA((2, NC)),
            pltpu.SemaphoreType.DMA((NC,)),
            pltpu.SemaphoreType.DMA((NC, 2, 2)),
            pltpu.SemaphoreType.DMA((2,)),
            pltpu.SemaphoreType.DMA(()),
        ],
        compiler_params=pltpu.CompilerParams(vmem_limit_bytes=PRODUCT_VMEM * MIB),
        name="product",
    )(received.reshape(half, 2, NC, 2, ROWS, COLS), other)


def gate_kernel(pair_ref, gain_ref, shift_ref, weight_ref, bias_ref, out_ref):
    cells = pair_ref[...].astype(F32).reshape(STEP * COLS, CH)
    normed = normalize(cells, gain_ref[...], shift_ref[...]).astype(BF)
    gate = jnp.dot(normed, weight_ref[...], preferred_element_type=F32) + bias_ref[...]
    out_ref[...] = sigmoid(gate).reshape(STEP, COLS, CH)


def gates(pair, gain, shift, weight, bias):
    whole = lambda *shape: pl.BlockSpec(shape, lambda s: (0,) * len(shape))
    block = pl.BlockSpec((STEP, COLS, CH), lambda s: (s, 0, 0))
    return pl.pallas_call(
        gate_kernel,
        grid=(ROWS // STEP,),
        out_shape=jax.ShapeDtypeStruct((ROWS, COLS, CH), F32),
        in_specs=[block, whole(1, CH), whole(1, CH), whole(CH, CH), whole(1, CH)],
        out_specs=block,
        compiler_params=pltpu.CompilerParams(vmem_limit_bytes=24 * MIB),
        cost_estimate=pl.CostEstimate(
            flops=2 * ROWS * COLS * CH * CH, bytes_accessed=6 * ROWS * COLS * CH, transcendentals=ROWS * COLS * CH
        ),
        name="gates",
    )(pair, gain, shift, weight, bias)


USTEP = 16
UNROLL_U = 1
UGROUP = 8
PITCH = 72


def update_kernel(
    pair_ref, own_gate_ref, tri_ref, mirror_ref, gain_ref, shift_ref, gate_ref, gate_bias_ref,
    out_weight_ref, out_bias_ref, sym_ref, cells_ref, lay_ref,
):
    step = pl.program_id(0)

    @pl.when(step == 0)
    def _():
        for d in range(128):
            for e in range(2):
                at = (e * 64 + d // 2) * PITCH + (d % 2) * 32
                cells_ref[at : at + 32, :] = mirror_ref[d, 0, e * 32 : e * 32 + 32, :].astype(F32)

    tri = tri_ref[:, :, :, 0].astype(F32)
    mean = jnp.mean(tri, axis=(0, 2), keepdims=True)
    centred = tri - mean
    spread = jnp.mean(centred * centred, axis=(0, 2), keepdims=True)
    lay_ref[...] = (centred * lax.rsqrt(spread + EPS)).reshape(2 * HID * USTEP, COLS)

    def body(part, carry):
        first = part * UGROUP
        change, cells = [], []
        for k in range(UGROUP):
            mid = lay_ref[pl.ds(first + k, 2 * HID, stride=USTEP), :].astype(BF)
            change.append(
                lax.dot_general(mid, out_weight_ref[...], TN, preferred_element_type=F32)
            )
            cells.append(
                cells_ref[pl.ds(step * USTEP + first + k, COLS, stride=PITCH), :]
            )
        change = jnp.concatenate(change, axis=0) + out_bias_ref[...]
        cells = jnp.concatenate(cells, axis=0)
        size = UGROUP * COLS
        own = (
            pair_ref[pl.ds(first, UGROUP)].astype(F32).reshape(size, CH)
            + own_gate_ref[pl.ds(first, UGROUP)].reshape(size, CH) * change[:, :CH]
        )
        normed = normalize(cells, gain_ref[...], shift_ref[...]).astype(BF)
        gate = sigmoid(
            jnp.dot(normed, gate_ref[...], preferred_element_type=F32) + gate_bias_ref[...]
        )
        mirrored = cells + gate * change[:, CH:]
        total = own.astype(BF).astype(F32) + mirrored.astype(BF).astype(F32)
        sym_ref[pl.ds(first, UGROUP)] = (total * 0.5).astype(BF).reshape(UGROUP, COLS, CH)
        return carry

    lax.fori_loop(0, USTEP // UGROUP, body, 0, unroll=UNROLL_U)


def update(pair, own_gate, received, gain, shift, gate, gate_bias, out_weight, out_bias):
    whole = lambda *shape: pl.BlockSpec(shape, lambda s: (0,) * len(shape))
    tri = received.reshape(8, 2, 8, 2, ROWS, COLS)
    cells = received.reshape(128, 2, ROWS, COLS)
    block = pl.BlockSpec((USTEP, COLS, CH), lambda s: (s, 0, 0))
    return pl.pallas_call(
        update_kernel,
        grid=(ROWS // USTEP,),
        out_shape=jax.ShapeDtypeStruct((ROWS, COLS, CH), BF),
        in_specs=[
            block,
            block,
            pl.BlockSpec((8, 2, 8, 1, USTEP, COLS), lambda s: (0, 0, 0, 0, s, 0)),
            pl.BlockSpec((128, 1, ROWS, COLS), lambda s: (0, 1, 0, 0)),
            whole(1, CH),
            whole(1, CH),
            whole(CH, CH),
            whole(1, CH),
            whole(2 * HID, 2 * CH),
            whole(1, 2 * CH),
        ],
        out_specs=block,
        scratch_shapes=[
            pltpu.VMEM((COLS * PITCH, CH), F32),
            pltpu.VMEM((2 * HID * USTEP, COLS), F32),
        ],
        compiler_params=pltpu.CompilerParams(vmem_limit_bytes=48 * MIB),
        name="update",
    )(pair, own_gate, tri, cells, gain, shift, gate, gate_bias, out_weight, out_bias)


def output_weight(weight, bias, gain, shift):
    scaled = (gain[:, None] * weight.astype(F32)).astype(BF).reshape(8, 1, 8, CH)
    nothing = jnp.zeros_like(scaled)
    own = jnp.concatenate([scaled, nothing], axis=1)
    mirrored = jnp.concatenate([nothing, scaled], axis=1)
    full = jnp.concatenate([own, mirrored], axis=3).reshape(2 * HID, 2 * CH)
    offset = bias + jnp.sum(shift[:, None] * weight.astype(F32), axis=0)
    return full, jnp.concatenate([offset, offset])[None]


def activation_kernel(sym_ref, gain_ref, shift_ref, out_ref):
    cells = sym_ref[...].astype(F32).reshape(STEP * COLS, CH)
    act = jnp.maximum(normalize(cells, gain_ref[0:1], shift_ref[0:1]), 0.0)
    out_ref[...] = act.astype(BF).reshape(STEP, COLS, CH)


def activations(sym, gain, shift):
    whole = lambda *shape: pl.BlockSpec(shape, lambda s: (0,) * len(shape))
    block = pl.BlockSpec((STEP, COLS, CH), lambda s: (s, 0, 0))
    return pl.pallas_call(
        activation_kernel,
        grid=(ROWS // STEP,),
        out_shape=jax.ShapeDtypeStruct((ROWS, COLS, CH), BF),
        in_specs=[block, whole(2, CH), whole(2, CH)],
        out_specs=block,
        compiler_params=pltpu.CompilerParams(vmem_limit_bytes=60 * MIB),
        cost_estimate=pl.CostEstimate(
            flops=16 * ROWS * COLS * CH, bytes_accessed=4 * ROWS * COLS * CH, transcendentals=ROWS * COLS
        ),
        name="activations",
    )(sym, gain, shift)


TALL = ROWS + 2 * HALO
SIDE = 8
WIDE = COLS + 4 * SIDE
FIRST_TALL = ROWS + 2 * SECOND_DILATION
FIRST_WIDE = COLS + 2 * SIDE
GROUP_B, GROUP_C = 4, 8
INNER_B, SLOTS_C = 9, 2
CONV_VMEM = 62


def convolution_kernel(
    place_ref, sym_ref, act_ref, top_ref, bottom_ref, low_ref, high_ref, gain_ref, shift_ref,
    bias_ref, weight_hbm, out_hbm, tall_ref, wide_ref, first_ref, second_ref, shifted_ref,
    late_ref, weight_ref, out_ref, sems, out_sems,
):
    top_copy = pltpu.make_async_copy(top_ref, tall_ref.at[0:HALO], sems.at[0])
    bottom_copy = pltpu.make_async_copy(bottom_ref, tall_ref.at[HALO + ROWS : TALL], sems.at[1])
    act_copy = pltpu.make_async_copy(
        act_ref, wide_ref.at[HALO : HALO + ROWS, 16 : 16 + COLS], sems.at[2]
    )
    weight_copy = pltpu.make_async_copy(weight_hbm, weight_ref, sems.at[3])
    sym_copy = pltpu.make_async_copy(sym_ref, tall_ref.at[HALO : HALO + ROWS], sems.at[4])
    for copy in (top_copy, bottom_copy, act_copy, weight_copy, sym_copy):
        copy.start()
    above = place_ref[0] > 0
    below = place_ref[0] < (NR - 1) * ROWS
    low_ok = (place_ref[1] > 0).astype(F32)
    high_ok = (place_ref[1] < (NC - 1) * COLS).astype(F32)

    def activate(cells, which):
        return jnp.maximum(
            normalize(
                cells,
                gain_ref[which : which + 1].reshape(1, 1, CH),
                shift_ref[which : which + 1].reshape(1, 1, CH),
            ),
            0.0,
        )

    nothing = jnp.zeros((TALL, SIDE, CH), F32)
    low = activate(low_ref[...].astype(F32), 0) * low_ok
    wide_ref[:, 0:16, :] = jnp.concatenate([nothing, low], axis=1).astype(BF)
    high = activate(high_ref[...].astype(F32), 0) * high_ok
    wide_ref[:, 16 + COLS :, :] = jnp.concatenate([high, nothing], axis=1).astype(BF)
    top_copy.wait()
    bottom_copy.wait()
    wide_ref[0:HALO, 16 : 16 + COLS, :] = activate(tall_ref[0:HALO].astype(F32), 0).astype(BF)
    wide_ref[HALO + ROWS :, 16 : 16 + COLS, :] = activate(
        tall_ref[HALO + ROWS :].astype(F32), 0
    ).astype(BF)

    @pl.when(jnp.logical_not(above))
    def _():
        wide_ref[0:HALO] = jnp.zeros((HALO, WIDE, CH), BF)

    @pl.when(jnp.logical_not(below))
    def _():
        wide_ref[HALO + ROWS :] = jnp.zeros((HALO, WIDE, CH), BF)

    def paired(source_ref, at, spacing, group, width, which):
        sets = group // (2 * spacing)
        lhs = jnp.concatenate(
            [
                jnp.concatenate(
                    [
                        source_ref[pl.ds(at + 2 * spacing * k + spacing * slot, spacing)]
                        for k in range(sets)
                    ],
                    axis=0,
                ).reshape(group // 2 * width, CH)
                for slot in range(4)
            ],
            axis=1,
        )
        total = jnp.dot(lhs, weight_ref[which], preferred_element_type=F32)
        taps = []
        for tap in range(3):
            near = total[:, tap * CH : (tap + 1) * CH].reshape(sets, spacing, width, CH)
            far = total[:, (3 + tap) * CH : (4 + tap) * CH].reshape(sets, spacing, width, CH)
            taps.append(jnp.concatenate([near, far], axis=1).reshape(group, width, CH))
        return taps

    def first_rows(at, slot):
        before, centre, after = paired(wide_ref, at, FIRST_DILATION, GROUP_B, WIDE, 0)
        shifted_ref[slot, 0] = before
        shifted_ref[slot, 1] = after
        residual = jnp.concatenate(
            [
                low_ref[pl.ds(at + 2, GROUP_B)].astype(F32),
                tall_ref[pl.ds(at + 2, GROUP_B)].astype(F32),
                high_ref[pl.ds(at + 2, GROUP_B)].astype(F32),
            ],
            axis=1,
        )
        first = (
            centre[:, 8 : 8 + FIRST_WIDE]
            + shifted_ref[slot, 0, :, 6 : 6 + FIRST_WIDE, :]
            + shifted_ref[slot, 1, :, 10 : 10 + FIRST_WIDE, :]
            + residual
            + bias_ref[0:1].reshape(1, 1, CH)
        )
        first_ref[pl.ds(at, GROUP_B)] = first[:, SIDE : SIDE + COLS]
        act = activate(first, 1)
        second_ref[pl.ds(at, GROUP_B)] = jnp.concatenate(
            [
                act[:, :SIDE] * low_ok,
                act[:, SIDE : SIDE + COLS],
                act[:, SIDE + COLS :] * high_ok,
            ],
            axis=1,
        ).astype(BF)

    def convolve_first(step, carry):
        for k in range(INNER_B):
            first_rows(step * (GROUP_B * INNER_B) + k * GROUP_B, k)
        return carry

    act_copy.wait()
    weight_copy.wait()
    sym_copy.wait()
    lax.fori_loop(0, FIRST_TALL // (GROUP_B * INNER_B), convolve_first, 0)

    @pl.when(jnp.logical_not(above))
    def _():
        second_ref[0:SECOND_DILATION] = jnp.zeros((SECOND_DILATION, FIRST_WIDE, CH), BF)

    @pl.when(jnp.logical_not(below))
    def _():
        second_ref[SECOND_DILATION + ROWS :] = jnp.zeros((SECOND_DILATION, FIRST_WIDE, CH), BF)

    def out_copy(k):
        return pltpu.make_async_copy(
            out_ref.at[16 * k : 16 * k + 16], out_hbm.at[16 * k : 16 * k + 16], out_sems.at[k]
        )

    for k in range(4):
        for part in range(16 // GROUP_C):
            at = 16 * k + part * GROUP_C
            slot = at // GROUP_C % SLOTS_C
            before, centre, after = paired(
                second_ref, at, SECOND_DILATION, GROUP_C, FIRST_WIDE, 1
            )
            late_ref[slot, 0] = before
            late_ref[slot, 1] = after
            out_ref[at : at + GROUP_C] = (
                centre[:, SIDE : SIDE + COLS]
                + late_ref[slot, 0, :, 4 : 4 + COLS, :]
                + late_ref[slot, 1, :, 12 : 12 + COLS, :]
                + first_ref[at + 4 : at + 4 + GROUP_C]
                + bias_ref[1:2].reshape(1, 1, CH)
            ).astype(BF)
        out_copy(k).start()
    for k in range(4):
        out_copy(k).wait()


def convolutions(place, sym, act, top, bottom, low, high, gain, shift, bias, weight):
    vmem = pl.BlockSpec(memory_space=pltpu.VMEM)
    anywhere = pl.BlockSpec(memory_space=pl.ANY)
    return pl.pallas_call(
        convolution_kernel,
        out_shape=jax.ShapeDtypeStruct((ROWS, COLS, CH), BF),
        in_specs=[pl.BlockSpec(memory_space=pltpu.SMEM)]
        + [anywhere] * 4
        + [vmem] * 5
        + [anywhere],
        out_specs=anywhere,
        scratch_shapes=[
            pltpu.VMEM((TALL, COLS, CH), BF),
            pltpu.VMEM((TALL, WIDE, CH), BF),
            pltpu.VMEM((FIRST_TALL, COLS, CH), F32),
            pltpu.VMEM((FIRST_TALL, FIRST_WIDE, CH), BF),
            pltpu.VMEM((INNER_B, 2, GROUP_B, WIDE, CH), F32),
            pltpu.VMEM((SLOTS_C, 2, GROUP_C, FIRST_WIDE, CH), F32),
            pltpu.VMEM((2, 4 * CH, 6 * CH), BF),
            pltpu.VMEM((ROWS, COLS, CH), BF),
            pltpu.SemaphoreType.DMA((5,)),
            pltpu.SemaphoreType.DMA((4,)),
        ],
        compiler_params=pltpu.CompilerParams(vmem_limit_bytes=CONV_VMEM * MIB),
        name="convolutions",
    )(place, sym, act, top, bottom, low, high, gain, shift, bias, weight)


def paired_weight(weight):
    taps = jnp.transpose(weight.reshape(3, 3, CH, CH), (0, 2, 1, 3)).reshape(3, CH, 3 * CH)
    near = jnp.concatenate([taps, jnp.zeros_like(taps[:1])], axis=0)
    far = jnp.concatenate([jnp.zeros_like(taps[:1]), taps], axis=0)
    return jnp.concatenate([near, far], axis=2).reshape(4 * CH, 6 * CH)


def neighbours(low_strip, high_strip, axis):
    count = lax.axis_size(axis)
    forward = [(i, i + 1) for i in range(count - 1)]
    backward = [(i + 1, i) for i in range(count - 1)]
    return lax.ppermute(high_strip, axis, forward), lax.ppermute(low_strip, axis, backward)


def local(
    pair, norm_gain, norm_shift, proj_weight, proj_bias, mid_gain, mid_shift, out_weight, out_bias,
    conv_gain, conv_shift, convolution_weight, convolution_bias,
):
    gain, shift = norm_gain[None], norm_shift[None]
    sent = factors(pair, gain, shift, proj_weight, proj_bias.reshape(1, 4 * HID + CH))
    received = lax.all_to_all(
        sent.reshape(128, 2, ROWS, COLS), ("row", "col"), split_axis=0, concat_axis=0, tiled=True
    ).reshape(NR, NC, 2, ROWS, COLS)
    other = lax.ppermute(plane(received), "row", [(i, i ^ 1) for i in range(NR)])
    back = product(received, other)
    returned = lax.all_to_all(
        back.reshape(128, 2, ROWS, COLS), ("row", "col"), split_axis=0, concat_axis=0, tiled=True
    )
    gate, gate_bias = proj_weight[:, 4 * HID :], proj_bias[None, 4 * HID :]
    sym = update(
        pair, gates(pair, gain, shift, gate, gate_bias), returned, gain, shift, gate, gate_bias,
        *output_weight(out_weight, out_bias, mid_gain, mid_shift),
    )
    top, bottom = neighbours(sym[:HALO], sym[ROWS - HALO :], "row")
    edge = lambda low, high: jnp.concatenate(
        [top[:, low:high], sym[:, low:high], bottom[:, low:high]], axis=0
    )
    low, high = neighbours(edge(0, SIDE), edge(COLS - SIDE, COLS), "col")
    place = jnp.stack([lax.axis_index("row") * ROWS, lax.axis_index("col") * COLS]).astype(jnp.int32)
    return convolutions(
        place, sym, activations(sym, conv_gain, conv_shift), top, bottom, low, high, conv_gain, conv_shift, convolution_bias,
        jnp.stack([paired_weight(convolution_weight[0]), paired_weight(convolution_weight[1])]),
    )


def solution(mesh):
    return jax.shard_map(
        local,
        mesh=mesh,
        in_specs=(P("row", "col", None),) + (P(),) * 12,
        out_specs=P("row", "col", None),
        check_vma=False,
    )
```

```python
import jax
import jax.numpy as jnp
from jax import lax
from jax.experimental import pallas as pl
from jax.experimental.pallas import tpu as pltpu
from jax.sharding import PartitionSpec as P

FIRST_DILATION = 2
SECOND_DILATION = 4
HALO = FIRST_DILATION + SECOND_DILATION
EPS = 1e-05
BF = jnp.bfloat16
F32 = jnp.float32
MIB = 1 << 20
ROWS, COLS, CH, HID = 64, 128, 128, 64
NR, NC = 16, 8


def sigmoid(x):
    return 0.5 * jnp.tanh(0.5 * x) + 0.5


def normalize(values, gain, shift):
    mean = jnp.mean(values, axis=-1, keepdims=True)
    centred = values - mean
    spread = jnp.mean(centred * centred, axis=-1, keepdims=True)
    return centred * lax.rsqrt(spread + EPS) * gain + shift


NT = (((1,), (1,)), ((), ()))
TN = (((0,), (0,)), ((), ()))

STEP = 16


def factor_kernel(
    pair_ref, gain_ref, shift_ref, weight_ref, bias_ref, out_ref, lay_ref, stage_ref, cells_ref,
    cell_sems, stage_sems,
):
    step = pl.program_id(0)

    def cell_copy(k):
        return pltpu.make_async_copy(
            cells_ref.at[k], out_ref.at[pl.ds(2 * k, 2), :, :, :, 1], cell_sems.at[k]
        )

    def stage_copy(k):
        start = pl.multiple_of(k * STEP, STEP)
        return pltpu.make_async_copy(
            stage_ref.at[k], out_ref.at[:, :, :, :, 0, pl.ds(start, STEP), :], stage_sems.at[k]
        )

    for row in range(STEP):
        for q in range(2):
            for half in range(2):
                start = half * 64 + q * 32
                cells_ref[
                    step, row // 8, (row // 4) % 2, row % 4, q, half * 32 : half * 32 + 32, :
                ] = pair_ref[row, start : start + 32, :]
    cell_copy(step).start()
    cells = pair_ref[...].astype(F32).reshape(STEP * COLS, CH)
    normed = normalize(cells, gain_ref[...], shift_ref[...]).astype(BF)
    bias = jnp.transpose(jnp.broadcast_to(bias_ref[...][None], (COLS, 4 * HID + CH))[:, : 4 * HID])
    projected = lax.dot_general(
        weight_ref[:, : 4 * HID], normed, (((0,), (1,)), ((), ())), preferred_element_type=F32
    )
    for side in range(2):
        base = 2 * HID * side
        for row in range(STEP):
            part = slice(row * COLS, (row + 1) * COLS)
            gate = projected[base : base + HID, part] + bias[base : base + HID]
            value = projected[base + HID : base + 2 * HID, part] + bias[base + HID : base + 2 * HID]
            lay_ref[pl.ds(row, HID, stride=STEP), :] = sigmoid(gate) * value
        stage_ref[step, :, side] = lay_ref[...].astype(BF).reshape(8, 4, 2, STEP, COLS)
    stage_copy(step).start()

    @pl.when(step == ROWS // STEP - 1)
    def _():
        for k in range(ROWS // STEP):
            cell_copy(k).wait()
            stage_copy(k).wait()


FACTORS_VMEM = 60


def factors(pair, gain, shift, weight, bias):
    whole = lambda *shape: pl.BlockSpec(shape, lambda s: (0,) * len(shape))
    steps = ROWS // STEP
    return pl.pallas_call(
        factor_kernel,
        grid=(steps,),
        out_shape=jax.ShapeDtypeStruct((8, 2, 4, 2, 2, ROWS, COLS), BF),
        in_specs=[
            pl.BlockSpec((STEP, COLS, CH), lambda s: (s, 0, 0)),
            whole(1, CH),
            whole(1, CH),
            whole(CH, 4 * HID + CH),
            whole(4 * HID + CH),
        ],
        out_specs=pl.BlockSpec(memory_space=pl.ANY),
        scratch_shapes=[
            pltpu.VMEM((HID * STEP, COLS), F32),
            pltpu.VMEM((steps, 8, 2, 4, 2, STEP, COLS), BF),
            pltpu.VMEM((steps, 2, 2, 4, 2, ROWS, COLS), BF),
            pltpu.SemaphoreType.DMA((steps,)),
            pltpu.SemaphoreType.DMA((steps,)),
        ],
        compiler_params=pltpu.CompilerParams(vmem_limit_bytes=FACTORS_VMEM * MIB),
        name="factors",
    )(pair, gain, shift, weight, bias)


def plane_kernel(received_ref, out_ref, hold_ref, in_sems, out_sems):
    parts = [slice(k * NR // 4, (k + 1) * NR // 4) for k in range(4)]
    inward = [
        pltpu.make_async_copy(received_ref.at[part, :, 0], hold_ref.at[part], in_sems.at[k])
        for k, part in enumerate(parts)
    ]
    outward = [
        pltpu.make_async_copy(hold_ref.at[part], out_ref.at[part], out_sems.at[k])
        for k, part in enumerate(parts)
    ]
    for copy in inward:
        copy.start()
    for k in range(4):
        inward[k].wait()
        outward[k].start()
    for copy in outward:
        copy.wait()


def plane(received):
    return pl.pallas_call(
        plane_kernel,
        out_shape=jax.ShapeDtypeStruct((NR, NC, ROWS, COLS), BF),
        in_specs=[pl.BlockSpec(memory_space=pl.ANY)],
        out_specs=pl.BlockSpec(memory_space=pl.ANY),
        scratch_shapes=[
            pltpu.VMEM((NR, NC, ROWS, COLS), BF),
            pltpu.SemaphoreType.DMA((4,)),
            pltpu.SemaphoreType.DMA((4,)),
        ],
        compiler_params=pltpu.CompilerParams(vmem_limit_bytes=PLANE_VMEM * MIB),
        name="plane",
    )(received)


PLANE_VMEM = 16
PRODUCT_VMEM = 60


def product_kernel(
    received_ref, other_ref, out_ref, lhs_ref, rhs_ref, result_ref, cells_ref,
    lhs_sems, rhs_sems, cell_sems, out_sems, cell_out_sem,
):
    half = NR // 2

    def columns(col):
        return slice(col * COLS, (col + 1) * COLS)

    lhs = [
        pltpu.make_async_copy(
            received_ref.at[:, side, col, 0],
            lhs_ref.at[side, :, :, columns(col)],
            lhs_sems.at[side, col],
        )
        for side in range(2)
        for col in range(NC)
    ]
    rhs = [
        pltpu.make_async_copy(
            other_ref.at[:, col], rhs_ref.at[:, :, columns(col)], rhs_sems.at[col]
        )
        for col in range(NC)
    ]
    cells = [
        pltpu.make_async_copy(
            received_ref.at[col, e, :, 1, side * 32 : side * 32 + 32, :],
            cells_ref.at[:, side, col, e * 32 : e * 32 + 32, :],
            cell_sems.at[col, e, side],
        )
        for col in range(NC)
        for e in range(2)
        for side in range(2)
    ]
    for copy in rhs + lhs + cells:
        copy.start()
    for copy in rhs:
        copy.wait()
    outs = []
    for side in range(2):
        for copy in lhs[side * NC : side * NC + NC]:
            copy.wait()
        own = lhs_ref[side].reshape(half * ROWS, NC * COLS)
        for block in range(4):
            result = lax.dot_general(
                own,
                rhs_ref[4 * block : 4 * block + 4].reshape(256, NC * COLS),
                NT,
                preferred_element_type=F32,
            ).astype(BF)
            for col in range(2):
                result_ref[side, :, block * 2 + col] = result[:, columns(col)].reshape(
                    half, ROWS, COLS
                )
        copy = pltpu.make_async_copy(
            result_ref.at[side], out_ref.at[:, side, :, 0], out_sems.at[side]
        )
        copy.start()
        outs.append(copy)
        if side == 0:
            for moved in cells:
                moved.wait()
            copy = pltpu.make_async_copy(cells_ref, out_ref.at[:, :, :, 1], cell_out_sem)
            copy.start()
            outs.append(copy)
    for copy in outs:
        copy.wait()


def product(received, other):
    anywhere = pl.BlockSpec(memory_space=pl.ANY)
    half = NR // 2
    return pl.pallas_call(
        product_kernel,
        out_shape=jax.ShapeDtypeStruct((half, 2, NC, 2, ROWS, COLS), BF),
        in_specs=[anywhere, anywhere],
        out_specs=anywhere,
        scratch_shapes=[
            pltpu.VMEM((2, half, ROWS, NC * COLS), BF),
            pltpu.VMEM((NR, ROWS, NC * COLS), BF),
            pltpu.VMEM((2, half, NC, ROWS, COLS), BF),
            pltpu.VMEM((half, 2, NC, ROWS, COLS), BF),
            pltpu.SemaphoreType.DMA((2, NC)),
            pltpu.SemaphoreType.DMA((NC,)),
            pltpu.SemaphoreType.DMA((NC, 2, 2)),
            pltpu.SemaphoreType.DMA((2,)),
            pltpu.SemaphoreType.DMA(()),
        ],
        compiler_params=pltpu.CompilerParams(vmem_limit_bytes=PRODUCT_VMEM * MIB),
        name="product",
    )(received.reshape(half, 2, NC, 2, ROWS, COLS), other)


def gate_kernel(pair_ref, gain_ref, shift_ref, weight_ref, bias_ref, out_ref):
    cells = pair_ref[...].astype(F32).reshape(STEP * COLS, CH)
    normed = normalize(cells, gain_ref[...], shift_ref[...]).astype(BF)
    gate = jnp.dot(normed, weight_ref[...], preferred_element_type=F32) + bias_ref[...]
    out_ref[...] = sigmoid(gate).reshape(STEP, COLS, CH)


def gates(pair, gain, shift, weight, bias):
    whole = lambda *shape: pl.BlockSpec(shape, lambda s: (0,) * len(shape))
    block = pl.BlockSpec((STEP, COLS, CH), lambda s: (s, 0, 0))
    return pl.pallas_call(
        gate_kernel,
        grid=(ROWS // STEP,),
        out_shape=jax.ShapeDtypeStruct((ROWS, COLS, CH), F32),
        in_specs=[block, whole(1, CH), whole(1, CH), whole(CH, CH), whole(1, CH)],
        out_specs=block,
        compiler_params=pltpu.CompilerParams(vmem_limit_bytes=24 * MIB),
        cost_estimate=pl.CostEstimate(
            flops=2 * ROWS * COLS * CH * CH, bytes_accessed=6 * ROWS * COLS * CH, transcendentals=ROWS * COLS * CH
        ),
        name="gates",
    )(pair, gain, shift, weight, bias)


USTEP = 16
UNROLL_U = 1
UGROUP = 8
PITCH = 72


def update_kernel(
    pair_ref, own_gate_ref, tri_ref, mirror_ref, gain_ref, shift_ref, gate_ref, gate_bias_ref,
    out_weight_ref, out_bias_ref, sym_ref, cells_ref, lay_ref,
):
    step = pl.program_id(0)

    @pl.when(step == 0)
    def _():
        for d in range(128):
            for e in range(2):
                at = (e * 64 + d // 2) * PITCH + (d % 2) * 32
                cells_ref[at : at + 32, :] = mirror_ref[d, 0, e * 32 : e * 32 + 32, :].astype(F32)

    tri = tri_ref[:, :, :, 0].astype(F32)
    mean = jnp.mean(tri, axis=(0, 2), keepdims=True)
    centred = tri - mean
    spread = jnp.mean(centred * centred, axis=(0, 2), keepdims=True)
    lay_ref[...] = (centred * lax.rsqrt(spread + EPS)).reshape(2 * HID * USTEP, COLS)

    def body(part, carry):
        first = part * UGROUP
        change, cells = [], []
        for k in range(UGROUP):
            mid = lay_ref[pl.ds(first + k, 2 * HID, stride=USTEP), :].astype(BF)
            change.append(
                lax.dot_general(mid, out_weight_ref[...], TN, preferred_element_type=F32)
            )
            cells.append(
                cells_ref[pl.ds(step * USTEP + first + k, COLS, stride=PITCH), :]
            )
        change = jnp.concatenate(change, axis=0) + out_bias_ref[...]
        cells = jnp.concatenate(cells, axis=0)
        size = UGROUP * COLS
        own = (
            pair_ref[pl.ds(first, UGROUP)].astype(F32).reshape(size, CH)
            + own_gate_ref[pl.ds(first, UGROUP)].reshape(size, CH) * change[:, :CH]
        )
        normed = normalize(cells, gain_ref[...], shift_ref[...]).astype(BF)
        gate = sigmoid(
            jnp.dot(normed, gate_ref[...], preferred_element_type=F32) + gate_bias_ref[...]
        )
        mirrored = cells + gate * change[:, CH:]
        total = own.astype(BF).astype(F32) + mirrored.astype(BF).astype(F32)
        sym_ref[pl.ds(first, UGROUP)] = (total * 0.5).astype(BF).reshape(UGROUP, COLS, CH)
        return carry

    lax.fori_loop(0, USTEP // UGROUP, body, 0, unroll=UNROLL_U)


def update(pair, own_gate, received, gain, shift, gate, gate_bias, out_weight, out_bias):
    whole = lambda *shape: pl.BlockSpec(shape, lambda s: (0,) * len(shape))
    tri = received.reshape(8, 2, 8, 2, ROWS, COLS)
    cells = received.reshape(128, 2, ROWS, COLS)
    block = pl.BlockSpec((USTEP, COLS, CH), lambda s: (s, 0, 0))
    return pl.pallas_call(
        update_kernel,
        grid=(ROWS // USTEP,),
        out_shape=jax.ShapeDtypeStruct((ROWS, COLS, CH), BF),
        in_specs=[
            block,
            block,
            pl.BlockSpec((8, 2, 8, 1, USTEP, COLS), lambda s: (0, 0, 0, 0, s, 0)),
            pl.BlockSpec((128, 1, ROWS, COLS), lambda s: (0, 1, 0, 0)),
            whole(1, CH),
            whole(1, CH),
            whole(CH, CH),
            whole(1, CH),
            whole(2 * HID, 2 * CH),
            whole(1, 2 * CH),
        ],
        out_specs=block,
        scratch_shapes=[
            pltpu.VMEM((COLS * PITCH, CH), F32),
            pltpu.VMEM((2 * HID * USTEP, COLS), F32),
        ],
        compiler_params=pltpu.CompilerParams(vmem_limit_bytes=48 * MIB),
        name="update",
    )(pair, own_gate, tri, cells, gain, shift, gate, gate_bias, out_weight, out_bias)


def output_weight(weight, bias, gain, shift):
    scaled = (gain[:, None] * weight.astype(F32)).astype(BF).reshape(8, 1, 8, CH)
    nothing = jnp.zeros_like(scaled)
    own = jnp.concatenate([scaled, nothing], axis=1)
    mirrored = jnp.concatenate([nothing, scaled], axis=1)
    full = jnp.concatenate([own, mirrored], axis=3).reshape(2 * HID, 2 * CH)
    offset = bias + jnp.sum(shift[:, None] * weight.astype(F32), axis=0)
    return full, jnp.concatenate([offset, offset])[None]


def activation_kernel(sym_ref, gain_ref, shift_ref, out_ref):
    cells = sym_ref[...].astype(F32).reshape(STEP * COLS, CH)
    act = jnp.maximum(normalize(cells, gain_ref[0:1], shift_ref[0:1]), 0.0)
    out_ref[...] = act.astype(BF).reshape(STEP, COLS, CH)


def activations(sym, gain, shift):
    whole = lambda *shape: pl.BlockSpec(shape, lambda s: (0,) * len(shape))
    block = pl.BlockSpec((STEP, COLS, CH), lambda s: (s, 0, 0))
    return pl.pallas_call(
        activation_kernel,
        grid=(ROWS // STEP,),
        out_shape=jax.ShapeDtypeStruct((ROWS, COLS, CH), BF),
        in_specs=[block, whole(2, CH), whole(2, CH)],
        out_specs=block,
        compiler_params=pltpu.CompilerParams(vmem_limit_bytes=24 * MIB),
        cost_estimate=pl.CostEstimate(
            flops=16 * ROWS * COLS * CH, bytes_accessed=4 * ROWS * COLS * CH, transcendentals=ROWS * COLS
        ),
        name="activations",
    )(sym, gain, shift)


TALL = ROWS + 2 * HALO
SIDE = 8
WIDE = COLS + 4 * SIDE
FIRST_TALL = ROWS + 2 * SECOND_DILATION
FIRST_WIDE = COLS + 2 * SIDE
GROUP_B, GROUP_C = 4, 8
INNER_B, SLOTS_C = 9, 2
CONV_VMEM = 40


def convolution_kernel(
    place_ref, sym_ref, act_ref, top_ref, bottom_ref, low_ref, high_ref, gain_ref, shift_ref,
    bias_ref, weight_hbm, out_hbm, tall_ref, wide_ref, first_ref, second_ref, shifted_ref,
    late_ref, weight_ref, out_ref, sems, out_sems,
):
    top_copy = pltpu.make_async_copy(top_ref, tall_ref.at[0:HALO], sems.at[0])
    bottom_copy = pltpu.make_async_copy(bottom_ref, tall_ref.at[HALO + ROWS : TALL], sems.at[1])
    act_copy = pltpu.make_async_copy(
        act_ref, wide_ref.at[HALO : HALO + ROWS, 16 : 16 + COLS], sems.at[2]
    )
    weight_copy = pltpu.make_async_copy(weight_hbm, weight_ref, sems.at[3])
    sym_copy = pltpu.make_async_copy(sym_ref, tall_ref.at[HALO : HALO + ROWS], sems.at[4])
    for copy in (top_copy, bottom_copy, act_copy, weight_copy, sym_copy):
        copy.start()
    above = place_ref[0] > 0
    below = place_ref[0] < (NR - 1) * ROWS
    low_ok = (place_ref[1] > 0).astype(F32)
    high_ok = (place_ref[1] < (NC - 1) * COLS).astype(F32)

    def activate(cells, which):
        return jnp.maximum(
            normalize(
                cells,
                gain_ref[which : which + 1].reshape(1, 1, CH),
                shift_ref[which : which + 1].reshape(1, 1, CH),
            ),
            0.0,
        )

    nothing = jnp.zeros((TALL, SIDE, CH), F32)
    low = activate(low_ref[...].astype(F32), 0) * low_ok
    wide_ref[:, 0:16, :] = jnp.concatenate([nothing, low], axis=1).astype(BF)
    high = activate(high_ref[...].astype(F32), 0) * high_ok
    wide_ref[:, 16 + COLS :, :] = jnp.concatenate([high, nothing], axis=1).astype(BF)
    top_copy.wait()
    bottom_copy.wait()
    wide_ref[0:HALO, 16 : 16 + COLS, :] = activate(tall_ref[0:HALO].astype(F32), 0).astype(BF)
    wide_ref[HALO + ROWS :, 16 : 16 + COLS, :] = activate(
        tall_ref[HALO + ROWS :].astype(F32), 0
    ).astype(BF)

    @pl.when(jnp.logical_not(above))
    def _():
        wide_ref[0:HALO] = jnp.zeros((HALO, WIDE, CH), BF)

    @pl.when(jnp.logical_not(below))
    def _():
        wide_ref[HALO + ROWS :] = jnp.zeros((HALO, WIDE, CH), BF)

    def paired(source_ref, at, spacing, group, width, which):
        sets = group // (2 * spacing)
        lhs = jnp.concatenate(
            [
                jnp.concatenate(
                    [
                        source_ref[pl.ds(at + 2 * spacing * k + spacing * slot, spacing)]
                        for k in range(sets)
                    ],
                    axis=0,
                ).reshape(group // 2 * width, CH)
                for slot in range(4)
            ],
            axis=1,
        )
        total = jnp.dot(lhs, weight_ref[which], preferred_element_type=F32)
        taps = []
        for tap in range(3):
            near = total[:, tap * CH : (tap + 1) * CH].reshape(sets, spacing, width, CH)
            far = total[:, (3 + tap) * CH : (4 + tap) * CH].reshape(sets, spacing, width, CH)
            taps.append(jnp.concatenate([near, far], axis=1).reshape(group, width, CH))
        return taps

    def first_rows(at, slot):
        before, centre, after = paired(wide_ref, at, FIRST_DILATION, GROUP_B, WIDE, 0)
        shifted_ref[slot, 0] = before
        shifted_ref[slot, 1] = after
        residual = jnp.concatenate(
            [
                low_ref[pl.ds(at + 2, GROUP_B)].astype(F32),
                tall_ref[pl.ds(at + 2, GROUP_B)].astype(F32),
                high_ref[pl.ds(at + 2, GROUP_B)].astype(F32),
            ],
            axis=1,
        )
        first = (
            centre[:, 8 : 8 + FIRST_WIDE]
            + shifted_ref[slot, 0, :, 6 : 6 + FIRST_WIDE, :]
            + shifted_ref[slot, 1, :, 10 : 10 + FIRST_WIDE, :]
            + residual
            + bias_ref[0:1].reshape(1, 1, CH)
        )
        first_ref[pl.ds(at, GROUP_B)] = first[:, SIDE : SIDE + COLS]
        act = activate(first, 1)
        second_ref[pl.ds(at, GROUP_B)] = jnp.concatenate(
            [
                act[:, :SIDE] * low_ok,
                act[:, SIDE : SIDE + COLS],
                act[:, SIDE + COLS :] * high_ok,
            ],
            axis=1,
        ).astype(BF)

    def convolve_first(step, carry):
        for k in range(INNER_B):
            first_rows(step * (GROUP_B * INNER_B) + k * GROUP_B, k)
        return carry

    act_copy.wait()
    weight_copy.wait()
    sym_copy.wait()
    lax.fori_loop(0, FIRST_TALL // (GROUP_B * INNER_B), convolve_first, 0)

    @pl.when(jnp.logical_not(above))
    def _():
        second_ref[0:SECOND_DILATION] = jnp.zeros((SECOND_DILATION, FIRST_WIDE, CH), BF)

    @pl.when(jnp.logical_not(below))
    def _():
        second_ref[SECOND_DILATION + ROWS :] = jnp.zeros((SECOND_DILATION, FIRST_WIDE, CH), BF)

    def out_copy(k):
        return pltpu.make_async_copy(
            out_ref.at[16 * k : 16 * k + 16], out_hbm.at[16 * k : 16 * k + 16], out_sems.at[k]
        )

    for k in range(4):
        for part in range(16 // GROUP_C):
            at = 16 * k + part * GROUP_C
            slot = at // GROUP_C % SLOTS_C
            before, centre, after = paired(
                second_ref, at, SECOND_DILATION, GROUP_C, FIRST_WIDE, 1
            )
            late_ref[slot, 0] = before
            late_ref[slot, 1] = after
            out_ref[at : at + GROUP_C] = (
                centre[:, SIDE : SIDE + COLS]
                + late_ref[slot, 0, :, 4 : 4 + COLS, :]
                + late_ref[slot, 1, :, 12 : 12 + COLS, :]
                + first_ref[at + 4 : at + 4 + GROUP_C]
                + bias_ref[1:2].reshape(1, 1, CH)
            ).astype(BF)
        out_copy(k).start()
    for k in range(4):
        out_copy(k).wait()


def convolutions(place, sym, act, top, bottom, low, high, gain, shift, bias, weight):
    vmem = pl.BlockSpec(memory_space=pltpu.VMEM)
    anywhere = pl.BlockSpec(memory_space=pl.ANY)
    return pl.pallas_call(
        convolution_kernel,
        out_shape=jax.ShapeDtypeStruct((ROWS, COLS, CH), BF),
        in_specs=[pl.BlockSpec(memory_space=pltpu.SMEM)]
        + [anywhere] * 4
        + [vmem] * 5
        + [anywhere],
        out_specs=anywhere,
        scratch_shapes=[
            pltpu.VMEM((TALL, COLS, CH), BF),
            pltpu.VMEM((TALL, WIDE, CH), BF),
            pltpu.VMEM((FIRST_TALL, COLS, CH), F32),
            pltpu.VMEM((FIRST_TALL, FIRST_WIDE, CH), BF),
            pltpu.VMEM((INNER_B, 2, GROUP_B, WIDE, CH), F32),
            pltpu.VMEM((SLOTS_C, 2, GROUP_C, FIRST_WIDE, CH), F32),
            pltpu.VMEM((2, 4 * CH, 6 * CH), BF),
            pltpu.VMEM((ROWS, COLS, CH), BF),
            pltpu.SemaphoreType.DMA((5,)),
            pltpu.SemaphoreType.DMA((4,)),
        ],
        compiler_params=pltpu.CompilerParams(vmem_limit_bytes=CONV_VMEM * MIB),
        name="convolutions",
    )(place, sym, act, top, bottom, low, high, gain, shift, bias, weight)


def paired_weight(weight):
    taps = jnp.transpose(weight.reshape(3, 3, CH, CH), (0, 2, 1, 3)).reshape(3, CH, 3 * CH)
    near = jnp.concatenate([taps, jnp.zeros_like(taps[:1])], axis=0)
    far = jnp.concatenate([jnp.zeros_like(taps[:1]), taps], axis=0)
    return jnp.concatenate([near, far], axis=2).reshape(4 * CH, 6 * CH)


def neighbours(low_strip, high_strip, axis):
    count = lax.axis_size(axis)
    forward = [(i, i + 1) for i in range(count - 1)]
    backward = [(i + 1, i) for i in range(count - 1)]
    return lax.ppermute(high_strip, axis, forward), lax.ppermute(low_strip, axis, backward)


def local(
    pair, norm_gain, norm_shift, proj_weight, proj_bias, mid_gain, mid_shift, out_weight, out_bias,
    conv_gain, conv_shift, convolution_weight, convolution_bias,
):
    gain, shift = norm_gain[None], norm_shift[None]
    sent = factors(pair, gain, shift, proj_weight, proj_bias)
    received = lax.all_to_all(
        sent.reshape(128, 2, ROWS, COLS), ("row", "col"), split_axis=0, concat_axis=0, tiled=True
    ).reshape(NR, NC, 2, ROWS, COLS)
    other = lax.ppermute(plane(received), "row", [(i, i ^ 1) for i in range(NR)])
    back = product(received, other)
    returned = lax.all_to_all(
        back.reshape(128, 2, ROWS, COLS), ("row", "col"), split_axis=0, concat_axis=0, tiled=True
    )
    gate, gate_bias = proj_weight[:, 4 * HID :], proj_bias[None, 4 * HID :]
    paired = jnp.stack([paired_weight(convolution_weight[0]), paired_weight(convolution_weight[1])])
    gate, paired = lax.optimization_barrier((gate, paired))
    sym = update(
        pair, gates(pair, gain, shift, gate, gate_bias), returned, gain, shift, gate, gate_bias,
        *output_weight(out_weight, out_bias, mid_gain, mid_shift),
    )
    top, bottom = neighbours(sym[:HALO], sym[ROWS - HALO :], "row")
    edge = lambda low, high: jnp.concatenate(
        [top[:, low:high], sym[:, low:high], bottom[:, low:high]], axis=0
    )
    low, high = neighbours(edge(0, SIDE), edge(COLS - SIDE, COLS), "col")
    place = jnp.stack([lax.axis_index("row") * ROWS, lax.axis_index("col") * COLS]).astype(jnp.int32)
    return convolutions(
        place, sym, activations(sym, conv_gain, conv_shift), top, bottom, low, high, conv_gain, conv_shift, convolution_bias,
        paired,
    )


def solution(mesh):
    return jax.shard_map(
        local,
        mesh=mesh,
        in_specs=(P("row", "col", None),) + (P(),) * 12,
        out_specs=P("row", "col", None),
        check_vma=False,
    )
```

```python
import jax
import jax.numpy as jnp
from jax import lax
from jax.experimental import pallas as pl
from jax.experimental.pallas import tpu as pltpu
from jax.sharding import PartitionSpec as P

FIRST_DILATION = 2
SECOND_DILATION = 4
HALO = FIRST_DILATION + SECOND_DILATION
EPS = 1e-05
BF = jnp.bfloat16
F32 = jnp.float32
MIB = 1 << 20
ROWS, COLS, CH, HID = 64, 128, 128, 64
NR, NC = 16, 8


def sigmoid(x):
    return 0.5 * jnp.tanh(0.5 * x) + 0.5


def normalize(values, gain, shift):
    mean = jnp.mean(values, axis=-1, keepdims=True)
    centred = values - mean
    spread = jnp.mean(centred * centred, axis=-1, keepdims=True)
    return centred * lax.rsqrt(spread + EPS) * gain + shift


NT = (((1,), (1,)), ((), ()))
TN = (((0,), (0,)), ((), ()))

STEP = 16


def factor_kernel(
    pair_ref, gain_ref, shift_ref, weight_ref, bias_ref, out_ref, lay_ref, stage_ref, cells_ref,
    cell_sems, stage_sems,
):
    step = pl.program_id(0)

    def cell_copy(k):
        return pltpu.make_async_copy(
            cells_ref.at[k], out_ref.at[pl.ds(2 * k, 2), :, :, :, 1], cell_sems.at[k]
        )

    def stage_copy(k):
        start = pl.multiple_of(k * STEP, STEP)
        return pltpu.make_async_copy(
            stage_ref.at[k], out_ref.at[:, :, :, :, 0, pl.ds(start, STEP), :], stage_sems.at[k]
        )

    for row in range(STEP):
        for q in range(2):
            for half in range(2):
                start = half * 64 + q * 32
                cells_ref[
                    step, row // 8, (row // 4) % 2, row % 4, q, half * 32 : half * 32 + 32, :
                ] = pair_ref[row, start : start + 32, :]
    cell_copy(step).start()
    cells = pair_ref[...].astype(F32).reshape(STEP * COLS, CH)
    normed = normalize(cells, gain_ref[...], shift_ref[...]).astype(BF)
    bias = jnp.transpose(jnp.broadcast_to(bias_ref[...][None], (COLS, 4 * HID + CH))[:, : 4 * HID])
    projected = lax.dot_general(
        weight_ref[:, : 4 * HID], normed, (((0,), (1,)), ((), ())), preferred_element_type=F32
    )
    for side in range(2):
        base = 2 * HID * side
        for row in range(STEP):
            part = slice(row * COLS, (row + 1) * COLS)
            gate = projected[base : base + HID, part] + bias[base : base + HID]
            value = projected[base + HID : base + 2 * HID, part] + bias[base + HID : base + 2 * HID]
            lay_ref[pl.ds(row, HID, stride=STEP), :] = sigmoid(gate) * value
        stage_ref[step, :, side] = lay_ref[...].astype(BF).reshape(8, 4, 2, STEP, COLS)
    stage_copy(step).start()

    @pl.when(step == ROWS // STEP - 1)
    def _():
        for k in range(ROWS // STEP):
            cell_copy(k).wait()
            stage_copy(k).wait()


FACTORS_VMEM = 60


def factors(pair, gain, shift, weight, bias):
    whole = lambda *shape: pl.BlockSpec(shape, lambda s: (0,) * len(shape))
    steps = ROWS // STEP
    return pl.pallas_call(
        factor_kernel,
        grid=(steps,),
        out_shape=jax.ShapeDtypeStruct((8, 2, 4, 2, 2, ROWS, COLS), BF),
        in_specs=[
            pl.BlockSpec((STEP, COLS, CH), lambda s: (s, 0, 0)),
            whole(1, CH),
            whole(1, CH),
            whole(CH, 4 * HID + CH),
            whole(4 * HID + CH),
        ],
        out_specs=pl.BlockSpec(memory_space=pl.ANY),
        scratch_shapes=[
            pltpu.VMEM((HID * STEP, COLS), F32),
            pltpu.VMEM((steps, 8, 2, 4, 2, STEP, COLS), BF),
            pltpu.VMEM((steps, 2, 2, 4, 2, ROWS, COLS), BF),
            pltpu.SemaphoreType.DMA((steps,)),
            pltpu.SemaphoreType.DMA((steps,)),
        ],
        compiler_params=pltpu.CompilerParams(vmem_limit_bytes=FACTORS_VMEM * MIB),
        name="factors",
    )(pair, gain, shift, weight, bias)


SPLIT_VMEM = 16
PRODUCT_VMEM = 62


def split_kernel(
    received_ref, cells_out_ref, plane_out_ref, cells_ref, plane_ref, cell_sems, plane_sem, out_sems
):
    cells = [
        pltpu.make_async_copy(
            received_ref.at[col, e, :, 1, side * 32 : side * 32 + 32, :],
            cells_ref.at[:, side, col, e * 32 : e * 32 + 32, :],
            cell_sems.at[col, e, side],
        )
        for col in range(NC)
        for e in range(2)
        for side in range(2)
    ]
    own = pltpu.make_async_copy(received_ref.at[:, :, :, 0], plane_ref, plane_sem)
    for copy in cells + [own]:
        copy.start()
    for copy in cells:
        copy.wait()
    cells_out = pltpu.make_async_copy(cells_ref, cells_out_ref, out_sems.at[0])
    cells_out.start()
    own.wait()
    plane_out = pltpu.make_async_copy(plane_ref, plane_out_ref, out_sems.at[1])
    plane_out.start()
    cells_out.wait()
    plane_out.wait()


def split(received):
    anywhere = pl.BlockSpec(memory_space=pl.ANY)
    half = NR // 2
    return pl.pallas_call(
        split_kernel,
        out_shape=[jax.ShapeDtypeStruct((half, 2, NC, ROWS, COLS), BF)] * 2,
        in_specs=[anywhere],
        out_specs=[anywhere, anywhere],
        scratch_shapes=[
            pltpu.VMEM((half, 2, NC, ROWS, COLS), BF),
            pltpu.VMEM((half, 2, NC, ROWS, COLS), BF),
            pltpu.SemaphoreType.DMA((NC, 2, 2)),
            pltpu.SemaphoreType.DMA(()),
            pltpu.SemaphoreType.DMA((2,)),
        ],
        compiler_params=pltpu.CompilerParams(vmem_limit_bytes=SPLIT_VMEM * MIB),
        name="split",
    )(received.reshape(half, 2, NC, 2, ROWS, COLS))


def product_kernel(
    own_ref, other_ref, out_ref, lhs_ref, rhs_ref, result_ref, lhs_sems, rhs_sems, out_sems
):
    half = NR // 2

    def columns(col):
        return slice(col * COLS, (col + 1) * COLS)

    lhs = [
        pltpu.make_async_copy(
            own_ref.at[:, side, col], lhs_ref.at[side, :, :, columns(col)], lhs_sems.at[side, col]
        )
        for side in range(2)
        for col in range(NC)
    ]
    rhs = [
        pltpu.make_async_copy(
            other_ref.at[:, :, col], rhs_ref.at[:, :, :, columns(col)], rhs_sems.at[col]
        )
        for col in range(NC)
    ]
    for copy in rhs + lhs:
        copy.start()
    for copy in rhs:
        copy.wait()
    outs = []
    for side in range(2):
        for copy in lhs[side * NC : side * NC + NC]:
            copy.wait()
        own = lhs_ref[side].reshape(half * ROWS, NC * COLS)
        for block in range(4):
            result = lax.dot_general(
                own,
                rhs_ref[2 * block : 2 * block + 2].reshape(4 * ROWS, NC * COLS),
                NT,
                preferred_element_type=F32,
            ).astype(BF)
            for col in range(2):
                result_ref[side, :, block * 2 + col] = result[:, columns(col)].reshape(
                    half, ROWS, COLS
                )
        copy = pltpu.make_async_copy(
            result_ref.at[side], out_ref.at[:, side], out_sems.at[side]
        )
        copy.start()
        outs.append(copy)
    for copy in outs:
        copy.wait()


def product(own, other):
    anywhere = pl.BlockSpec(memory_space=pl.ANY)
    half = NR // 2
    return pl.pallas_call(
        product_kernel,
        out_shape=jax.ShapeDtypeStruct((half, 2, NC, ROWS, COLS), BF),
        in_specs=[anywhere, anywhere],
        out_specs=anywhere,
        scratch_shapes=[
            pltpu.VMEM((2, half, ROWS, NC * COLS), BF),
            pltpu.VMEM((half, 2, ROWS, NC * COLS), BF),
            pltpu.VMEM((2, half, NC, ROWS, COLS), BF),
            pltpu.SemaphoreType.DMA((2, NC)),
            pltpu.SemaphoreType.DMA((NC,)),
            pltpu.SemaphoreType.DMA((2,)),
        ],
        compiler_params=pltpu.CompilerParams(vmem_limit_bytes=PRODUCT_VMEM * MIB),
        cost_estimate=pl.CostEstimate(
            flops=2 * 1024**3, bytes_accessed=6 * MIB, transcendentals=0
        ),
        name="product",
    )(own, other)


def gate_kernel(pair_ref, gain_ref, shift_ref, weight_ref, bias_ref, out_ref):
    cells = pair_ref[...].astype(F32).reshape(STEP * COLS, CH)
    normed = normalize(cells, gain_ref[...], shift_ref[...]).astype(BF)
    gate = jnp.dot(normed, weight_ref[...], preferred_element_type=F32) + bias_ref[...]
    out_ref[...] = sigmoid(gate).astype(BF).reshape(STEP, COLS, CH)


def gates(pair, gain, shift, weight, bias):
    whole = lambda *shape: pl.BlockSpec(shape, lambda s: (0,) * len(shape))
    block = pl.BlockSpec((STEP, COLS, CH), lambda s: (s, 0, 0))
    return pl.pallas_call(
        gate_kernel,
        grid=(ROWS // STEP,),
        out_shape=jax.ShapeDtypeStruct((ROWS, COLS, CH), BF),
        in_specs=[block, whole(1, CH), whole(1, CH), whole(CH, CH), whole(1, CH)],
        out_specs=block,
        compiler_params=pltpu.CompilerParams(vmem_limit_bytes=24 * MIB),
        cost_estimate=pl.CostEstimate(
            flops=2 * ROWS * COLS * CH * CH, bytes_accessed=4 * ROWS * COLS * CH, transcendentals=ROWS * COLS * CH
        ),
        name="gates",
    )(pair, gain, shift, weight, bias)


PITCH = 24
MGROUP = 8


def mirror_kernel(
    mirror_ref, gain_ref, shift_ref, weight_ref, bias_ref, out_ref, gate_ref, cells_ref
):
    for e in range(2):
        for j in range(64):
            at = (e * 64 + j) * PITCH
            cells_ref[at : at + STEP, :] = mirror_ref[j, 0, e, 0].astype(F32)
    for part in range(STEP // MGROUP):
        rows = [
            cells_ref[pl.ds(part * MGROUP + k, COLS, stride=PITCH), :] for k in range(MGROUP)
        ]
        cells = jnp.concatenate(rows, axis=0)
        here = slice(part * MGROUP, (part + 1) * MGROUP)
        out_ref[here] = cells.astype(BF).reshape(MGROUP, COLS, CH)
        normed = normalize(cells, gain_ref[...], shift_ref[...]).astype(BF)
        gate = jnp.dot(normed, weight_ref[...], preferred_element_type=F32) + bias_ref[...]
        gate_ref[here] = sigmoid(gate).astype(BF).reshape(MGROUP, COLS, CH)


def mirror_gates(mirrored, gain, shift, weight, bias):
    whole = lambda *shape: pl.BlockSpec(shape, lambda s: (0,) * len(shape))
    block = pl.BlockSpec((STEP, COLS, CH), lambda s: (s, 0, 0))
    return pl.pallas_call(
        mirror_kernel,
        grid=(ROWS // STEP,),
        out_shape=[
            jax.ShapeDtypeStruct((ROWS, COLS, CH), BF),
            jax.ShapeDtypeStruct((ROWS, COLS, CH), BF),
        ],
        in_specs=[
            pl.BlockSpec((64, 1, 2, 1, STEP, CH), lambda s: (0, s // 2, 0, s % 2, 0, 0)),
            whole(1, CH),
            whole(1, CH),
            whole(CH, CH),
            whole(1, CH),
        ],
        out_specs=[block, block],
        scratch_shapes=[pltpu.VMEM((COLS * PITCH, CH), F32)],
        compiler_params=pltpu.CompilerParams(vmem_limit_bytes=24 * MIB),
        cost_estimate=pl.CostEstimate(
            flops=2 * ROWS * COLS * CH * CH, bytes_accessed=8 * ROWS * COLS * CH, transcendentals=ROWS * COLS * CH
        ),
        name="mirror_gates",
    )(mirrored.reshape(64, 2, 2, 2, STEP, CH), gain, shift, weight, bias)


USTEP = 16
UNROLL_U = 1
UGROUP = 8
UPDATE_VMEM = 50


def update_kernel(
    pair_ref, own_gate_ref, cells_ref, gate_ref, tri_ref, out_weight_ref, out_bias_ref, sym_ref,
    lay_ref,
):
    tri = tri_ref[...].astype(F32)
    mean = jnp.mean(tri, axis=(0, 2), keepdims=True)
    centred = tri - mean
    spread = jnp.mean(centred * centred, axis=(0, 2), keepdims=True)
    lay_ref[...] = (centred * lax.rsqrt(spread + EPS)).reshape(2 * HID * USTEP, COLS)
    size = UGROUP * COLS

    def rows(ref, first):
        return ref[pl.ds(first, UGROUP)].astype(F32).reshape(size, CH)

    def body(part, carry):
        first = part * UGROUP
        change = [
            lax.dot_general(
                lay_ref[pl.ds(first + k, 2 * HID, stride=USTEP), :].astype(BF),
                out_weight_ref[...],
                TN,
                preferred_element_type=F32,
            )
            for k in range(UGROUP)
        ]
        change = jnp.concatenate(change, axis=0) + out_bias_ref[...]
        own = rows(pair_ref, first) + rows(own_gate_ref, first) * change[:, :CH]
        mirrored = rows(cells_ref, first) + rows(gate_ref, first) * change[:, CH:]
        total = own.astype(BF).astype(F32) + mirrored.astype(BF).astype(F32)
        sym_ref[pl.ds(first, UGROUP)] = (total * 0.5).astype(BF).reshape(UGROUP, COLS, CH)
        return carry

    lax.fori_loop(0, USTEP // UGROUP, body, 0, unroll=UNROLL_U)


def update(pair, own_gate, cells, gate, returned, out_weight, out_bias):
    whole = lambda *shape: pl.BlockSpec(shape, lambda s: (0,) * len(shape))
    block = pl.BlockSpec((USTEP, COLS, CH), lambda s: (s, 0, 0))
    return pl.pallas_call(
        update_kernel,
        grid=(ROWS // USTEP,),
        out_shape=jax.ShapeDtypeStruct((ROWS, COLS, CH), BF),
        in_specs=[
            block,
            block,
            block,
            block,
            pl.BlockSpec((8, 2, 8, USTEP, COLS), lambda s: (0, 0, 0, s, 0)),
            whole(2 * HID, 2 * CH),
            whole(1, 2 * CH),
        ],
        out_specs=block,
        scratch_shapes=[pltpu.VMEM((2 * HID * USTEP, COLS), F32)],
        compiler_params=pltpu.CompilerParams(vmem_limit_bytes=UPDATE_VMEM * MIB),
        name="update",
    )(pair, own_gate, cells, gate, returned.reshape(8, 2, 8, ROWS, COLS), out_weight, out_bias)


def output_weight(weight, bias, gain, shift):
    scaled = (gain[:, None] * weight.astype(F32)).astype(BF).reshape(8, 1, 8, CH)
    nothing = jnp.zeros_like(scaled)
    own = jnp.concatenate([scaled, nothing], axis=1)
    mirrored = jnp.concatenate([nothing, scaled], axis=1)
    full = jnp.concatenate([own, mirrored], axis=3).reshape(2 * HID, 2 * CH)
    offset = bias + jnp.sum(shift[:, None] * weight.astype(F32), axis=0)
    return full, jnp.concatenate([offset, offset])[None]


def activation_kernel(sym_ref, gain_ref, shift_ref, out_ref):
    cells = sym_ref[...].astype(F32).reshape(STEP * COLS, CH)
    act = jnp.maximum(normalize(cells, gain_ref[0:1], shift_ref[0:1]), 0.0)
    out_ref[...] = act.astype(BF).reshape(STEP, COLS, CH)


def activations(sym, gain, shift):
    whole = lambda *shape: pl.BlockSpec(shape, lambda s: (0,) * len(shape))
    block = pl.BlockSpec((STEP, COLS, CH), lambda s: (s, 0, 0))
    return pl.pallas_call(
        activation_kernel,
        grid=(ROWS // STEP,),
        out_shape=jax.ShapeDtypeStruct((ROWS, COLS, CH), BF),
        in_specs=[block, whole(2, CH), whole(2, CH)],
        out_specs=block,
        compiler_params=pltpu.CompilerParams(vmem_limit_bytes=24 * MIB),
        cost_estimate=pl.CostEstimate(
            flops=16 * ROWS * COLS * CH, bytes_accessed=4 * ROWS * COLS * CH, transcendentals=ROWS * COLS
        ),
        name="activations",
    )(sym, gain, shift)


TALL = ROWS + 2 * HALO
SIDE = 8
WIDE = COLS + 4 * SIDE
FIRST_TALL = ROWS + 2 * SECOND_DILATION
FIRST_WIDE = COLS + 2 * SIDE
GROUP_B, GROUP_C = 4, 8
INNER_B, SLOTS_C = 9, 2
CONV_VMEM = 40


def convolution_kernel(
    place_ref, sym_ref, act_ref, top_ref, bottom_ref, low_ref, high_ref, gain_ref, shift_ref,
    bias_ref, weight_hbm, out_hbm, tall_ref, wide_ref, first_ref, second_ref, shifted_ref,
    late_ref, weight_ref, out_ref, sems, out_sems,
):
    top_copy = pltpu.make_async_copy(top_ref, tall_ref.at[0:HALO], sems.at[0])
    bottom_copy = pltpu.make_async_copy(bottom_ref, tall_ref.at[HALO + ROWS : TALL], sems.at[1])
    act_copy = pltpu.make_async_copy(
        act_ref, wide_ref.at[HALO : HALO + ROWS, 16 : 16 + COLS], sems.at[2]
    )
    weight_copy = pltpu.make_async_copy(weight_hbm, weight_ref, sems.at[3])
    sym_copy = pltpu.make_async_copy(sym_ref, tall_ref.at[HALO : HALO + ROWS], sems.at[4])
    for copy in (top_copy, bottom_copy, act_copy, weight_copy, sym_copy):
        copy.start()
    above = place_ref[0] > 0
    below = place_ref[0] < (NR - 1) * ROWS
    low_ok = (place_ref[1] > 0).astype(F32)
    high_ok = (place_ref[1] < (NC - 1) * COLS).astype(F32)

    def activate(cells, which):
        return jnp.maximum(
            normalize(
                cells,
                gain_ref[which : which + 1].reshape(1, 1, CH),
                shift_ref[which : which + 1].reshape(1, 1, CH),
            ),
            0.0,
        )

    nothing = jnp.zeros((TALL, SIDE, CH), F32)
    low = activate(low_ref[...].astype(F32), 0) * low_ok
    wide_ref[:, 0:16, :] = jnp.concatenate([nothing, low], axis=1).astype(BF)
    high = activate(high_ref[...].astype(F32), 0) * high_ok
    wide_ref[:, 16 + COLS :, :] = jnp.concatenate([high, nothing], axis=1).astype(BF)
    top_copy.wait()
    bottom_copy.wait()
    wide_ref[0:HALO, 16 : 16 + COLS, :] = activate(tall_ref[0:HALO].astype(F32), 0).astype(BF)
    wide_ref[HALO + ROWS :, 16 : 16 + COLS, :] = activate(
        tall_ref[HALO + ROWS :].astype(F32), 0
    ).astype(BF)

    @pl.when(jnp.logical_not(above))
    def _():
        wide_ref[0:HALO] = jnp.zeros((HALO, WIDE, CH), BF)

    @pl.when(jnp.logical_not(below))
    def _():
        wide_ref[HALO + ROWS :] = jnp.zeros((HALO, WIDE, CH), BF)

    def paired(source_ref, at, spacing, group, width, which):
        sets = group // (2 * spacing)
        lhs = jnp.concatenate(
            [
                jnp.concatenate(
                    [
                        source_ref[pl.ds(at + 2 * spacing * k + spacing * slot, spacing)]
                        for k in range(sets)
                    ],
                    axis=0,
                ).reshape(group // 2 * width, CH)
                for slot in range(4)
            ],
            axis=1,
        )
        total = jnp.dot(lhs, weight_ref[which], preferred_element_type=F32)
        taps = []
        for tap in range(3):
            near = total[:, tap * CH : (tap + 1) * CH].reshape(sets, spacing, width, CH)
            far = total[:, (3 + tap) * CH : (4 + tap) * CH].reshape(sets, spacing, width, CH)
            taps.append(jnp.concatenate([near, far], axis=1).reshape(group, width, CH))
        return taps

    def first_rows(at, slot):
        before, centre, after = paired(wide_ref, at, FIRST_DILATION, GROUP_B, WIDE, 0)
        shifted_ref[slot, 0] = before
        shifted_ref[slot, 1] = after
        residual = jnp.concatenate(
            [
                low_ref[pl.ds(at + 2, GROUP_B)].astype(F32),
                tall_ref[pl.ds(at + 2, GROUP_B)].astype(F32),
                high_ref[pl.ds(at + 2, GROUP_B)].astype(F32),
            ],
            axis=1,
        )
        first = (
            centre[:, 8 : 8 + FIRST_WIDE]
            + shifted_ref[slot, 0, :, 6 : 6 + FIRST_WIDE, :]
            + shifted_ref[slot, 1, :, 10 : 10 + FIRST_WIDE, :]
            + residual
            + bias_ref[0:1].reshape(1, 1, CH)
        )
        first_ref[pl.ds(at, GROUP_B)] = first[:, SIDE : SIDE + COLS]
        act = activate(first, 1)
        second_ref[pl.ds(at, GROUP_B)] = jnp.concatenate(
            [
                act[:, :SIDE] * low_ok,
                act[:, SIDE : SIDE + COLS],
                act[:, SIDE + COLS :] * high_ok,
            ],
            axis=1,
        ).astype(BF)

    def convolve_first(step, carry):
        for k in range(INNER_B):
            first_rows(step * (GROUP_B * INNER_B) + k * GROUP_B, k)
        return carry

    act_copy.wait()
    weight_copy.wait()
    sym_copy.wait()
    lax.fori_loop(0, FIRST_TALL // (GROUP_B * INNER_B), convolve_first, 0)

    @pl.when(jnp.logical_not(above))
    def _():
        second_ref[0:SECOND_DILATION] = jnp.zeros((SECOND_DILATION, FIRST_WIDE, CH), BF)

    @pl.when(jnp.logical_not(below))
    def _():
        second_ref[SECOND_DILATION + ROWS :] = jnp.zeros((SECOND_DILATION, FIRST_WIDE, CH), BF)

    def out_copy(k):
        return pltpu.make_async_copy(
            out_ref.at[16 * k : 16 * k + 16], out_hbm.at[16 * k : 16 * k + 16], out_sems.at[k]
        )

    for k in range(4):
        for part in range(16 // GROUP_C):
            at = 16 * k + part * GROUP_C
            slot = at // GROUP_C % SLOTS_C
            before, centre, after = paired(
                second_ref, at, SECOND_DILATION, GROUP_C, FIRST_WIDE, 1
            )
            late_ref[slot, 0] = before
            late_ref[slot, 1] = after
            out_ref[at : at + GROUP_C] = (
                centre[:, SIDE : SIDE + COLS]
                + late_ref[slot, 0, :, 4 : 4 + COLS, :]
                + late_ref[slot, 1, :, 12 : 12 + COLS, :]
                + first_ref[at + 4 : at + 4 + GROUP_C]
                + bias_ref[1:2].reshape(1, 1, CH)
            ).astype(BF)
        out_copy(k).start()
    for k in range(4):
        out_copy(k).wait()


def convolutions(place, sym, act, top, bottom, low, high, gain, shift, bias, weight):
    vmem = pl.BlockSpec(memory_space=pltpu.VMEM)
    anywhere = pl.BlockSpec(memory_space=pl.ANY)
    return pl.pallas_call(
        convolution_kernel,
        out_shape=jax.ShapeDtypeStruct((ROWS, COLS, CH), BF),
        in_specs=[pl.BlockSpec(memory_space=pltpu.SMEM)]
        + [anywhere] * 4
        + [vmem] * 5
        + [anywhere],
        out_specs=anywhere,
        scratch_shapes=[
            pltpu.VMEM((TALL, COLS, CH), BF),
            pltpu.VMEM((TALL, WIDE, CH), BF),
            pltpu.VMEM((FIRST_TALL, COLS, CH), F32),
            pltpu.VMEM((FIRST_TALL, FIRST_WIDE, CH), BF),
            pltpu.VMEM((INNER_B, 2, GROUP_B, WIDE, CH), F32),
            pltpu.VMEM((SLOTS_C, 2, GROUP_C, FIRST_WIDE, CH), F32),
            pltpu.VMEM((2, 4 * CH, 6 * CH), BF),
            pltpu.VMEM((ROWS, COLS, CH), BF),
            pltpu.SemaphoreType.DMA((5,)),
            pltpu.SemaphoreType.DMA((4,)),
        ],
        compiler_params=pltpu.CompilerParams(vmem_limit_bytes=CONV_VMEM * MIB),
        name="convolutions",
    )(place, sym, act, top, bottom, low, high, gain, shift, bias, weight)


def paired_weight(weight):
    taps = jnp.transpose(weight.reshape(3, 3, CH, CH), (0, 2, 1, 3)).reshape(3, CH, 3 * CH)
    near = jnp.concatenate([taps, jnp.zeros_like(taps[:1])], axis=0)
    far = jnp.concatenate([jnp.zeros_like(taps[:1]), taps], axis=0)
    return jnp.concatenate([near, far], axis=2).reshape(4 * CH, 6 * CH)


def neighbours(low_strip, high_strip, axis):
    count = lax.axis_size(axis)
    forward = [(i, i + 1) for i in range(count - 1)]
    backward = [(i + 1, i) for i in range(count - 1)]
    return lax.ppermute(high_strip, axis, forward), lax.ppermute(low_strip, axis, backward)


def local(
    pair, norm_gain, norm_shift, proj_weight, proj_bias, mid_gain, mid_shift, out_weight, out_bias,
    conv_gain, conv_shift, convolution_weight, convolution_bias,
):
    gain, shift = norm_gain[None], norm_shift[None]
    sent = factors(pair, gain, shift, proj_weight, proj_bias)
    exchange = lambda v: lax.all_to_all(
        v, ("row", "col"), split_axis=0, concat_axis=0, tiled=True
    )
    received = exchange(sent.reshape(128, 2, ROWS, COLS))
    cells, own = split(received)
    mirrored = exchange(cells.reshape(128, ROWS, COLS))
    other = lax.ppermute(own, "row", [(i, i ^ 1) for i in range(NR)])
    returned = exchange(product(own, other).reshape(128, ROWS, COLS))
    gate, gate_bias = proj_weight[:, 4 * HID :], proj_bias[None, 4 * HID :]
    paired = jnp.stack([paired_weight(convolution_weight[0]), paired_weight(convolution_weight[1])])
    gate, paired = lax.optimization_barrier((gate, paired))
    sym = update(
        pair,
        gates(pair, gain, shift, gate, gate_bias),
        *mirror_gates(mirrored, gain, shift, gate, gate_bias),
        returned,
        *output_weight(out_weight, out_bias, mid_gain, mid_shift),
    )
    top, bottom = neighbours(sym[:HALO], sym[ROWS - HALO :], "row")
    edge = lambda low, high: jnp.concatenate(
        [top[:, low:high], sym[:, low:high], bottom[:, low:high]], axis=0
    )
    low, high = neighbours(edge(0, SIDE), edge(COLS - SIDE, COLS), "col")
    place = jnp.stack([lax.axis_index("row") * ROWS, lax.axis_index("col") * COLS]).astype(jnp.int32)
    return convolutions(
        place, sym, activations(sym, conv_gain, conv_shift), top, bottom, low, high, conv_gain, conv_shift, convolution_bias,
        paired,
    )


def solution(mesh):
    return jax.shard_map(
        local,
        mesh=mesh,
        in_specs=(P("row", "col", None),) + (P(),) * 12,
        out_specs=P("row", "col", None),
        check_vma=False,
    )
```

```python
import jax
import jax.numpy as jnp
from jax import lax
from jax.experimental import pallas as pl
from jax.experimental.pallas import tpu as pltpu
from jax.sharding import PartitionSpec as P

FIRST_DILATION = 2
SECOND_DILATION = 4
HALO = FIRST_DILATION + SECOND_DILATION
EPS = 1e-05
BF = jnp.bfloat16
F32 = jnp.float32
MIB = 1 << 20
ROWS, COLS, CH, HID = 64, 128, 128, 64
NR, NC = 16, 8


def sigmoid(x):
    return 0.5 * jnp.tanh(0.5 * x) + 0.5


def normalize(values, gain, shift):
    mean = jnp.mean(values, axis=-1, keepdims=True)
    centred = values - mean
    spread = jnp.mean(centred * centred, axis=-1, keepdims=True)
    return centred * lax.rsqrt(spread + EPS) * gain + shift


NT = (((1,), (1,)), ((), ()))
TN = (((0,), (0,)), ((), ()))

STEP = 16


def factor_kernel(
    pair_ref, gain_ref, shift_ref, weight_ref, bias_ref, out_ref, lay_ref, stage_ref, cells_ref,
    cell_sems, stage_sems,
):
    step = pl.program_id(0)

    def cell_copy(k):
        return pltpu.make_async_copy(
            cells_ref.at[k], out_ref.at[pl.ds(2 * k, 2), :, :, :, 1], cell_sems.at[k]
        )

    def stage_copy(k):
        start = pl.multiple_of(k * STEP, STEP)
        return pltpu.make_async_copy(
            stage_ref.at[k], out_ref.at[:, :, :, :, 0, pl.ds(start, STEP), :], stage_sems.at[k]
        )

    for row in range(STEP):
        for q in range(2):
            for half in range(2):
                start = half * 64 + q * 32
                cells_ref[
                    step, row // 8, (row // 4) % 2, row % 4, q, half * 32 : half * 32 + 32, :
                ] = pair_ref[row, start : start + 32, :]
    cell_copy(step).start()
    cells = pair_ref[...].astype(F32).reshape(STEP * COLS, CH)
    normed = normalize(cells, gain_ref[...], shift_ref[...]).astype(BF)
    bias = jnp.transpose(jnp.broadcast_to(bias_ref[...][None], (COLS, 4 * HID + CH))[:, : 4 * HID])
    projected = lax.dot_general(
        weight_ref[:, : 4 * HID], normed, (((0,), (1,)), ((), ())), preferred_element_type=F32
    )
    for side in range(2):
        base = 2 * HID * side
        for row in range(STEP):
            part = slice(row * COLS, (row + 1) * COLS)
            gate = projected[base : base + HID, part] + bias[base : base + HID]
            value = projected[base + HID : base + 2 * HID, part] + bias[base + HID : base + 2 * HID]
            lay_ref[pl.ds(row, HID, stride=STEP), :] = sigmoid(gate) * value
        stage_ref[step, :, side] = lay_ref[...].astype(BF).reshape(8, 4, 2, STEP, COLS)
    stage_copy(step).start()

    @pl.when(step == ROWS // STEP - 1)
    def _():
        for k in range(ROWS // STEP):
            cell_copy(k).wait()
            stage_copy(k).wait()


FACTORS_VMEM = 60


def factors(pair, gain, shift, weight, bias):
    whole = lambda *shape: pl.BlockSpec(shape, lambda s: (0,) * len(shape))
    steps = ROWS // STEP
    return pl.pallas_call(
        factor_kernel,
        grid=(steps,),
        out_shape=jax.ShapeDtypeStruct((8, 2, 4, 2, 2, ROWS, COLS), BF),
        in_specs=[
            pl.BlockSpec((STEP, COLS, CH), lambda s: (s, 0, 0)),
            whole(1, CH),
            whole(1, CH),
            whole(CH, 4 * HID + CH),
            whole(4 * HID + CH),
        ],
        out_specs=pl.BlockSpec(memory_space=pl.ANY),
        scratch_shapes=[
            pltpu.VMEM((HID * STEP, COLS), F32),
            pltpu.VMEM((steps, 8, 2, 4, 2, STEP, COLS), BF),
            pltpu.VMEM((steps, 2, 2, 4, 2, ROWS, COLS), BF),
            pltpu.SemaphoreType.DMA((steps,)),
            pltpu.SemaphoreType.DMA((steps,)),
        ],
        compiler_params=pltpu.CompilerParams(vmem_limit_bytes=FACTORS_VMEM * MIB),
        name="factors",
    )(pair, gain, shift, weight, bias)


REGROUP_VMEM = 16
PLANE_VMEM = 16
PRODUCT_VMEM = 62
PIECES = 4


def regroup_kernel(received_ref, out_ref, cells_ref, in_sems, out_sems):
    inward = [
        [
            pltpu.make_async_copy(
                received_ref.at[col, e, :, 1, side * 32 : side * 32 + 32, :],
                cells_ref.at[:, side, col, e * 32 : e * 32 + 32, :],
                in_sems.at[col, e, side],
            )
            for e in range(2)
            for side in range(2)
        ]
        for col in range(NC)
    ]
    for copies in inward:
        for copy in copies:
            copy.start()
    outward = []
    width = NC // PIECES
    for piece in range(PIECES):
        part = slice(piece * width, (piece + 1) * width)
        for copies in inward[part]:
            for copy in copies:
                copy.wait()
        copy = pltpu.make_async_copy(
            cells_ref.at[:, :, part], out_ref.at[:, :, part], out_sems.at[piece]
        )
        copy.start()
        outward.append(copy)
    for copy in outward:
        copy.wait()


def regroup(received):
    anywhere = pl.BlockSpec(memory_space=pl.ANY)
    half = NR // 2
    return pl.pallas_call(
        regroup_kernel,
        out_shape=jax.ShapeDtypeStruct((half, 2, NC, ROWS, COLS), BF),
        in_specs=[anywhere],
        out_specs=anywhere,
        scratch_shapes=[
            pltpu.VMEM((half, 2, NC, ROWS, COLS), BF),
            pltpu.SemaphoreType.DMA((NC, 2, 2)),
            pltpu.SemaphoreType.DMA((PIECES,)),
        ],
        compiler_params=pltpu.CompilerParams(vmem_limit_bytes=REGROUP_VMEM * MIB),
        name="regroup",
    )(received)


def plane_kernel(received_ref, out_ref, hold_ref, in_sems, out_sems):
    inward = [
        pltpu.make_async_copy(
            received_ref.at[2 * k : 2 * k + 2, :, :, 0], hold_ref.at[2 * k : 2 * k + 2], in_sems.at[k]
        )
        for k in range(4)
    ]
    outward = [
        pltpu.make_async_copy(
            hold_ref.at[2 * k : 2 * k + 2], out_ref.at[2 * k : 2 * k + 2], out_sems.at[k]
        )
        for k in range(4)
    ]
    for copy in inward:
        copy.start()
    for k in range(4):
        inward[k].wait()
        outward[k].start()
    for copy in outward:
        copy.wait()


def plane(received):
    anywhere = pl.BlockSpec(memory_space=pl.ANY)
    half = NR // 2
    return pl.pallas_call(
        plane_kernel,
        out_shape=jax.ShapeDtypeStruct((half, 2, NC, ROWS, COLS), BF),
        in_specs=[anywhere],
        out_specs=anywhere,
        scratch_shapes=[
            pltpu.VMEM((half, 2, NC, ROWS, COLS), BF),
            pltpu.SemaphoreType.DMA((4,)),
            pltpu.SemaphoreType.DMA((4,)),
        ],
        compiler_params=pltpu.CompilerParams(vmem_limit_bytes=PLANE_VMEM * MIB),
        cost_estimate=pl.CostEstimate(flops=0, bytes_accessed=4 * MIB, transcendentals=0),
        name="plane",
    )(received)


def product_kernel(
    own_ref, other_ref, out_ref, lhs_ref, rhs_ref, result_ref, lhs_sems, rhs_sems, out_sems
):
    half = NR // 2

    def columns(col):
        return slice(col * COLS, (col + 1) * COLS)

    lhs = [
        pltpu.make_async_copy(
            own_ref.at[:, side, col], lhs_ref.at[side, :, :, columns(col)], lhs_sems.at[side, col]
        )
        for side in range(2)
        for col in range(NC)
    ]
    rhs = [
        pltpu.make_async_copy(
            other_ref.at[:, :, col], rhs_ref.at[:, :, :, columns(col)], rhs_sems.at[col]
        )
        for col in range(NC)
    ]
    for copy in rhs + lhs:
        copy.start()
    for copy in rhs:
        copy.wait()
    outs = []
    for side in range(2):
        for copy in lhs[side * NC : side * NC + NC]:
            copy.wait()
        own = lhs_ref[side].reshape(half * ROWS, NC * COLS)
        for block in range(4):
            result = lax.dot_general(
                own,
                rhs_ref[2 * block : 2 * block + 2].reshape(4 * ROWS, NC * COLS),
                NT,
                preferred_element_type=F32,
            ).astype(BF)
            for col in range(2):
                result_ref[side, :, block * 2 + col] = result[:, columns(col)].reshape(
                    half, ROWS, COLS
                )
        copy = pltpu.make_async_copy(
            result_ref.at[side], out_ref.at[:, side], out_sems.at[side]
        )
        copy.start()
        outs.append(copy)
    for copy in outs:
        copy.wait()


def product(own, other):
    anywhere = pl.BlockSpec(memory_space=pl.ANY)
    half = NR // 2
    return pl.pallas_call(
        product_kernel,
        out_shape=jax.ShapeDtypeStruct((half, 2, NC, ROWS, COLS), BF),
        in_specs=[anywhere, anywhere],
        out_specs=anywhere,
        scratch_shapes=[
            pltpu.VMEM((2, half, ROWS, NC * COLS), BF),
            pltpu.VMEM((half, 2, ROWS, NC * COLS), BF),
            pltpu.VMEM((2, half, NC, ROWS, COLS), BF),
            pltpu.SemaphoreType.DMA((2, NC)),
            pltpu.SemaphoreType.DMA((NC,)),
            pltpu.SemaphoreType.DMA((2,)),
        ],
        compiler_params=pltpu.CompilerParams(vmem_limit_bytes=PRODUCT_VMEM * MIB),
        cost_estimate=pl.CostEstimate(
            flops=2 * 1024**3, bytes_accessed=6 * MIB, transcendentals=0
        ),
        name="product",
    )(own, other)


def gate_kernel(pair_ref, gain_ref, shift_ref, weight_ref, bias_ref, out_ref):
    cells = pair_ref[...].astype(F32).reshape(STEP * COLS, CH)
    normed = normalize(cells, gain_ref[...], shift_ref[...]).astype(BF)
    gate = jnp.dot(normed, weight_ref[...], preferred_element_type=F32) + bias_ref[...]
    out_ref[...] = sigmoid(gate).astype(BF).reshape(STEP, COLS, CH)


def gates(pair, gain, shift, weight, bias):
    whole = lambda *shape: pl.BlockSpec(shape, lambda s: (0,) * len(shape))
    block = pl.BlockSpec((STEP, COLS, CH), lambda s: (s, 0, 0))
    return pl.pallas_call(
        gate_kernel,
        grid=(ROWS // STEP,),
        out_shape=jax.ShapeDtypeStruct((ROWS, COLS, CH), BF),
        in_specs=[block, whole(1, CH), whole(1, CH), whole(CH, CH), whole(1, CH)],
        out_specs=block,
        compiler_params=pltpu.CompilerParams(vmem_limit_bytes=24 * MIB),
        cost_estimate=pl.CostEstimate(
            flops=2 * ROWS * COLS * CH * CH, bytes_accessed=4 * ROWS * COLS * CH, transcendentals=ROWS * COLS * CH
        ),
        name="gates",
    )(pair, gain, shift, weight, bias)


PITCH = 24
MGROUP = 8


def mirror_kernel(
    mirror_ref, gain_ref, shift_ref, weight_ref, bias_ref, out_ref, gate_ref, cells_ref
):
    for e in range(2):
        for j in range(64):
            at = (e * 64 + j) * PITCH
            cells_ref[at : at + STEP, :] = mirror_ref[j, 0, e, 0].astype(F32)
    for part in range(STEP // MGROUP):
        rows = [
            cells_ref[pl.ds(part * MGROUP + k, COLS, stride=PITCH), :] for k in range(MGROUP)
        ]
        cells = jnp.concatenate(rows, axis=0)
        here = slice(part * MGROUP, (part + 1) * MGROUP)
        out_ref[here] = cells.astype(BF).reshape(MGROUP, COLS, CH)
        normed = normalize(cells, gain_ref[...], shift_ref[...]).astype(BF)
        gate = jnp.dot(normed, weight_ref[...], preferred_element_type=F32) + bias_ref[...]
        gate_ref[here] = sigmoid(gate).astype(BF).reshape(MGROUP, COLS, CH)


def mirror_gates(mirrored, gain, shift, weight, bias):
    whole = lambda *shape: pl.BlockSpec(shape, lambda s: (0,) * len(shape))
    block = pl.BlockSpec((STEP, COLS, CH), lambda s: (s, 0, 0))
    return pl.pallas_call(
        mirror_kernel,
        grid=(ROWS // STEP,),
        out_shape=[
            jax.ShapeDtypeStruct((ROWS, COLS, CH), BF),
            jax.ShapeDtypeStruct((ROWS, COLS, CH), BF),
        ],
        in_specs=[
            pl.BlockSpec((64, 1, 2, 1, STEP, CH), lambda s: (0, s // 2, 0, s % 2, 0, 0)),
            whole(1, CH),
            whole(1, CH),
            whole(CH, CH),
            whole(1, CH),
        ],
        out_specs=[block, block],
        scratch_shapes=[pltpu.VMEM((COLS * PITCH, CH), F32)],
        compiler_params=pltpu.CompilerParams(vmem_limit_bytes=24 * MIB),
        cost_estimate=pl.CostEstimate(
            flops=2 * ROWS * COLS * CH * CH, bytes_accessed=8 * ROWS * COLS * CH, transcendentals=ROWS * COLS * CH
        ),
        name="mirror_gates",
    )(mirrored.reshape(64, 2, 2, 2, STEP, CH), gain, shift, weight, bias)


USTEP = 16
UNROLL_U = 1
UGROUP = 16
UPDATE_VMEM = 50


def update_kernel(
    pair_ref, own_gate_ref, cells_ref, gate_ref, tri_ref, out_weight_ref, out_bias_ref, sym_ref,
    lay_ref,
):
    tri = tri_ref[...].astype(F32)
    mean = jnp.mean(tri, axis=(0, 2), keepdims=True)
    centred = tri - mean
    spread = jnp.mean(centred * centred, axis=(0, 2), keepdims=True)
    lay_ref[...] = (centred * lax.rsqrt(spread + EPS)).reshape(2 * HID * USTEP, COLS)
    size = UGROUP * COLS

    def rows(ref, first):
        return ref[pl.ds(first, UGROUP)].astype(F32).reshape(size, CH)

    def body(part, carry):
        first = part * UGROUP
        change = [
            lax.dot_general(
                lay_ref[pl.ds(first + k, 2 * HID, stride=USTEP), :].astype(BF),
                out_weight_ref[...],
                TN,
                preferred_element_type=F32,
            )
            for k in range(UGROUP)
        ]
        change = jnp.concatenate(change, axis=0) + out_bias_ref[...]
        own = rows(pair_ref, first) + rows(own_gate_ref, first) * change[:, :CH]
        mirrored = rows(cells_ref, first) + rows(gate_ref, first) * change[:, CH:]
        total = own.astype(BF).astype(F32) + mirrored.astype(BF).astype(F32)
        sym_ref[pl.ds(first, UGROUP)] = (total * 0.5).astype(BF).reshape(UGROUP, COLS, CH)
        return carry

    lax.fori_loop(0, USTEP // UGROUP, body, 0, unroll=UNROLL_U)


def update(pair, own_gate, cells, gate, returned, out_weight, out_bias):
    whole = lambda *shape: pl.BlockSpec(shape, lambda s: (0,) * len(shape))
    block = pl.BlockSpec((USTEP, COLS, CH), lambda s: (s, 0, 0))
    return pl.pallas_call(
        update_kernel,
        grid=(ROWS // USTEP,),
        out_shape=jax.ShapeDtypeStruct((ROWS, COLS, CH), BF),
        in_specs=[
            block,
            block,
            block,
            block,
            pl.BlockSpec((8, 2, 8, USTEP, COLS), lambda s: (0, 0, 0, s, 0)),
            whole(2 * HID, 2 * CH),
            whole(1, 2 * CH),
        ],
        out_specs=block,
        scratch_shapes=[pltpu.VMEM((2 * HID * USTEP, COLS), F32)],
        compiler_params=pltpu.CompilerParams(vmem_limit_bytes=UPDATE_VMEM * MIB),
        name="update",
    )(pair, own_gate, cells, gate, returned.reshape(8, 2, 8, ROWS, COLS), out_weight, out_bias)


def output_weight(weight, bias, gain, shift):
    scaled = (gain[:, None] * weight.astype(F32)).astype(BF).reshape(8, 1, 8, CH)
    nothing = jnp.zeros_like(scaled)
    own = jnp.concatenate([scaled, nothing], axis=1)
    mirrored = jnp.concatenate([nothing, scaled], axis=1)
    full = jnp.concatenate([own, mirrored], axis=3).reshape(2 * HID, 2 * CH)
    offset = bias + jnp.sum(shift[:, None] * weight.astype(F32), axis=0)
    return full, jnp.concatenate([offset, offset])[None]


def activation_kernel(sym_ref, gain_ref, shift_ref, out_ref):
    cells = sym_ref[...].astype(F32).reshape(STEP * COLS, CH)
    act = jnp.maximum(normalize(cells, gain_ref[0:1], shift_ref[0:1]), 0.0)
    out_ref[...] = act.astype(BF).reshape(STEP, COLS, CH)


def activations(sym, gain, shift):
    whole = lambda *shape: pl.BlockSpec(shape, lambda s: (0,) * len(shape))
    block = pl.BlockSpec((STEP, COLS, CH), lambda s: (s, 0, 0))
    return pl.pallas_call(
        activation_kernel,
        grid=(ROWS // STEP,),
        out_shape=jax.ShapeDtypeStruct((ROWS, COLS, CH), BF),
        in_specs=[block, whole(2, CH), whole(2, CH)],
        out_specs=block,
        compiler_params=pltpu.CompilerParams(vmem_limit_bytes=24 * MIB),
        cost_estimate=pl.CostEstimate(
            flops=16 * ROWS * COLS * CH, bytes_accessed=4 * ROWS * COLS * CH, transcendentals=ROWS * COLS
        ),
        name="activations",
    )(sym, gain, shift)


TALL = ROWS + 2 * HALO
SIDE = 8
WIDE = COLS + 4 * SIDE
FIRST_TALL = ROWS + 2 * SECOND_DILATION
FIRST_WIDE = COLS + 2 * SIDE
GROUP_B, GROUP_C = 4, 8
INNER_B, SLOTS_C = 18, 4
CONV_VMEM = 40


def convolution_kernel(
    place_ref, sym_ref, act_ref, top_ref, bottom_ref, low_ref, high_ref, gain_ref, shift_ref,
    bias_ref, weight_hbm, out_hbm, tall_ref, wide_ref, first_ref, second_ref, shifted_ref,
    late_ref, weight_ref, out_ref, sems, out_sems,
):
    top_copy = pltpu.make_async_copy(top_ref, tall_ref.at[0:HALO], sems.at[0])
    bottom_copy = pltpu.make_async_copy(bottom_ref, tall_ref.at[HALO + ROWS : TALL], sems.at[1])
    act_copy = pltpu.make_async_copy(
        act_ref, wide_ref.at[HALO : HALO + ROWS, 16 : 16 + COLS], sems.at[2]
    )
    weight_copy = pltpu.make_async_copy(weight_hbm, weight_ref, sems.at[3])
    sym_copy = pltpu.make_async_copy(sym_ref, tall_ref.at[HALO : HALO + ROWS], sems.at[4])
    for copy in (top_copy, bottom_copy, act_copy, weight_copy, sym_copy):
        copy.start()
    above = place_ref[0] > 0
    below = place_ref[0] < (NR - 1) * ROWS
    low_ok = (place_ref[1] > 0).astype(F32)
    high_ok = (place_ref[1] < (NC - 1) * COLS).astype(F32)

    def activate(cells, which):
        return jnp.maximum(
            normalize(
                cells,
                gain_ref[which : which + 1].reshape(1, 1, CH),
                shift_ref[which : which + 1].reshape(1, 1, CH),
            ),
            0.0,
        )

    nothing = jnp.zeros((TALL, SIDE, CH), F32)
    low = activate(low_ref[...].astype(F32), 0) * low_ok
    wide_ref[:, 0:16, :] = jnp.concatenate([nothing, low], axis=1).astype(BF)
    high = activate(high_ref[...].astype(F32), 0) * high_ok
    wide_ref[:, 16 + COLS :, :] = jnp.concatenate([high, nothing], axis=1).astype(BF)
    top_copy.wait()
    bottom_copy.wait()
    wide_ref[0:HALO, 16 : 16 + COLS, :] = activate(tall_ref[0:HALO].astype(F32), 0).astype(BF)
    wide_ref[HALO + ROWS :, 16 : 16 + COLS, :] = activate(
        tall_ref[HALO + ROWS :].astype(F32), 0
    ).astype(BF)

    @pl.when(jnp.logical_not(above))
    def _():
        wide_ref[0:HALO] = jnp.zeros((HALO, WIDE, CH), BF)

    @pl.when(jnp.logical_not(below))
    def _():
        wide_ref[HALO + ROWS :] = jnp.zeros((HALO, WIDE, CH), BF)

    def paired(source_ref, at, spacing, group, width, which):
        sets = group // (2 * spacing)
        lhs = jnp.concatenate(
            [
                jnp.concatenate(
                    [
                        source_ref[pl.ds(at + 2 * spacing * k + spacing * slot, spacing)]
                        for k in range(sets)
                    ],
                    axis=0,
                ).reshape(group // 2 * width, CH)
                for slot in range(4)
            ],
            axis=1,
        )
        total = jnp.dot(lhs, weight_ref[which], preferred_element_type=F32)
        taps = []
        for tap in range(3):
            near = total[:, tap * CH : (tap + 1) * CH].reshape(sets, spacing, width, CH)
            far = total[:, (3 + tap) * CH : (4 + tap) * CH].reshape(sets, spacing, width, CH)
            taps.append(jnp.concatenate([near, far], axis=1).reshape(group, width, CH))
        return taps

    def first_rows(at, slot):
        before, centre, after = paired(wide_ref, at, FIRST_DILATION, GROUP_B, WIDE, 0)
        shifted_ref[slot, 0] = before
        shifted_ref[slot, 1] = after
        residual = jnp.concatenate(
            [
                low_ref[pl.ds(at + 2, GROUP_B)].astype(F32),
                tall_ref[pl.ds(at + 2, GROUP_B)].astype(F32),
                high_ref[pl.ds(at + 2, GROUP_B)].astype(F32),
            ],
            axis=1,
        )
        first = (
            centre[:, 8 : 8 + FIRST_WIDE]
            + shifted_ref[slot, 0, :, 6 : 6 + FIRST_WIDE, :]
            + shifted_ref[slot, 1, :, 10 : 10 + FIRST_WIDE, :]
            + residual
            + bias_ref[0:1].reshape(1, 1, CH)
        )
        first_ref[pl.ds(at, GROUP_B)] = first[:, SIDE : SIDE + COLS]
        act = activate(first, 1)
        second_ref[pl.ds(at, GROUP_B)] = jnp.concatenate(
            [
                act[:, :SIDE] * low_ok,
                act[:, SIDE : SIDE + COLS],
                act[:, SIDE + COLS :] * high_ok,
            ],
            axis=1,
        ).astype(BF)

    def convolve_first(step, carry):
        for k in range(INNER_B):
            first_rows(step * (GROUP_B * INNER_B) + k * GROUP_B, k)
        return carry

    act_copy.wait()
    weight_copy.wait()
    sym_copy.wait()
    lax.fori_loop(0, FIRST_TALL // (GROUP_B * INNER_B), convolve_first, 0)

    @pl.when(jnp.logical_not(above))
    def _():
        second_ref[0:SECOND_DILATION] = jnp.zeros((SECOND_DILATION, FIRST_WIDE, CH), BF)

    @pl.when(jnp.logical_not(below))
    def _():
        second_ref[SECOND_DILATION + ROWS :] = jnp.zeros((SECOND_DILATION, FIRST_WIDE, CH), BF)

    def out_copy(k):
        return pltpu.make_async_copy(
            out_ref.at[16 * k : 16 * k + 16], out_hbm.at[16 * k : 16 * k + 16], out_sems.at[k]
        )

    for k in range(4):
        for part in range(16 // GROUP_C):
            at = 16 * k + part * GROUP_C
            slot = at // GROUP_C % SLOTS_C
            before, centre, after = paired(
                second_ref, at, SECOND_DILATION, GROUP_C, FIRST_WIDE, 1
            )
            late_ref[slot, 0] = before
            late_ref[slot, 1] = after
            out_ref[at : at + GROUP_C] = (
                centre[:, SIDE : SIDE + COLS]
                + late_ref[slot, 0, :, 4 : 4 + COLS, :]
                + late_ref[slot, 1, :, 12 : 12 + COLS, :]
                + first_ref[at + 4 : at + 4 + GROUP_C]
                + bias_ref[1:2].reshape(1, 1, CH)
            ).astype(BF)
        out_copy(k).start()
    for k in range(4):
        out_copy(k).wait()


def convolutions(place, sym, act, top, bottom, low, high, gain, shift, bias, weight):
    vmem = pl.BlockSpec(memory_space=pltpu.VMEM)
    anywhere = pl.BlockSpec(memory_space=pl.ANY)
    return pl.pallas_call(
        convolution_kernel,
        out_shape=jax.ShapeDtypeStruct((ROWS, COLS, CH), BF),
        in_specs=[pl.BlockSpec(memory_space=pltpu.SMEM)]
        + [anywhere] * 4
        + [vmem] * 5
        + [anywhere],
        out_specs=anywhere,
        scratch_shapes=[
            pltpu.VMEM((TALL, COLS, CH), BF),
            pltpu.VMEM((TALL, WIDE, CH), BF),
            pltpu.VMEM((FIRST_TALL, COLS, CH), F32),
            pltpu.VMEM((FIRST_TALL, FIRST_WIDE, CH), BF),
            pltpu.VMEM((INNER_B, 2, GROUP_B, WIDE, CH), F32),
            pltpu.VMEM((SLOTS_C, 2, GROUP_C, FIRST_WIDE, CH), F32),
            pltpu.VMEM((2, 4 * CH, 6 * CH), BF),
            pltpu.VMEM((ROWS, COLS, CH), BF),
            pltpu.SemaphoreType.DMA((5,)),
            pltpu.SemaphoreType.DMA((4,)),
        ],
        compiler_params=pltpu.CompilerParams(vmem_limit_bytes=CONV_VMEM * MIB),
        name="convolutions",
    )(place, sym, act, top, bottom, low, high, gain, shift, bias, weight)


def paired_weight(weight):
    taps = jnp.transpose(weight.reshape(3, 3, CH, CH), (0, 2, 1, 3)).reshape(3, CH, 3 * CH)
    near = jnp.concatenate([taps, jnp.zeros_like(taps[:1])], axis=0)
    far = jnp.concatenate([jnp.zeros_like(taps[:1]), taps], axis=0)
    return jnp.concatenate([near, far], axis=2).reshape(4 * CH, 6 * CH)


def neighbours(low_strip, high_strip, axis):
    count = lax.axis_size(axis)
    forward = [(i, i + 1) for i in range(count - 1)]
    backward = [(i + 1, i) for i in range(count - 1)]
    return lax.ppermute(high_strip, axis, forward), lax.ppermute(low_strip, axis, backward)


def local(
    pair, norm_gain, norm_shift, proj_weight, proj_bias, mid_gain, mid_shift, out_weight, out_bias,
    conv_gain, conv_shift, convolution_weight, convolution_bias,
):
    gain, shift = norm_gain[None], norm_shift[None]
    sent = factors(pair, gain, shift, proj_weight, proj_bias)
    exchange = lambda v: lax.all_to_all(
        v, ("row", "col"), split_axis=0, concat_axis=0, tiled=True
    )
    received = exchange(sent.reshape(128, 2, ROWS, COLS))
    received = received.reshape(NR // 2, 2, NC, 2, ROWS, COLS)
    cells = regroup(received)
    mirrored = exchange(cells.reshape(128, ROWS, COLS))
    own = plane(lax.optimization_barrier((received, cells))[0])
    other = lax.ppermute(own, "row", [(i, i ^ 1) for i in range(NR)])
    returned = exchange(product(own, other).reshape(128, ROWS, COLS))
    gate, gate_bias = proj_weight[:, 4 * HID :], proj_bias[None, 4 * HID :]
    paired = jnp.stack([paired_weight(convolution_weight[0]), paired_weight(convolution_weight[1])])
    gate, paired = lax.optimization_barrier((gate, paired))
    sym = update(
        pair,
        gates(pair, gain, shift, gate, gate_bias),
        *mirror_gates(mirrored, gain, shift, gate, gate_bias),
        returned,
        *output_weight(out_weight, out_bias, mid_gain, mid_shift),
    )
    top, bottom = neighbours(sym[:HALO], sym[ROWS - HALO :], "row")
    edge = lambda low, high: jnp.concatenate(
        [top[:, low:high], sym[:, low:high], bottom[:, low:high]], axis=0
    )
    low, high = neighbours(edge(0, SIDE), edge(COLS - SIDE, COLS), "col")
    place = jnp.stack([lax.axis_index("row") * ROWS, lax.axis_index("col") * COLS]).astype(jnp.int32)
    return convolutions(
        place, sym, activations(sym, conv_gain, conv_shift), top, bottom, low, high, conv_gain, conv_shift, convolution_bias,
        paired,
    )


def solution(mesh):
    return jax.shard_map(
        local,
        mesh=mesh,
        in_specs=(P("row", "col", None),) + (P(),) * 12,
        out_specs=P("row", "col", None),
        check_vma=False,
    )
```

```python
import jax
import jax.numpy as jnp
from jax import lax
from jax.experimental import pallas as pl
from jax.experimental.pallas import tpu as pltpu
from jax.sharding import PartitionSpec as P

FIRST_DILATION = 2
SECOND_DILATION = 4
HALO = FIRST_DILATION + SECOND_DILATION
EPS = 1e-05
BF = jnp.bfloat16
F32 = jnp.float32
MIB = 1 << 20
ROWS, COLS, CH, HID = 64, 128, 128, 64
NR, NC = 16, 8


def sigmoid(x):
    return 0.5 * jnp.tanh(0.5 * x) + 0.5


def normalize(values, gain, shift):
    mean = jnp.mean(values, axis=-1, keepdims=True)
    centred = values - mean
    spread = jnp.mean(centred * centred, axis=-1, keepdims=True)
    return centred * lax.rsqrt(spread + EPS) * gain + shift


NT = (((1,), (1,)), ((), ()))
TN = (((0,), (0,)), ((), ()))

STEP = 16


def factor_kernel(
    pair_ref, gain_ref, shift_ref, weight_ref, bias_ref, out_ref, lay_ref, stage_ref, cells_ref,
    cell_sems, stage_sems,
):
    step = pl.program_id(0)

    def cell_copy(k):
        return pltpu.make_async_copy(
            cells_ref.at[k], out_ref.at[pl.ds(2 * k, 2), :, :, :, 1], cell_sems.at[k]
        )

    def stage_copy(k):
        start = pl.multiple_of(k * STEP, STEP)
        return pltpu.make_async_copy(
            stage_ref.at[k], out_ref.at[:, :, :, :, 0, pl.ds(start, STEP), :], stage_sems.at[k]
        )

    for row in range(STEP):
        for q in range(2):
            for half in range(2):
                start = half * 64 + q * 32
                cells_ref[
                    step, row // 8, (row // 4) % 2, row % 4, q, half * 32 : half * 32 + 32, :
                ] = pair_ref[row, start : start + 32, :]
    cell_copy(step).start()
    cells = pair_ref[...].astype(F32).reshape(STEP * COLS, CH)
    normed = normalize(cells, gain_ref[...], shift_ref[...]).astype(BF)
    bias = jnp.transpose(jnp.broadcast_to(bias_ref[...][None], (COLS, 4 * HID + CH))[:, : 4 * HID])
    projected = lax.dot_general(
        weight_ref[:, : 4 * HID], normed, (((0,), (1,)), ((), ())), preferred_element_type=F32
    )
    for side in range(2):
        base = 2 * HID * side
        for row in range(STEP):
            part = slice(row * COLS, (row + 1) * COLS)
            gate = projected[base : base + HID, part] + bias[base : base + HID]
            value = projected[base + HID : base + 2 * HID, part] + bias[base + HID : base + 2 * HID]
            lay_ref[pl.ds(row, HID, stride=STEP), :] = sigmoid(gate) * value
        stage_ref[step, :, side] = lay_ref[...].astype(BF).reshape(8, 4, 2, STEP, COLS)
    stage_copy(step).start()

    @pl.when(step == ROWS // STEP - 1)
    def _():
        for k in range(ROWS // STEP):
            cell_copy(k).wait()
            stage_copy(k).wait()


FACTORS_VMEM = 60


def factors(pair, gain, shift, weight, bias):
    whole = lambda *shape: pl.BlockSpec(shape, lambda s: (0,) * len(shape))
    steps = ROWS // STEP
    return pl.pallas_call(
        factor_kernel,
        grid=(steps,),
        out_shape=jax.ShapeDtypeStruct((8, 2, 4, 2, 2, ROWS, COLS), BF),
        in_specs=[
            pl.BlockSpec((STEP, COLS, CH), lambda s: (s, 0, 0)),
            whole(1, CH),
            whole(1, CH),
            whole(CH, 4 * HID + CH),
            whole(4 * HID + CH),
        ],
        out_specs=pl.BlockSpec(memory_space=pl.ANY),
        scratch_shapes=[
            pltpu.VMEM((HID * STEP, COLS), F32),
            pltpu.VMEM((steps, 8, 2, 4, 2, STEP, COLS), BF),
            pltpu.VMEM((steps, 2, 2, 4, 2, ROWS, COLS), BF),
            pltpu.SemaphoreType.DMA((steps,)),
            pltpu.SemaphoreType.DMA((steps,)),
        ],
        compiler_params=pltpu.CompilerParams(vmem_limit_bytes=FACTORS_VMEM * MIB),
        name="factors",
    )(pair, gain, shift, weight, bias)


REGROUP_VMEM = 16
PLANE_VMEM = 16
PRODUCT_VMEM = 62
PIECES = 4


def regroup_kernel(received_ref, out_ref, cells_ref, in_sems, out_sems):
    inward = [
        [
            pltpu.make_async_copy(
                received_ref.at[col, e, :, 1, side * 32 : side * 32 + 32, :],
                cells_ref.at[:, side, col, e * 32 : e * 32 + 32, :],
                in_sems.at[col, e, side],
            )
            for e in range(2)
            for side in range(2)
        ]
        for col in range(NC)
    ]
    for copies in inward:
        for copy in copies:
            copy.start()
    outward = []
    width = NC // PIECES
    for piece in range(PIECES):
        part = slice(piece * width, (piece + 1) * width)
        for copies in inward[part]:
            for copy in copies:
                copy.wait()
        copy = pltpu.make_async_copy(
            cells_ref.at[:, :, part], out_ref.at[:, :, part], out_sems.at[piece]
        )
        copy.start()
        outward.append(copy)
    for copy in outward:
        copy.wait()


def regroup(received):
    anywhere = pl.BlockSpec(memory_space=pl.ANY)
    half = NR // 2
    return pl.pallas_call(
        regroup_kernel,
        out_shape=jax.ShapeDtypeStruct((half, 2, NC, ROWS, COLS), BF),
        in_specs=[anywhere],
        out_specs=anywhere,
        scratch_shapes=[
            pltpu.VMEM((half, 2, NC, ROWS, COLS), BF),
            pltpu.SemaphoreType.DMA((NC, 2, 2)),
            pltpu.SemaphoreType.DMA((PIECES,)),
        ],
        compiler_params=pltpu.CompilerParams(vmem_limit_bytes=REGROUP_VMEM * MIB),
        name="regroup",
    )(received)


def plane_kernel(received_ref, out_ref, hold_ref, in_sems, out_sems):
    inward = [
        pltpu.make_async_copy(
            received_ref.at[2 * k : 2 * k + 2, :, :, 0], hold_ref.at[2 * k : 2 * k + 2], in_sems.at[k]
        )
        for k in range(4)
    ]
    outward = [
        pltpu.make_async_copy(
            hold_ref.at[2 * k : 2 * k + 2], out_ref.at[2 * k : 2 * k + 2], out_sems.at[k]
        )
        for k in range(4)
    ]
    for copy in inward:
        copy.start()
    for k in range(4):
        inward[k].wait()
        outward[k].start()
    for copy in outward:
        copy.wait()


def plane(received):
    anywhere = pl.BlockSpec(memory_space=pl.ANY)
    half = NR // 2
    return pl.pallas_call(
        plane_kernel,
        out_shape=jax.ShapeDtypeStruct((half, 2, NC, ROWS, COLS), BF),
        in_specs=[anywhere],
        out_specs=anywhere,
        scratch_shapes=[
            pltpu.VMEM((half, 2, NC, ROWS, COLS), BF),
            pltpu.SemaphoreType.DMA((4,)),
            pltpu.SemaphoreType.DMA((4,)),
        ],
        compiler_params=pltpu.CompilerParams(vmem_limit_bytes=PLANE_VMEM * MIB),
        cost_estimate=pl.CostEstimate(flops=0, bytes_accessed=4 * MIB, transcendentals=0),
        name="plane",
    )(received)


def product_kernel(
    own_ref, other_ref, out_ref, lhs_ref, rhs_ref, result_ref, lhs_sems, rhs_sems, out_sems
):
    half = NR // 2

    def columns(col):
        return slice(col * COLS, (col + 1) * COLS)

    lhs = [
        pltpu.make_async_copy(
            own_ref.at[:, side, col], lhs_ref.at[side, :, :, columns(col)], lhs_sems.at[side, col]
        )
        for side in range(2)
        for col in range(NC)
    ]
    rhs = [
        pltpu.make_async_copy(
            other_ref.at[:, :, col], rhs_ref.at[:, :, :, columns(col)], rhs_sems.at[col]
        )
        for col in range(NC)
    ]
    for copy in rhs + lhs:
        copy.start()
    for copy in rhs:
        copy.wait()
    outs = []
    for side in range(2):
        for copy in lhs[side * NC : side * NC + NC]:
            copy.wait()
        own = lhs_ref[side].reshape(half * ROWS, NC * COLS)
        for block in range(4):
            result = lax.dot_general(
                own,
                rhs_ref[2 * block : 2 * block + 2].reshape(4 * ROWS, NC * COLS),
                NT,
                preferred_element_type=F32,
            ).astype(BF)
            for col in range(2):
                result_ref[side, :, block * 2 + col] = result[:, columns(col)].reshape(
                    half, ROWS, COLS
                )
        copy = pltpu.make_async_copy(
            result_ref.at[side], out_ref.at[:, side], out_sems.at[side]
        )
        copy.start()
        outs.append(copy)
    for copy in outs:
        copy.wait()


def product(own, other):
    anywhere = pl.BlockSpec(memory_space=pl.ANY)
    half = NR // 2
    return pl.pallas_call(
        product_kernel,
        out_shape=jax.ShapeDtypeStruct((half, 2, NC, ROWS, COLS), BF),
        in_specs=[anywhere, anywhere],
        out_specs=anywhere,
        scratch_shapes=[
            pltpu.VMEM((2, half, ROWS, NC * COLS), BF),
            pltpu.VMEM((half, 2, ROWS, NC * COLS), BF),
            pltpu.VMEM((2, half, NC, ROWS, COLS), BF),
            pltpu.SemaphoreType.DMA((2, NC)),
            pltpu.SemaphoreType.DMA((NC,)),
            pltpu.SemaphoreType.DMA((2,)),
        ],
        compiler_params=pltpu.CompilerParams(vmem_limit_bytes=PRODUCT_VMEM * MIB),
        cost_estimate=pl.CostEstimate(
            flops=2 * 1024**3, bytes_accessed=6 * MIB, transcendentals=0
        ),
        name="product",
    )(own, other)


def gate_kernel(pair_ref, gain_ref, shift_ref, weight_ref, bias_ref, out_ref):
    cells = pair_ref[...].astype(F32).reshape(STEP * COLS, CH)
    normed = normalize(cells, gain_ref[...], shift_ref[...]).astype(BF)
    gate = jnp.dot(normed, weight_ref[...], preferred_element_type=F32) + bias_ref[...]
    out_ref[...] = sigmoid(gate).astype(BF).reshape(STEP, COLS, CH)


def gates(pair, gain, shift, weight, bias):
    whole = lambda *shape: pl.BlockSpec(shape, lambda s: (0,) * len(shape))
    block = pl.BlockSpec((STEP, COLS, CH), lambda s: (s, 0, 0))
    return pl.pallas_call(
        gate_kernel,
        grid=(ROWS // STEP,),
        out_shape=jax.ShapeDtypeStruct((ROWS, COLS, CH), BF),
        in_specs=[block, whole(1, CH), whole(1, CH), whole(CH, CH), whole(1, CH)],
        out_specs=block,
        compiler_params=pltpu.CompilerParams(vmem_limit_bytes=24 * MIB),
        cost_estimate=pl.CostEstimate(
            flops=2 * ROWS * COLS * CH * CH, bytes_accessed=4 * ROWS * COLS * CH, transcendentals=ROWS * COLS * CH
        ),
        name="gates",
    )(pair, gain, shift, weight, bias)


PITCH = 24
MGROUP = 8


def mirror_kernel(
    mirror_ref, gain_ref, shift_ref, weight_ref, bias_ref, out_ref, gate_ref, cells_ref
):
    for e in range(2):
        for j in range(64):
            at = (e * 64 + j) * PITCH
            cells_ref[at : at + STEP, :] = mirror_ref[j, 0, e, 0].astype(F32)
    for part in range(STEP // MGROUP):
        rows = [
            cells_ref[pl.ds(part * MGROUP + k, COLS, stride=PITCH), :] for k in range(MGROUP)
        ]
        cells = jnp.concatenate(rows, axis=0)
        here = slice(part * MGROUP, (part + 1) * MGROUP)
        out_ref[here] = cells.astype(BF).reshape(MGROUP, COLS, CH)
        normed = normalize(cells, gain_ref[...], shift_ref[...]).astype(BF)
        gate = jnp.dot(normed, weight_ref[...], preferred_element_type=F32) + bias_ref[...]
        gate_ref[here] = sigmoid(gate).astype(BF).reshape(MGROUP, COLS, CH)


def mirror_gates(mirrored, gain, shift, weight, bias):
    whole = lambda *shape: pl.BlockSpec(shape, lambda s: (0,) * len(shape))
    block = pl.BlockSpec((STEP, COLS, CH), lambda s: (s, 0, 0))
    return pl.pallas_call(
        mirror_kernel,
        grid=(ROWS // STEP,),
        out_shape=[
            jax.ShapeDtypeStruct((ROWS, COLS, CH), BF),
            jax.ShapeDtypeStruct((ROWS, COLS, CH), BF),
        ],
        in_specs=[
            pl.BlockSpec((64, 1, 2, 1, STEP, CH), lambda s: (0, s // 2, 0, s % 2, 0, 0)),
            whole(1, CH),
            whole(1, CH),
            whole(CH, CH),
            whole(1, CH),
        ],
        out_specs=[block, block],
        scratch_shapes=[pltpu.VMEM((COLS * PITCH, CH), F32)],
        compiler_params=pltpu.CompilerParams(vmem_limit_bytes=24 * MIB),
        cost_estimate=pl.CostEstimate(
            flops=2 * ROWS * COLS * CH * CH, bytes_accessed=8 * ROWS * COLS * CH, transcendentals=ROWS * COLS * CH
        ),
        name="mirror_gates",
    )(mirrored.reshape(64, 2, 2, 2, STEP, CH), gain, shift, weight, bias)


USTEP = 16
UNROLL_U = 1
UGROUP = 16
UPDATE_VMEM = 50


def update_kernel(
    pair_ref, own_gate_ref, cells_ref, gate_ref, tri_ref, out_weight_ref, out_bias_ref, sym_ref,
    lay_ref,
):
    tri = tri_ref[...].astype(F32)
    mean = jnp.mean(tri, axis=(0, 2), keepdims=True)
    centred = tri - mean
    spread = jnp.mean(centred * centred, axis=(0, 2), keepdims=True)
    lay_ref[...] = (centred * lax.rsqrt(spread + EPS)).reshape(2 * HID * USTEP, COLS)
    size = UGROUP * COLS

    def rows(ref, first):
        return ref[pl.ds(first, UGROUP)].astype(F32).reshape(size, CH)

    def body(part, carry):
        first = part * UGROUP
        change = [
            lax.dot_general(
                lay_ref[pl.ds(first + k, 2 * HID, stride=USTEP), :].astype(BF),
                out_weight_ref[...],
                TN,
                preferred_element_type=F32,
            )
            for k in range(UGROUP)
        ]
        change = jnp.concatenate(change, axis=0) + out_bias_ref[...]
        own = rows(pair_ref, first) + rows(own_gate_ref, first) * change[:, :CH]
        mirrored = rows(cells_ref, first) + rows(gate_ref, first) * change[:, CH:]
        total = own.astype(BF).astype(F32) + mirrored.astype(BF).astype(F32)
        sym_ref[pl.ds(first, UGROUP)] = (total * 0.5).astype(BF).reshape(UGROUP, COLS, CH)
        return carry

    lax.fori_loop(0, USTEP // UGROUP, body, 0, unroll=UNROLL_U)


def update(pair, own_gate, cells, gate, returned, out_weight, out_bias):
    whole = lambda *shape: pl.BlockSpec(shape, lambda s: (0,) * len(shape))
    block = pl.BlockSpec((USTEP, COLS, CH), lambda s: (s, 0, 0))
    return pl.pallas_call(
        update_kernel,
        grid=(ROWS // USTEP,),
        out_shape=jax.ShapeDtypeStruct((ROWS, COLS, CH), BF),
        in_specs=[
            block,
            block,
            block,
            block,
            pl.BlockSpec((8, 2, 8, USTEP, COLS), lambda s: (0, 0, 0, s, 0)),
            whole(2 * HID, 2 * CH),
            whole(1, 2 * CH),
        ],
        out_specs=block,
        scratch_shapes=[pltpu.VMEM((2 * HID * USTEP, COLS), F32)],
        compiler_params=pltpu.CompilerParams(vmem_limit_bytes=UPDATE_VMEM * MIB),
        name="update",
    )(pair, own_gate, cells, gate, returned.reshape(8, 2, 8, ROWS, COLS), out_weight, out_bias)


def output_weight(weight, bias, gain, shift):
    scaled = (gain[:, None] * weight.astype(F32)).astype(BF).reshape(8, 1, 8, CH)
    nothing = jnp.zeros_like(scaled)
    own = jnp.concatenate([scaled, nothing], axis=1)
    mirrored = jnp.concatenate([nothing, scaled], axis=1)
    full = jnp.concatenate([own, mirrored], axis=3).reshape(2 * HID, 2 * CH)
    offset = bias + jnp.sum(shift[:, None] * weight.astype(F32), axis=0)
    return full, jnp.concatenate([offset, offset])[None]


def activation_kernel(sym_ref, gain_ref, shift_ref, out_ref):
    cells = sym_ref[...].astype(F32).reshape(STEP * COLS, CH)
    act = jnp.maximum(normalize(cells, gain_ref[0:1], shift_ref[0:1]), 0.0)
    out_ref[...] = act.astype(BF).reshape(STEP, COLS, CH)


def activations(sym, gain, shift):
    whole = lambda *shape: pl.BlockSpec(shape, lambda s: (0,) * len(shape))
    block = pl.BlockSpec((STEP, COLS, CH), lambda s: (s, 0, 0))
    return pl.pallas_call(
        activation_kernel,
        grid=(ROWS // STEP,),
        out_shape=jax.ShapeDtypeStruct((ROWS, COLS, CH), BF),
        in_specs=[block, whole(2, CH), whole(2, CH)],
        out_specs=block,
        compiler_params=pltpu.CompilerParams(vmem_limit_bytes=24 * MIB),
        cost_estimate=pl.CostEstimate(
            flops=16 * ROWS * COLS * CH, bytes_accessed=4 * ROWS * COLS * CH, transcendentals=ROWS * COLS
        ),
        name="activations",
    )(sym, gain, shift)


TALL = ROWS + 2 * HALO
SIDE = 8
WIDE = COLS + 4 * SIDE
FIRST_TALL = ROWS + 2 * SECOND_DILATION
FIRST_WIDE = COLS + 2 * SIDE
GROUP_B, GROUP_C = 4, 16
INNER_B, SLOTS_C = 18, 2
CONV_VMEM = 40


def convolution_kernel(
    place_ref, sym_ref, act_ref, top_ref, bottom_ref, low_ref, high_ref, gain_ref, shift_ref,
    bias_ref, weight_hbm, out_hbm, tall_ref, wide_ref, first_ref, second_ref, shifted_ref,
    late_ref, weight_ref, out_ref, sems, out_sems,
):
    top_copy = pltpu.make_async_copy(top_ref, tall_ref.at[0:HALO], sems.at[0])
    bottom_copy = pltpu.make_async_copy(bottom_ref, tall_ref.at[HALO + ROWS : TALL], sems.at[1])
    act_copy = pltpu.make_async_copy(
        act_ref, wide_ref.at[HALO : HALO + ROWS, 16 : 16 + COLS], sems.at[2]
    )
    weight_copy = pltpu.make_async_copy(weight_hbm, weight_ref, sems.at[3])
    sym_copy = pltpu.make_async_copy(sym_ref, tall_ref.at[HALO : HALO + ROWS], sems.at[4])
    for copy in (top_copy, bottom_copy, act_copy, weight_copy, sym_copy):
        copy.start()
    above = place_ref[0] > 0
    below = place_ref[0] < (NR - 1) * ROWS
    low_ok = (place_ref[1] > 0).astype(F32)
    high_ok = (place_ref[1] < (NC - 1) * COLS).astype(F32)

    def activate(cells, which):
        return jnp.maximum(
            normalize(
                cells,
                gain_ref[which : which + 1].reshape(1, 1, CH),
                shift_ref[which : which + 1].reshape(1, 1, CH),
            ),
            0.0,
        )

    nothing = jnp.zeros((TALL, SIDE, CH), F32)
    low = activate(low_ref[...].astype(F32), 0) * low_ok
    wide_ref[:, 0:16, :] = jnp.concatenate([nothing, low], axis=1).astype(BF)
    high = activate(high_ref[...].astype(F32), 0) * high_ok
    wide_ref[:, 16 + COLS :, :] = jnp.concatenate([high, nothing], axis=1).astype(BF)
    top_copy.wait()
    bottom_copy.wait()
    wide_ref[0:HALO, 16 : 16 + COLS, :] = activate(tall_ref[0:HALO].astype(F32), 0).astype(BF)
    wide_ref[HALO + ROWS :, 16 : 16 + COLS, :] = activate(
        tall_ref[HALO + ROWS :].astype(F32), 0
    ).astype(BF)

    @pl.when(jnp.logical_not(above))
    def _():
        wide_ref[0:HALO] = jnp.zeros((HALO, WIDE, CH), BF)

    @pl.when(jnp.logical_not(below))
    def _():
        wide_ref[HALO + ROWS :] = jnp.zeros((HALO, WIDE, CH), BF)

    def paired(source_ref, at, spacing, group, width, which):
        sets = group // (2 * spacing)
        lhs = jnp.concatenate(
            [
                jnp.concatenate(
                    [
                        source_ref[pl.ds(at + 2 * spacing * k + spacing * slot, spacing)]
                        for k in range(sets)
                    ],
                    axis=0,
                ).reshape(group // 2 * width, CH)
                for slot in range(4)
            ],
            axis=1,
        )
        total = jnp.dot(lhs, weight_ref[which], preferred_element_type=F32)
        taps = []
        for tap in range(3):
            near = total[:, tap * CH : (tap + 1) * CH].reshape(sets, spacing, width, CH)
            far = total[:, (3 + tap) * CH : (4 + tap) * CH].reshape(sets, spacing, width, CH)
            taps.append(jnp.concatenate([near, far], axis=1).reshape(group, width, CH))
        return taps

    def first_rows(at, slot):
        before, centre, after = paired(wide_ref, at, FIRST_DILATION, GROUP_B, WIDE, 0)
        shifted_ref[slot, 0] = before
        shifted_ref[slot, 1] = after
        residual = jnp.concatenate(
            [
                low_ref[pl.ds(at + 2, GROUP_B)].astype(F32),
                tall_ref[pl.ds(at + 2, GROUP_B)].astype(F32),
                high_ref[pl.ds(at + 2, GROUP_B)].astype(F32),
            ],
            axis=1,
        )
        first = (
            centre[:, 8 : 8 + FIRST_WIDE]
            + shifted_ref[slot, 0, :, 6 : 6 + FIRST_WIDE, :]
            + shifted_ref[slot, 1, :, 10 : 10 + FIRST_WIDE, :]
            + residual
            + bias_ref[0:1].reshape(1, 1, CH)
        )
        first_ref[pl.ds(at, GROUP_B)] = first[:, SIDE : SIDE + COLS]
        act = activate(first, 1)
        second_ref[pl.ds(at, GROUP_B)] = jnp.concatenate(
            [
                act[:, :SIDE] * low_ok,
                act[:, SIDE : SIDE + COLS],
                act[:, SIDE + COLS :] * high_ok,
            ],
            axis=1,
        ).astype(BF)

    def convolve_first(step, carry):
        for k in range(INNER_B):
            first_rows(step * (GROUP_B * INNER_B) + k * GROUP_B, k)
        return carry

    act_copy.wait()
    weight_copy.wait()
    sym_copy.wait()
    lax.fori_loop(0, FIRST_TALL // (GROUP_B * INNER_B), convolve_first, 0)

    @pl.when(jnp.logical_not(above))
    def _():
        second_ref[0:SECOND_DILATION] = jnp.zeros((SECOND_DILATION, FIRST_WIDE, CH), BF)

    @pl.when(jnp.logical_not(below))
    def _():
        second_ref[SECOND_DILATION + ROWS :] = jnp.zeros((SECOND_DILATION, FIRST_WIDE, CH), BF)

    def out_copy(k):
        return pltpu.make_async_copy(
            out_ref.at[16 * k : 16 * k + 16], out_hbm.at[16 * k : 16 * k + 16], out_sems.at[k]
        )

    for k in range(4):
        for part in range(16 // GROUP_C):
            at = 16 * k + part * GROUP_C
            slot = at // GROUP_C % SLOTS_C
            before, centre, after = paired(
                second_ref, at, SECOND_DILATION, GROUP_C, FIRST_WIDE, 1
            )
            late_ref[slot, 0] = before
            late_ref[slot, 1] = after
            out_ref[at : at + GROUP_C] = (
                centre[:, SIDE : SIDE + COLS]
                + late_ref[slot, 0, :, 4 : 4 + COLS, :]
                + late_ref[slot, 1, :, 12 : 12 + COLS, :]
                + first_ref[at + 4 : at + 4 + GROUP_C]
                + bias_ref[1:2].reshape(1, 1, CH)
            ).astype(BF)
        out_copy(k).start()
    for k in range(4):
        out_copy(k).wait()


def convolutions(place, sym, act, top, bottom, low, high, gain, shift, bias, weight):
    vmem = pl.BlockSpec(memory_space=pltpu.VMEM)
    anywhere = pl.BlockSpec(memory_space=pl.ANY)
    return pl.pallas_call(
        convolution_kernel,
        out_shape=jax.ShapeDtypeStruct((ROWS, COLS, CH), BF),
        in_specs=[pl.BlockSpec(memory_space=pltpu.SMEM)]
        + [anywhere] * 4
        + [vmem] * 5
        + [anywhere],
        out_specs=anywhere,
        scratch_shapes=[
            pltpu.VMEM((TALL, COLS, CH), BF),
            pltpu.VMEM((TALL, WIDE, CH), BF),
            pltpu.VMEM((FIRST_TALL, COLS, CH), F32),
            pltpu.VMEM((FIRST_TALL, FIRST_WIDE, CH), BF),
            pltpu.VMEM((INNER_B, 2, GROUP_B, WIDE, CH), F32),
            pltpu.VMEM((SLOTS_C, 2, GROUP_C, FIRST_WIDE, CH), F32),
            pltpu.VMEM((2, 4 * CH, 6 * CH), BF),
            pltpu.VMEM((ROWS, COLS, CH), BF),
            pltpu.SemaphoreType.DMA((5,)),
            pltpu.SemaphoreType.DMA((4,)),
        ],
        compiler_params=pltpu.CompilerParams(vmem_limit_bytes=CONV_VMEM * MIB),
        name="convolutions",
    )(place, sym, act, top, bottom, low, high, gain, shift, bias, weight)


def paired_weight(weight):
    taps = jnp.transpose(weight.reshape(3, 3, CH, CH), (0, 2, 1, 3)).reshape(3, CH, 3 * CH)
    near = jnp.concatenate([taps, jnp.zeros_like(taps[:1])], axis=0)
    far = jnp.concatenate([jnp.zeros_like(taps[:1]), taps], axis=0)
    return jnp.concatenate([near, far], axis=2).reshape(4 * CH, 6 * CH)


def neighbours(low_strip, high_strip, axis):
    count = lax.axis_size(axis)
    forward = [(i, i + 1) for i in range(count - 1)]
    backward = [(i + 1, i) for i in range(count - 1)]
    return lax.ppermute(high_strip, axis, forward), lax.ppermute(low_strip, axis, backward)


def local(
    pair, norm_gain, norm_shift, proj_weight, proj_bias, mid_gain, mid_shift, out_weight, out_bias,
    conv_gain, conv_shift, convolution_weight, convolution_bias,
):
    gain, shift = norm_gain[None], norm_shift[None]
    sent = factors(pair, gain, shift, proj_weight, proj_bias)
    exchange = lambda v: lax.all_to_all(
        v, ("row", "col"), split_axis=0, concat_axis=0, tiled=True
    )
    received = exchange(sent.reshape(128, 2, ROWS, COLS))
    received = received.reshape(NR // 2, 2, NC, 2, ROWS, COLS)
    cells = regroup(received)
    mirrored = exchange(cells.reshape(128, ROWS, COLS))
    own = plane(lax.optimization_barrier((received, cells))[0])
    other = lax.ppermute(own, "row", [(i, i ^ 1) for i in range(NR)])
    returned = exchange(product(own, other).reshape(128, ROWS, COLS))
    gate, gate_bias = proj_weight[:, 4 * HID :], proj_bias[None, 4 * HID :]
    paired = jnp.stack([paired_weight(convolution_weight[0]), paired_weight(convolution_weight[1])])
    gate, paired = lax.optimization_barrier((gate, paired))
    sym = update(
        pair,
        gates(pair, gain, shift, gate, gate_bias),
        *mirror_gates(mirrored, gain, shift, gate, gate_bias),
        returned,
        *output_weight(out_weight, out_bias, mid_gain, mid_shift),
    )
    top, bottom = neighbours(sym[:HALO], sym[ROWS - HALO :], "row")
    edge = lambda low, high: jnp.concatenate(
        [top[:, low:high], sym[:, low:high], bottom[:, low:high]], axis=0
    )
    low, high = neighbours(edge(0, SIDE), edge(COLS - SIDE, COLS), "col")
    place = jnp.stack([lax.axis_index("row") * ROWS, lax.axis_index("col") * COLS]).astype(jnp.int32)
    return convolutions(
        place, sym, activations(sym, conv_gain, conv_shift), top, bottom, low, high, conv_gain, conv_shift, convolution_bias,
        paired,
    )


def solution(mesh):
    return jax.shard_map(
        local,
        mesh=mesh,
        in_specs=(P("row", "col", None),) + (P(),) * 12,
        out_specs=P("row", "col", None),
        check_vma=False,
    )
```
